256 devices in a mesh: batch: 8 (over y, x_lo), tm: 32 (over x_hi, z, core).
Axes of the slice: x: 4 (x_hi: 2, x_lo: 2; x = x_hi * 2 + x_lo), y: 4, z: 8, core: 2. Of those that a mesh axis runs over, the one named last changes fastest.
Arguments:
- inputs: bfloat16 [8, 4096, 1536], P('batch', 'tm'), may hold values from -6 to 6
- lengths: int32 [8], P('batch'), may hold values from 2048 to 4096, as said below
- kernel: float32 [31, 1536], replicated, may hold values from -1 to 1
- norm_gain: float32 [1536], replicated, may hold values from 0.25 to 1.75
- weight: bfloat16 [1536, 1536], P('batch'), may hold values from -0.15625 to 0.15625
- cotangent: bfloat16 [8, 4096, 1536], P('batch', 'tm'), may hold values from -6 to 6
Outputs:
- projected: bfloat16 [8, 4096, 1536], P('batch', 'tm')
- grad_input: bfloat16 [8, 4096, 1536], P('batch', 'tm')
- grad_weight: float32 [1536, 1536], P(('batch', 'tm'))
- grad_kernel: float32 [31, 1536], replicated
- grad_gain: float32 [1536], replicated
The draws below stay inside these ranges and needn't reach their ends.
Inputs may be any that keep to these rules, and one draw needn't show every extreme that they name: `lengths`: some utterance is valid over all 4096 frames.
All inputs are finite; a program needn't handle non-finite values.
Results may differ from the reference program's by a relative error of at most 0.0049.
Values may be sent and summed in bfloat16 or wider, within the bound.
A program may use at most 64 MiB of HBM per device.

```python
import jax
import jax.numpy as jnp
from jax import lax

D = 1536
KERNEL = 31
UTTS = 8
FRAMES = 4096


def draw_lengths(key, part):
    key = jax.random.fold_in(key, 11)
    first, second = jax.random.split(key)
    values = jax.random.randint(first, (UTTS,), FRAMES // 2, FRAMES + 1)
    chosen = jax.random.randint(second, (), 0, UTTS)
    return jnp.where(jnp.arange(UTTS) == chosen, FRAMES, values).astype(jnp.int32)


def level_of(rng, shape, shards, least, largest):
    factor_of = 1.0
    for dim, shards_of in shards:
        heights = jax.random.uniform(jax.random.fold_in(jax.random.fold_in(rng, 6), dim), (shards_of,), jnp.float32, least / len(shards), largest / len(shards))
        factor_of = factor_of * jnp.repeat(jnp.exp(heights), shape[dim] // shards_of).reshape((-1,) + (1,) * (len(shape) - 1 - dim))
    return factor_of


def noise(key, extent, scale, bound, shards=(), kind=jnp.bfloat16):
    result = scale * jax.random.normal(key, extent, jnp.float32)
    if shards:
        result = result * level_of(key, extent, shards, -0.22, 0.18)
    return jnp.clip(result, -bound, bound).astype(kind)


def setup_inputs(seed: int = 0) -> dict:
    splits = jax.random.split(jax.random.key(seed), 7)
    inputs = noise(splits[0], (UTTS, FRAMES, D), 1.0, 6.0, ((0, 8), (1, 32)))
    lengths = draw_lengths(jax.random.fold_in(splits[6], 71), 0)
    kernel = noise(splits[2], (KERNEL, D), KERNEL ** -0.5, 1.0, (), jnp.float32)
    norm_gain = jnp.clip(1.0 + 0.15 * jax.random.normal(splits[3], (D,), jnp.float32), 0.25, 1.75)
    weight = noise(splits[4], (D, D), D ** -0.5, 0.15625, ((0, 8),))
    cotangent = noise(splits[5], (UTTS, FRAMES, D), 1.0, 6.0, ((0, 8), (1, 32)))
    return dict(inputs=inputs, lengths=lengths, kernel=kernel, norm_gain=norm_gain, weight=weight, cotangent=cotangent)


def conv_taps(padded, kernel, frames):
    total = jnp.zeros((padded.shape[0], frames, padded.shape[2]), jnp.float32)
    for tap in range(kernel.shape[0]):
        total = total + kernel[tap] * padded[:, tap:tap + frames, :]
    return total

def norm_forward(convolved):
    average = lax.optimization_barrier(jnp.mean(convolved, axis=-1, keepdims=True))
    centred = convolved - average
    variance = lax.optimization_barrier(jnp.mean(centred * centred, axis=-1, keepdims=True))
    inv_scale = lax.rsqrt(variance + 1e-05)
    return (centred * inv_scale, inv_scale)

def norm_backward(act_grad, scaled, normed, inv_scale, norm_gain, live_mask):
    sigmoid_u = jax.nn.sigmoid(scaled)
    scaled_grad = act_grad * sigmoid_u * (1.0 + scaled * (1.0 - sigmoid_u))
    gain_grad = lax.optimization_barrier(jnp.sum(scaled_grad * normed, axis=(0, 1)))
    normed_grad = scaled_grad * norm_gain
    first = lax.optimization_barrier(jnp.mean(normed_grad, axis=-1, keepdims=True))
    second = lax.optimization_barrier(jnp.mean(normed_grad * normed, axis=-1, keepdims=True))
    conv_grad = inv_scale * (normed_grad - first - normed * second) * live_mask
    return (gain_grad, conv_grad)

def reference(inputs, lengths, kernel, norm_gain, weight, cotangent):
    reach = (KERNEL - 1) // 2

    def one_utterance(carry, items):
        source, length, upstream_raw = items
        position = jnp.arange(FRAMES, dtype=jnp.int32)
        live_mask = (position < length).astype(jnp.float32)[None, :, None]
        masked = source[None] * live_mask.astype(jnp.bfloat16)
        padded = jnp.pad(masked.astype(jnp.float32), ((0, 0), (reach, reach), (0, 0)))
        convolved = conv_taps(padded, kernel, FRAMES) * live_mask
        normed, inv_scale = norm_forward(convolved)
        scaled = normed * norm_gain
        activated = (scaled * jax.nn.sigmoid(scaled)).astype(jnp.bfloat16)
        act_rows = activated[0]
        projected = jnp.dot(act_rows, weight, preferred_element_type=jnp.float32).astype(jnp.bfloat16)
        grad_rows = upstream_raw * live_mask[0].astype(jnp.bfloat16)
        act_grad = jnp.dot(grad_rows, weight.T, preferred_element_type=jnp.float32)[None]
        weight_term = jnp.dot(act_rows.T, grad_rows, preferred_element_type=jnp.float32)
        gain_grad, conv_grad = norm_backward(act_grad, scaled, normed, inv_scale, norm_gain, live_mask)
        kernel_grad = jnp.stack([lax.optimization_barrier(jnp.sum(conv_grad * padded[:, tap:tap + FRAMES, :], axis=(0, 1))) for tap in range(KERNEL)])
        grad_pad = jnp.pad(conv_grad, ((0, 0), (reach, reach), (0, 0)))
        back = jnp.zeros((1, FRAMES, D), jnp.float32)
        for tap in range(KERNEL):
            back = back + kernel[tap] * grad_pad[:, 2 * reach - tap:2 * reach - tap + FRAMES, :]
        grad_input = (back * live_mask).astype(jnp.bfloat16)[0]
        totals = (carry[0] + weight_term, carry[1] + kernel_grad, carry[2] + gain_grad)
        return (totals, (projected, grad_input))
    start = (jnp.zeros((D, D), jnp.float32), jnp.zeros((KERNEL, D), jnp.float32), jnp.zeros((D,), jnp.float32))
    totals, outputs = lax.scan(one_utterance, start, (inputs, lengths, cotangent))
    return (outputs[0], outputs[1], totals[0], totals[1], totals[2])
```

```python
import jax
import jax.numpy as jnp
from jax import lax
from jax.experimental import pallas as pl
from jax.experimental.pallas import tpu as pltpu
from jax.sharding import PartitionSpec as P

F32, BF16 = jnp.float32, jnp.bfloat16
MESH = pl.DeviceIdType.MESH
D, T, H, TAPS = 1536, 128, 768, 31
PAD = 16
LANES = 128
CHUNKS = D // LANES


def lanes_of(k):
    return pl.ds(pl.multiple_of(k * LANES, LANES), LANES)


def fused(
    x_ref, len_ref, kern_ref, gain_ref, w_ref, cot_ref,
    proj_ref, gin_ref, gw_ref, gk_ref, gg_ref,
    xm, hx, xf, cv, ds, ab, at, us, ub, wb, px, py, rx, ry, s2x, s2y, r2x, r2y,
    facc, zs, rz, fin, cr, agp, agr, pj, pjr, cg, gkb, gcr, gh, zr, xs, ys, fg, fgr,
    sem_halo_s, sem_halo_r, sem_w_s, sem_w_r, sem_c_s, sem_c_r, sem_p_s, sem_p_r,
    sem_z_s, sem_z_r, sem_t_s, sem_t_r,
):
    b = lax.axis_index("batch")
    t = lax.axis_index("tm")
    y, xl = b // 2, b % 2
    xh, z, c = t // 16, (t // 2) % 8, t % 2
    x = xh * 2 + xl
    oc = 1 - c

    def dev(y_, x_, z_, c_):
        return (y_ * 2 + x_ % 2, (x_ // 2) * 16 + z_ * 2 + c_)

    def along_y(i):
        return dev((y + i) % 4, x, z, c)

    def along_x(i):
        return dev(y, (x + i) % 4, z, c)

    def along_z(i):
        return dev(y, x, (z + i) % 8, c)

    mate = dev(y, x, z, oc)
    before, after = (b, t - 1), (b, t + 1)

    def block_of(x_):
        return (x_ % 2) * 2 + x_ // 2

    q = block_of(x)

    def half(c_):
        return pl.ds(pl.multiple_of(c_ * H, H), H)

    def frames_of(c_):
        return pl.ds(pl.multiple_of(c_ * T, T), T)

    started = []

    def copy(src, dst, ss, rs, to):
        return pltpu.make_async_remote_copy(
            src_ref=src, dst_ref=dst, send_sem=ss, recv_sem=rs, device_id=to, device_id_type=MESH
        )

    def send(*args):
        item = copy(*args)
        item.start()
        started.append(item)
        return item

    barrier = pltpu.get_barrier_semaphore()

    def greet(to):
        pl.semaphore_signal(barrier, inc=1, device_id=to, device_id_type=MESH)

    greet(mate)
    for i in range(1, 4):
        greet(along_y(i))
        greet(along_x(i))
    for i in range(1, 8):
        greet(along_z(i))

    @pl.when(t > 0)
    def _():
        greet(before)

    @pl.when(t < 31)
    def _():
        greet(after)

    length = len_ref[0]
    position = t * T + lax.broadcasted_iota(jnp.int32, (T, LANES), 0)
    live = jnp.where(position < length, 1.0, 0.0).astype(F32)

    def mask_chunk(k, _):
        at_lanes = lanes_of(k)
        masked = x_ref[:, at_lanes].astype(F32) * live
        xm[:, at_lanes] = masked.astype(BF16)
        xf[PAD:PAD + T, at_lanes] = masked
        us[:, at_lanes] = (cot_ref[:, at_lanes].astype(F32) * live).astype(BF16)
        return 0

    lax.fori_loop(0, CHUNKS, mask_chunk, 0)

    others = 14 + jnp.where(t > 0, 1, 0) + jnp.where(t < 31, 1, 0)
    pl.semaphore_wait(barrier, others)

    to_before = copy(xm.at[pl.ds(0, PAD)], hx.at[1], sem_halo_s.at[0], sem_halo_r.at[1], before)
    to_after = copy(xm.at[pl.ds(T - PAD, PAD)], hx.at[0], sem_halo_s.at[1], sem_halo_r.at[0], after)

    @pl.when(t > 0)
    def _():
        to_before.start()

    @pl.when(t < 31)
    def _():
        to_after.start()

    mine = w_ref.at[:, half(c)]

    def rows_of(y_, xl_, start, count):
        return pl.ds(pl.multiple_of((y_ * 2 + xl_) * 192 + start, 96), count)

    w_own = rows_of(y, xl, 0, 192)
    u_swap = send(us.at[:, half(oc)], ub.at[frames_of(c)], sem_c_s.at[0], sem_c_r.at[0], mate)
    for i in range(1, 4):
        send(mine, wb.at[w_own], sem_w_s.at[i - 1], sem_w_r.at[i - 1], along_y(i))
    for side, step in ((0, 1), (1, 3)):
        send(
            w_ref.at[pl.ds(side * 96, 96), half(c)], wb.at[rows_of(y, xl, side * 96, 96)],
            sem_w_s.at[3 + side], sem_w_r.at[3 + side], along_x(step),
        )
    wb[w_own, :] = w_ref[:, half(c)]
    ub[frames_of(c), :] = us[:, half(c)]

    @pl.when(t > 0)
    def _():
        to_after.wait_recv()
        xf[0:PAD, :] = hx[0].astype(F32)

    @pl.when(t == 0)
    def _():
        xf[0:PAD, :] = jnp.zeros((PAD, D), F32)

    @pl.when(t < 31)
    def _():
        to_before.wait_recv()
        xf[PAD + T:, :] = hx[1].astype(F32)

    @pl.when(t == 31)
    def _():
        xf[PAD + T:, :] = jnp.zeros((PAD, D), F32)

    def conv(source, taps, forward):
        total = jnp.zeros((T, LANES), F32)
        for r in range(8):
            shifted = source[r:r + T + 24]
            for k in range(4):
                offset = 8 * k + r
                tap = offset - 1 if forward else TAPS - offset
                if 0 <= tap < TAPS:
                    total = total + taps[tap:tap + 1] * shifted[8 * k:8 * k + T]
        return total

    def conv_chunk(k, total):
        at_lanes = lanes_of(k)
        value = conv(xf[:, at_lanes], kern_ref[:, at_lanes], True) * live
        cv[:, at_lanes] = value
        return total + value

    zero = jnp.zeros((T, LANES), F32)
    total = lax.fori_loop(0, CHUNKS, conv_chunk, zero)
    average = jnp.broadcast_to(jnp.sum(total, axis=1, keepdims=True) * (1.0 / D), (T, LANES))

    def variance_chunk(k, total):
        centred = cv[:, lanes_of(k)] - average
        return total + centred * centred

    total = lax.fori_loop(0, CHUNKS, variance_chunk, zero)
    variance = jnp.sum(total, axis=1, keepdims=True) * (1.0 / D)
    inv = jnp.broadcast_to(lax.rsqrt(variance + 1e-05), (T, LANES))

    def act_chunk(k, _):
        at_lanes = lanes_of(k)
        normed = (cv[:, at_lanes] - average) * inv
        scaled = normed * gain_ref[:, at_lanes]
        gate = 1.0 / (1.0 + jnp.exp(-scaled))
        act = scaled * gate
        cv[:, at_lanes] = normed
        ds[:, at_lanes] = gate * (1.0 + scaled * (1.0 - gate))
        ab[frames_of(c), at_lanes] = act.astype(BF16)
        at[lanes_of(k), frames_of(c)] = act.T.astype(BF16)
        return 0

    swaps = []
    for part in range(3):
        lax.fori_loop(part * 4, part * 4 + 4, act_chunk, 0)
        cols = pl.ds(part * 512, 512)
        here = at.at[cols, frames_of(c)]
        swaps.append(send(here, here, sem_c_s.at[1 + part], sem_c_r.at[1 + part], mate))
        here = ab.at[frames_of(c), cols]
        swaps.append(send(here, here, sem_c_s.at[4 + part], sem_c_r.at[4 + part], mate))

    for i in range(1, 4):
        from_y = (y + 4 - i) % 4
        copy(mine, wb.at[rows_of(from_y, xl, 0, 192)], sem_w_s.at[i - 1], sem_w_r.at[i - 1], along_y(i)).wait_recv()
        for side, step in ((0, 1), (1, 3)):
            here = wb.at[rows_of(from_y, xl, side * 96, 96)]
            n = 3 + 2 * i + side
            send(here, here, sem_w_s.at[n], sem_w_r.at[n], along_x(step))

    u_swap.wait_recv()
    for item in swaps[0::2]:
        item.wait_recv()

    def partial(dst, start):
        def body(n, _):
            rows = pl.ds(pl.multiple_of(n * 384, 384), 384)
            value = jnp.dot(at[rows, :], ub[:, start:start + 384], preferred_element_type=F32)
            dst[n] = value.reshape(4, 96, 384).astype(BF16)
            return 0
        lax.fori_loop(0, 4, body, 0)

    partial(px, 0)
    x_first = [
        send(px.at[:, block_of((x + i) % 4)], rx.at[i - 1], sem_p_s.at[i - 1], sem_p_r.at[i - 1], along_x(i))
        for i in range(1, 4)
    ]
    partial(py, 384)
    y_first = [
        send(py.at[(y + i) % 4], ry.at[i - 1], sem_p_s.at[2 + i], sem_p_r.at[2 + i], along_y(i))
        for i in range(1, 4)
    ]

    for i in range(4):
        from_y = (y + 4 - i) % 4
        for side, step in ((0, 1), (1, 3)):
            here = wb.at[rows_of(from_y, 1 - xl, side * 96, 96)]
            n = 3 + 2 * i + side
            copy(here, here, sem_w_s.at[n], sem_w_r.at[n], along_x(step)).wait_recv()

    def act_grad_chunk(n, _):
        cols = pl.ds(pl.multiple_of(n * 256, 256), 256)
        value = lax.dot_general(
            ub[...], wb[cols, :], (((1,), (1,)), ((), ())), preferred_element_type=F32
        )
        agp[0, :, cols] = value[:T]
        agp[1, :, cols] = value[T:]
        return 0

    ag_swaps = []
    for part in range(3):
        lax.fori_loop(part * 2, part * 2 + 2, act_grad_chunk, 0)
        cols = pl.ds(part * 512, 512)
        ag_swaps.append(
            send(agp.at[oc, :, cols], agr.at[:, cols], sem_c_s.at[7 + part], sem_c_r.at[7 + part], mate)
        )

    for item in swaps[1::2]:
        item.wait_recv()

    def project_chunk(n, _):
        cols = pl.ds(pl.multiple_of(n * 256, 256), 256)
        value = jnp.dot(ab[...], wb[:, cols], preferred_element_type=F32).astype(BF16)
        pj[0, :, cols] = value[:T]
        pj[1, :, cols] = value[T:]
        return 0

    lax.fori_loop(0, 3, project_chunk, 0)
    pj_swap = send(pj.at[oc], pjr, sem_c_s.at[10], sem_c_r.at[10], mate)
    proj_ref[:, half(c)] = pj[c]

    for item in ag_swaps:
        item.wait_recv()

    def back_chunk(k, sums):
        at_lanes = lanes_of(k)
        normed = cv[:, at_lanes]
        scaled_grad = (agp[c, :, at_lanes] + agr[:, at_lanes]) * ds[:, at_lanes]
        gkb[TAPS:TAPS + 1, at_lanes] = jnp.sum(scaled_grad * normed, axis=0, keepdims=True)
        normed_grad = scaled_grad * gain_ref[:, at_lanes]
        ds[:, at_lanes] = normed_grad
        return (sums[0] + normed_grad, sums[1] + normed_grad * normed)

    sums = lax.fori_loop(0, CHUNKS, back_chunk, (zero, zero))
    first, second = [
        jnp.broadcast_to(jnp.sum(s, axis=1, keepdims=True) * (1.0 / D), (T, LANES)) for s in sums
    ]
    inv_live = inv * live

    def conv_grad_chunk(k, _):
        at_lanes = lanes_of(k)
        cg[PAD:PAD + T, at_lanes] = inv_live * (ds[:, at_lanes] - first - cv[:, at_lanes] * second)
        return 0

    lax.fori_loop(0, CHUNKS, conv_grad_chunk, 0)

    g_before = copy(cg.at[pl.ds(PAD, PAD)], cg.at[pl.ds(PAD + T, PAD)], sem_halo_s.at[2], sem_halo_r.at[3], before)
    g_after = copy(cg.at[pl.ds(T, PAD)], cg.at[pl.ds(0, PAD)], sem_halo_s.at[3], sem_halo_r.at[2], after)

    @pl.when(t > 0)
    def _():
        g_before.start()

    @pl.when(t < 31)
    def _():
        g_after.start()

    def taps_chunk(k, _):
        at_lanes = lanes_of(k)
        source = xf[:, at_lanes]
        grad = cg[PAD:PAD + T, at_lanes]
        for r in range(8):
            shifted = source[r:r + T + 24]
            for j in range(4):
                tap = 8 * j + r - 1
                if 0 <= tap < TAPS:
                    gkb[tap:tap + 1, at_lanes] = jnp.sum(grad * shifted[8 * j:8 * j + T], axis=0, keepdims=True)
        return 0

    lax.fori_loop(0, CHUNKS, taps_chunk, 0)
    gk_swap = send(gkb.at[:, half(oc)], gcr, sem_t_s.at[0], sem_t_r.at[0], mate)

    for item in x_first:
        item.wait_recv()

    def add_x(n, _):
        value = px[n, q].astype(F32)
        for i in range(3):
            value = value + rx[i, n].astype(F32)
        s2x[n] = value.astype(BF16)
        return 0

    lax.fori_loop(0, 4, add_x, 0)
    x_second = [
        send(s2x.at[(y + i) % 4], r2x.at[i - 1], sem_p_s.at[5 + i], sem_p_r.at[5 + i], along_y(i))
        for i in range(1, 4)
    ]
    for item in y_first:
        item.wait_recv()

    def add_y(n, _):
        value = py[y, n].astype(F32)
        for i in range(3):
            value = value + ry[i, n].astype(F32)
        s2y[n] = value.astype(BF16)
        return 0

    lax.fori_loop(0, 4, add_y, 0)
    y_second = [
        send(s2y.at[block_of((x + i) % 4)], r2y.at[i - 1], sem_p_s.at[8 + i], sem_p_r.at[8 + i], along_x(i))
        for i in range(1, 4)
    ]

    def piece(z_):
        return (
            pl.ds(pl.multiple_of((z_ // 2) * 8, 8), 8),
            pl.ds(pl.multiple_of((z_ % 2) * 384, 384), 384),
        )

    gk_swap.wait_recv()
    gh[...] = gkb[:, half(c)] + gcr[...]
    t_z = [
        send(gh.at[piece((z + i) % 8)], zr.at[i - 1], sem_t_s.at[i], sem_t_r.at[i], along_z(i))
        for i in range(1, 8)
    ]

    @pl.when(t > 0)
    def _():
        g_after.wait_recv()

    @pl.when(t == 0)
    def _():
        cg[0:PAD, :] = jnp.zeros((PAD, D), F32)

    @pl.when(t < 31)
    def _():
        g_before.wait_recv()

    @pl.when(t == 31)
    def _():
        cg[PAD + T:, :] = jnp.zeros((PAD, D), F32)

    def input_chunk(k, _):
        at_lanes = lanes_of(k)
        value = conv(cg[:, at_lanes], kern_ref[:, at_lanes], False) * live
        gin_ref[:, at_lanes] = value.astype(BF16)
        return 0

    lax.fori_loop(0, 6, input_chunk, 0)

    for item in t_z:
        item.wait_recv()
    mine_t = gh[piece(z)]
    for i in range(7):
        mine_t = mine_t + zr[i]
    xs[x] = mine_t
    t_x = [send(xs.at[x], xs.at[x], sem_t_s.at[7 + i], sem_t_r.at[7 + i], along_x(i)) for i in range(1, 4)]

    for item in x_second + y_second:
        item.wait_recv()
    left, right = s2x[y].astype(F32), s2y[q].astype(F32)
    for i in range(3):
        left = left + r2x[i].astype(F32)
        right = right + r2y[i].astype(F32)
    facc[0:96, 0:384] = left
    facc[0:96, 384:768] = right
    facc[96:104, :] = jnp.zeros((8, H), F32)
    for n in range(8):
        zs[n] = facc[12 * n:12 * n + 16, :].astype(BF16)
    w_z = [
        send(zs.at[(z + i) % 8], rz.at[i - 1], sem_z_s.at[i - 1], sem_z_r.at[i - 1], along_z(i))
        for i in range(1, 8)
    ]

    def wait_slots(slots, me, sems, base):
        for i in range(1, 4):
            slot = slots.at[(me + 4 - i) % 4]
            copy(slot, slot, sem_t_s.at[base + i], sem_t_r.at[base + i], mate).wait_recv()

    wait_slots(xs, x, sem_t_r, 7)
    ys[y] = xs[0] + xs[1] + xs[2] + xs[3]
    t_y = [send(ys.at[y], ys.at[y], sem_t_s.at[10 + i], sem_t_r.at[10 + i], along_y(i)) for i in range(1, 4)]
    lax.fori_loop(6, CHUNKS, input_chunk, 0)
    wait_slots(ys, y, sem_t_r, 10)
    fg[piece(z)] = ys[0] + ys[1] + ys[2] + ys[3]
    for i in range(1, 8):
        here = fg.at[piece(z)]
        send(here, here, sem_t_s.at[13 + i], sem_t_r.at[13 + i], along_z(i))

    pj_swap.wait_recv()
    proj_ref[:, half(oc)] = pjr[...]

    for item in w_z:
        item.wait_recv()
    rows = zs[z].astype(F32)
    for i in range(7):
        rows = rows + rz[i].astype(F32)
    fin[...] = jnp.zeros((2, 8, H), F32)
    fin[0, 0:6, :] = rows[0:6]
    fin[1, 0:6, :] = rows[6:12]
    w_swap = send(fin.at[oc], cr, sem_z_s.at[7], sem_z_r.at[7], mate)

    for i in range(1, 8):
        slot = fg.at[piece((z + 8 - i) % 8)]
        copy(slot, slot, sem_t_s.at[13 + i], sem_t_r.at[13 + i], mate).wait_recv()
    t_swap = send(fg, fgr, sem_t_s.at[21], sem_t_r.at[21], mate)

    def put_taps(cols, value):
        gk_ref[:, cols] = value[0:TAPS]
        gg_ref[:, cols] = value[TAPS:TAPS + 1]

    put_taps(half(c), fg[...])
    gw_ref[:, half(c)] = fin[c][0:6]
    w_swap.wait_recv()
    gw_ref[:, half(oc)] = cr[0:6, :]
    t_swap.wait_recv()
    put_taps(half(oc), fgr[...])

    @pl.when(t > 0)
    def _():
        to_before.wait_send()
        g_before.wait_send()

    @pl.when(t < 31)
    def _():
        to_after.wait_send()
        g_after.wait_send()

    for item in started:
        item.wait_send()


def on_device(inputs, lengths, kernel, norm_gain, weight, cotangent):
    vmem = pl.BlockSpec(memory_space=pltpu.VMEM)
    dma = pltpu.SemaphoreType.DMA
    scratch = [
        pltpu.VMEM((T, D), BF16),
        pltpu.VMEM((2, PAD, D), BF16),
        pltpu.VMEM((T + 2 * PAD, D), F32),
        pltpu.VMEM((T, D), F32),
        pltpu.VMEM((T, D), F32),
        pltpu.VMEM((2 * T, D), BF16),
        pltpu.VMEM((D, 2 * T), BF16),
        pltpu.VMEM((T, D), BF16),
        pltpu.VMEM((2 * T, H), BF16),
        pltpu.VMEM((D, H), BF16),
        pltpu.VMEM((4, 4, 96, 384), BF16),
        pltpu.VMEM((4, 4, 96, 384), BF16),
        pltpu.VMEM((3, 4, 96, 384), BF16),
        pltpu.VMEM((3, 4, 96, 384), BF16),
        pltpu.VMEM((4, 96, 384), BF16),
        pltpu.VMEM((4, 96, 384), BF16),
        pltpu.VMEM((3, 96, 384), BF16),
        pltpu.VMEM((3, 96, 384), BF16),
        pltpu.VMEM((104, H), F32),
        pltpu.VMEM((8, 16, H), BF16),
        pltpu.VMEM((7, 16, H), BF16),
        pltpu.VMEM((2, 8, H), F32),
        pltpu.VMEM((8, H), F32),
        pltpu.VMEM((2, T, D), F32),
        pltpu.VMEM((T, D), F32),
        pltpu.VMEM((2, T, H), BF16),
        pltpu.VMEM((T, H), BF16),
        pltpu.VMEM((T + 2 * PAD, D), F32),
        pltpu.VMEM((32, D), F32),
        pltpu.VMEM((32, H), F32),
        pltpu.VMEM((32, H), F32),
        pltpu.VMEM((7, 8, 384), F32),
        pltpu.VMEM((4, 8, 384), F32),
        pltpu.VMEM((4, 8, 384), F32),
        pltpu.VMEM((32, H), F32),
        pltpu.VMEM((32, H), F32),
        dma((4,)), dma((4,)),
        dma((11,)), dma((11,)),
        dma((11,)), dma((11,)),
        dma((12,)), dma((12,)),
        dma((8,)), dma((8,)),
        dma((22,)), dma((22,)),
    ]
    projected, grad_input, grad_weight, grad_kernel, grad_gain = pl.pallas_call(
        fused,
        out_shape=(
            jax.ShapeDtypeStruct((T, D), BF16),
            jax.ShapeDtypeStruct((T, D), BF16),
            jax.ShapeDtypeStruct((6, D), F32),
            jax.ShapeDtypeStruct((TAPS, D), F32),
            jax.ShapeDtypeStruct((1, D), F32),
        ),
        in_specs=[vmem, pl.BlockSpec(memory_space=pltpu.SMEM), vmem, vmem, vmem, vmem],
        out_specs=[vmem] * 5,
        scratch_shapes=scratch,
        compiler_params=pltpu.CompilerParams(
            collective_id=0, has_side_effects=True, vmem_limit_bytes=48 << 20
        ),
        name="conv_module",
    )(inputs[0], lengths, kernel, norm_gain[None], weight, cotangent[0])
    return (projected[None], grad_input[None], grad_weight, grad_kernel, grad_gain[0])


def solution(mesh):
    in_specs = (
        P("batch", "tm", None),
        P("batch"),
        P(),
        P(),
        P("batch", None),
        P("batch", "tm", None),
    )
    out_specs = (P("batch", "tm", None), P("batch", "tm", None), P(("batch", "tm"), None), P(), P())
    return jax.shard_map(
        on_device, mesh=mesh, in_specs=in_specs, out_specs=out_specs, check_vma=False
    )
```

```python
import jax
import jax.numpy as jnp
from jax import lax
from jax.experimental import pallas as pl
from jax.experimental.pallas import tpu as pltpu
from jax.sharding import PartitionSpec as P

F32, BF16 = jnp.float32, jnp.bfloat16
MESH = pl.DeviceIdType.MESH
D, T, H, TAPS = 1536, 128, 768, 31
PAD = 16
CX, CY = 256, 512
LANES = 128
CHUNKS = D // LANES


def lanes_of(k):
    return pl.ds(pl.multiple_of(k * LANES, LANES), LANES)


def fused(
    x_hbm, len_ref, kern_hbm, gain_hbm, w_hbm, cot_hbm,
    proj_hbm, gin_hbm, gw_hbm, gk_hbm, gg_hbm,
    x_ref, kern_ref, gain_ref, cot_ref, proj_ref, gin_ref, gw_ref, gk_ref, gg_ref,
    xm, hx, xf, cv, ds, ab, at, us, ub, wb, px, py, rx, ry, s2x, s2y, r2x, r2y,
    facc, zs, rz, fin, cr, agp, agr, pj, pjr, cg, gkb, gcr, gh, zr, xs, ys, fg, fgr,
    sem_halo_s, sem_halo_r, sem_w_s, sem_w_r, sem_c_s, sem_c_r, sem_p_s, sem_p_r,
    sem_z_s, sem_z_r, sem_t_s, sem_t_r, sem_in, sem_out,
):
    b = lax.axis_index("batch")
    t = lax.axis_index("tm")
    y, xl = b // 2, b % 2
    xh, z, c = t // 16, (t // 2) % 8, t % 2
    x = xh * 2 + xl
    oc = 1 - c

    def dev(y_, x_, z_, c_):
        return (y_ * 2 + x_ % 2, (x_ // 2) * 16 + z_ * 2 + c_)

    def along_y(i):
        return dev((y + i) % 4, x, z, c)

    def along_x(i):
        return dev(y, (x + i) % 4, z, c)

    def along_z(i):
        return dev(y, x, (z + i) % 8, c)

    mate = dev(y, x, z, oc)
    before, after = (b, t - 1), (b, t + 1)

    def block_of(x_):
        return (x_ % 2) * 2 + x_ // 2

    q = block_of(x)

    def half(c_):
        return pl.ds(pl.multiple_of(c_ * H, H), H)

    def frames_of(c_):
        return pl.ds(pl.multiple_of(c_ * T, T), T)

    started = []

    def copy(src, dst, ss, rs, to):
        return pltpu.make_async_remote_copy(
            src_ref=src, dst_ref=dst, send_sem=ss, recv_sem=rs, device_id=to, device_id_type=MESH
        )

    def send(*args):
        item = copy(*args)
        item.start()
        started.append(item)
        return item

    barrier = pltpu.get_barrier_semaphore()

    def greet(to):
        pl.semaphore_signal(barrier, inc=1, device_id=to, device_id_type=MESH)

    greet(mate)
    for i in range(1, 4):
        greet(along_y(i))
        greet(along_x(i))
    for i in range(1, 8):
        greet(along_z(i))

    @pl.when(t > 0)
    def _():
        greet(before)

    @pl.when(t < 31)
    def _():
        greet(after)

    w_own = pl.ds(pl.multiple_of((y * 2 + xl) * 192, 192), 192)
    loads = [
        pltpu.make_async_copy(src, dst, sem_in.at[n])
        for n, (src, dst) in enumerate((
            (x_hbm, x_ref), (cot_hbm, cot_ref), (w_hbm.at[:, half(c)], wb.at[w_own]),
            (kern_hbm, kern_ref), (gain_hbm, gain_ref),
        ))
    ]
    for item in loads:
        item.start()
    length = len_ref[0]
    position = t * T + lax.broadcasted_iota(jnp.int32, (T, LANES), 0)
    live = jnp.where(position < length, 1.0, 0.0).astype(F32)

    for item in loads[:2]:
        item.wait()

    def mask_chunk(k, _):
        at_lanes = lanes_of(k)
        masked = x_ref[:, at_lanes].astype(F32) * live
        xm[:, at_lanes] = masked.astype(BF16)
        xf[PAD:PAD + T, at_lanes] = masked
        us[:, at_lanes] = (cot_ref[:, at_lanes].astype(F32) * live).astype(BF16)
        return 0

    lax.fori_loop(0, CHUNKS, mask_chunk, 0)

    others = 14 + jnp.where(t > 0, 1, 0) + jnp.where(t < 31, 1, 0)
    pl.semaphore_wait(barrier, others)

    to_before = copy(xm.at[pl.ds(0, PAD)], hx.at[1], sem_halo_s.at[0], sem_halo_r.at[1], before)
    to_after = copy(xm.at[pl.ds(T - PAD, PAD)], hx.at[0], sem_halo_s.at[1], sem_halo_r.at[0], after)

    @pl.when(t > 0)
    def _():
        to_before.start()

    @pl.when(t < 31)
    def _():
        to_after.start()

    u_swap = send(us.at[:, half(oc)], ub.at[frames_of(c)], sem_c_s.at[0], sem_c_r.at[0], mate)

    def rows_of(y_, xl_, side):
        return wb.at[pl.ds(pl.multiple_of((y_ * 2 + xl_) * 192 + side * 96, 96), 96)]

    y_up, y_down, y_far = (y + 1) % 4, (y + 3) % 4, (y + 2) % 4
    x_step = (1, 3)

    def push(here, n, to):
        send(here, here, sem_w_s.at[n], sem_w_r.at[n], to)

    def landed(here, n):
        copy(here, here, sem_w_s.at[n], sem_w_r.at[n], mate).wait_recv()

    loads[2].wait()
    for side in range(2):
        own = rows_of(y, xl, side)
        push(own, side, along_y(1))
        push(own, 2 + side, along_y(3))
        push(own, 6 + side, along_x(x_step[side]))
    ub[frames_of(c), :] = us[:, half(c)]

    @pl.when(t > 0)
    def _():
        to_after.wait_recv()
        xf[0:PAD, :] = hx[0].astype(F32)

    @pl.when(t == 0)
    def _():
        xf[0:PAD, :] = jnp.zeros((PAD, D), F32)

    @pl.when(t < 31)
    def _():
        to_before.wait_recv()
        xf[PAD + T:, :] = hx[1].astype(F32)

    @pl.when(t == 31)
    def _():
        xf[PAD + T:, :] = jnp.zeros((PAD, D), F32)

    for item in loads[3:]:
        item.wait()

    def conv(source, taps, forward):
        total = jnp.zeros((T, LANES), F32)
        for r in range(8):
            shifted = source[r:r + T + 24]
            for k in range(4):
                offset = 8 * k + r
                tap = offset - 1 if forward else TAPS - offset
                if 0 <= tap < TAPS:
                    total = total + taps[tap:tap + 1] * shifted[8 * k:8 * k + T]
        return total

    def conv_chunk(k, total):
        at_lanes = lanes_of(k)
        value = conv(xf[:, at_lanes], kern_ref[:, at_lanes], True) * live
        cv[:, at_lanes] = value
        return total + value

    zero = jnp.zeros((T, LANES), F32)
    total = lax.fori_loop(0, CHUNKS, conv_chunk, zero)

    for side in range(2):
        for n, from_y in ((0, y_down), (2, y_up)):
            here = rows_of(from_y, xl, side)
            landed(here, n + side)
            push(here, 8 + n + side, along_x(x_step[side]))
            if n == 0 and side == 0:
                push(here, 4, along_y(1))
            if n == 2 and side == 1:
                push(here, 5, along_y(3))

    average = jnp.broadcast_to(jnp.sum(total, axis=1, keepdims=True) * (1.0 / D), (T, LANES))

    def variance_chunk(k, total):
        centred = cv[:, lanes_of(k)] - average
        return total + centred * centred

    total = lax.fori_loop(0, CHUNKS, variance_chunk, zero)
    variance = jnp.sum(total, axis=1, keepdims=True) * (1.0 / D)
    inv = jnp.broadcast_to(lax.rsqrt(variance + 1e-05), (T, LANES))

    def act_chunk(k, _):
        at_lanes = lanes_of(k)
        normed = (cv[:, at_lanes] - average) * inv
        scaled = normed * gain_ref[at_lanes][None]
        gate = 1.0 / (1.0 + jnp.exp(-scaled))
        act = scaled * gate
        cv[:, at_lanes] = normed
        ds[:, at_lanes] = gate * (1.0 + scaled * (1.0 - gate))
        ab[frames_of(c), at_lanes] = act.astype(BF16)
        at[lanes_of(k), frames_of(c)] = act.T.astype(BF16)
        return 0

    swaps = []
    for part in range(3):
        lax.fori_loop(part * 4, part * 4 + 4, act_chunk, 0)
        cols = pl.ds(part * 512, 512)
        here = at.at[cols, frames_of(c)]
        swaps.append(send(here, here, sem_c_s.at[1 + part], sem_c_r.at[1 + part], mate))
        here = ab.at[frames_of(c), cols]
        swaps.append(send(here, here, sem_c_s.at[4 + part], sem_c_r.at[4 + part], mate))

    u_swap.wait_recv()
    for item in swaps[0::2]:
        item.wait_recv()

    def partial(n, start, width):
        rows = pl.ds(pl.multiple_of(n * 384, 384), 384)
        value = jnp.dot(at[rows, :], ub[:, start:start + width], preferred_element_type=F32)
        return value.reshape(4, 96, width).astype(BF16)

    y_first = []
    for i in (1, 3, 2, 0):
        to_y = (y + i) % 4
        py[to_y] = partial(to_y, CX, CY)
        if i:
            y_first.append(send(py.at[to_y], ry.at[i - 1], sem_p_s.at[2 + i], sem_p_r.at[2 + i], along_y(i)))

    for side in range(2):
        here = rows_of(y_far, xl, side)
        landed(here, 4 + side)
        push(here, 12 + side, along_x(x_step[side]))

    def partial_x(n, _):
        px[n] = partial(n, 0, CX)
        return 0

    lax.fori_loop(0, 4, partial_x, 0)
    x_first = [
        send(px.at[:, block_of((x + i) % 4)], rx.at[i - 1], sem_p_s.at[i - 1], sem_p_r.at[i - 1], along_x(i))
        for i in (1, 3, 2)
    ]

    ag_swaps = []
    for n, from_y in ((6, y), (8, y_down), (10, y_up), (12, y_far)):
        for side in range(2):
            landed(rows_of(from_y, 1 - xl, side), n + side)
        cols = pl.ds(pl.multiple_of(from_y * 384, 384), 384)
        value = lax.dot_general(
            ub[...], wb[cols, :], (((1,), (1,)), ((), ())), preferred_element_type=F32
        )
        agp[0, :, cols] = value[:T]
        agp[1, :, cols] = value[T:]
        k = len(ag_swaps)
        ag_swaps.append(
            send(agp.at[oc, :, cols], agr.at[:, cols], sem_c_s.at[7 + k], sem_c_r.at[7 + k], mate)
        )

    for item in swaps[1::2]:
        item.wait_recv()

    def project_chunk(n, _):
        cols = pl.ds(pl.multiple_of(n * 256, 256), 256)
        value = jnp.dot(ab[...], wb[:, cols], preferred_element_type=F32).astype(BF16)
        pj[0, :, cols] = value[:T]
        pj[1, :, cols] = value[T:]
        return 0

    lax.fori_loop(0, 3, project_chunk, 0)
    pj_swap = send(pj.at[oc], pjr, sem_c_s.at[11], sem_c_r.at[11], mate)
    proj_ref[:, half(c)] = pj[c]

    for item in ag_swaps:
        item.wait_recv()

    def back_chunk(k, sums):
        at_lanes = lanes_of(k)
        normed = cv[:, at_lanes]
        scaled_grad = (agp[c, :, at_lanes] + agr[:, at_lanes]) * ds[:, at_lanes]
        gkb[TAPS:TAPS + 1, at_lanes] = jnp.sum(scaled_grad * normed, axis=0, keepdims=True)
        normed_grad = scaled_grad * gain_ref[at_lanes][None]
        ds[:, at_lanes] = normed_grad
        return (sums[0] + normed_grad, sums[1] + normed_grad * normed)

    sums = lax.fori_loop(0, CHUNKS, back_chunk, (zero, zero))
    first, second = [
        jnp.broadcast_to(jnp.sum(s, axis=1, keepdims=True) * (1.0 / D), (T, LANES)) for s in sums
    ]
    inv_live = inv * live

    def conv_grad_chunk(k, _):
        at_lanes = lanes_of(k)
        cg[PAD:PAD + T, at_lanes] = inv_live * (ds[:, at_lanes] - first - cv[:, at_lanes] * second)
        return 0

    lax.fori_loop(0, CHUNKS, conv_grad_chunk, 0)

    g_before = copy(cg.at[pl.ds(PAD, PAD)], cg.at[pl.ds(PAD + T, PAD)], sem_halo_s.at[2], sem_halo_r.at[3], before)
    g_after = copy(cg.at[pl.ds(T, PAD)], cg.at[pl.ds(0, PAD)], sem_halo_s.at[3], sem_halo_r.at[2], after)

    @pl.when(t > 0)
    def _():
        g_before.start()

    @pl.when(t < 31)
    def _():
        g_after.start()

    def taps_chunk(k, _):
        at_lanes = lanes_of(k)
        source = xf[:, at_lanes]
        grad = cg[PAD:PAD + T, at_lanes]
        for r in range(8):
            shifted = source[r:r + T + 24]
            for j in range(4):
                tap = 8 * j + r - 1
                if 0 <= tap < TAPS:
                    gkb[tap:tap + 1, at_lanes] = jnp.sum(grad * shifted[8 * j:8 * j + T], axis=0, keepdims=True)
        return 0

    lax.fori_loop(0, CHUNKS, taps_chunk, 0)
    gk_swap = send(gkb.at[:, half(oc)], gcr, sem_t_s.at[0], sem_t_r.at[0], mate)

    @pl.when(t > 0)
    def _():
        g_after.wait_recv()

    @pl.when(t == 0)
    def _():
        cg[0:PAD, :] = jnp.zeros((PAD, D), F32)

    @pl.when(t < 31)
    def _():
        g_before.wait_recv()

    @pl.when(t == 31)
    def _():
        cg[PAD + T:, :] = jnp.zeros((PAD, D), F32)

    def input_chunk(k, _):
        at_lanes = lanes_of(k)
        value = conv(cg[:, at_lanes], kern_ref[:, at_lanes], False) * live
        gin_ref[:, at_lanes] = value.astype(BF16)
        return 0

    lax.fori_loop(0, 3, input_chunk, 0)

    def piece(z_):
        return (
            pl.ds(pl.multiple_of((z_ // 2) * 8, 8), 8),
            pl.ds(pl.multiple_of((z_ % 2) * 384, 384), 384),
        )

    gk_swap.wait_recv()
    gh[...] = gkb[:, half(c)] + gcr[...]
    t_z = [
        send(gh.at[piece((z + i) % 8)], zr.at[i - 1], sem_t_s.at[i], sem_t_r.at[i], along_z(i))
        for i in (4, 3, 5, 2, 6, 1, 7)
    ]

    lax.fori_loop(3, CHUNKS, input_chunk, 0)
    stores = [pltpu.make_async_copy(gin_ref, gin_hbm, sem_out.at[0])]
    stores[0].start()
    pj_swap.wait_recv()
    proj_ref[:, half(oc)] = pjr[...]
    stores.append(pltpu.make_async_copy(proj_ref, proj_hbm, sem_out.at[1]))
    stores[1].start()

    for item in t_z:
        item.wait_recv()
    mine_t = gh[piece(z)]
    for i in range(7):
        mine_t = mine_t + zr[i]
    xs[x] = mine_t
    for i in range(1, 4):
        send(xs.at[x], xs.at[x], sem_t_s.at[7 + i], sem_t_r.at[7 + i], along_x(i))

    for item in x_first:
        item.wait_recv()

    def add_x(n, _):
        value = px[n, q].astype(F32)
        for i in range(3):
            value = value + rx[i, n].astype(F32)
        s2x[n] = value.astype(BF16)
        return 0

    lax.fori_loop(0, 4, add_x, 0)
    x_second = [
        send(s2x.at[(y + i) % 4], r2x.at[i - 1], sem_p_s.at[5 + i], sem_p_r.at[5 + i], along_y(i))
        for i in range(1, 4)
    ]

    def wait_slots(slots, me, base):
        for i in range(1, 4):
            slot = slots.at[(me + 4 - i) % 4]
            copy(slot, slot, sem_t_s.at[base + i], sem_t_r.at[base + i], mate).wait_recv()

    wait_slots(xs, x, 7)
    ys[y] = xs[0] + xs[1] + xs[2] + xs[3]
    for i in range(1, 4):
        send(ys.at[y], ys.at[y], sem_t_s.at[10 + i], sem_t_r.at[10 + i], along_y(i))

    for item in y_first:
        item.wait_recv()

    def add_y(n, _):
        value = py[y, n].astype(F32)
        for i in range(3):
            value = value + ry[i, n].astype(F32)
        s2y[n] = value.astype(BF16)
        return 0

    lax.fori_loop(0, 4, add_y, 0)
    y_second = [
        send(s2y.at[block_of((x + i) % 4)], r2y.at[i - 1], sem_p_s.at[8 + i], sem_p_r.at[8 + i], along_x(i))
        for i in range(1, 4)
    ]

    wait_slots(ys, y, 10)
    fg[piece(z)] = ys[0] + ys[1] + ys[2] + ys[3]
    for i in (4, 3, 5, 2, 6, 1, 7):
        here = fg.at[piece(z)]
        send(here, here, sem_t_s.at[13 + i], sem_t_r.at[13 + i], along_z(i))

    for item in x_second + y_second:
        item.wait_recv()
    left, right = s2x[y].astype(F32), s2y[q].astype(F32)
    for i in range(3):
        left = left + r2x[i].astype(F32)
        right = right + r2y[i].astype(F32)
    facc[0:96, 0:CX] = left
    facc[0:96, CX:H] = right
    facc[96:104, :] = jnp.zeros((8, H), F32)
    for n in range(8):
        zs[n] = facc[12 * n:12 * n + 16, :].astype(BF16)
    w_z = [
        send(zs.at[(z + i) % 8], rz.at[i - 1], sem_z_s.at[i - 1], sem_z_r.at[i - 1], along_z(i))
        for i in (4, 3, 5, 2, 6, 1, 7)
    ]

    for i in range(1, 8):
        slot = fg.at[piece((z + 8 - i) % 8)]
        copy(slot, slot, sem_t_s.at[13 + i], sem_t_r.at[13 + i], mate).wait_recv()
    t_swap = send(fg, fgr, sem_t_s.at[21], sem_t_r.at[21], mate)

    for item in w_z:
        item.wait_recv()
    rows = zs[z].astype(F32)
    for i in range(7):
        rows = rows + rz[i].astype(F32)
    fin[...] = jnp.zeros((2, 8, H), F32)
    fin[0, 0:6, :] = rows[0:6]
    fin[1, 0:6, :] = rows[6:12]
    w_swap = send(fin.at[oc], cr, sem_z_s.at[7], sem_z_r.at[7], mate)

    def put_taps(cols, value):
        gk_ref[:, cols] = value[0:TAPS]
        gg_ref[:, cols] = value[TAPS:TAPS + 1]

    put_taps(half(c), fg[...])
    gw_ref[:, half(c)] = fin[c][0:6]
    t_swap.wait_recv()
    put_taps(half(oc), fgr[...])
    w_swap.wait_recv()
    gw_ref[:, half(oc)] = cr[0:6, :]
    for n, (src, dst) in enumerate(((gw_ref, gw_hbm), (gk_ref, gk_hbm), (gg_ref, gg_hbm))):
        stores.append(pltpu.make_async_copy(src, dst, sem_out.at[2 + n]))
        stores[-1].start()

    @pl.when(t > 0)
    def _():
        to_before.wait_send()
        g_before.wait_send()

    @pl.when(t < 31)
    def _():
        to_after.wait_send()
        g_after.wait_send()

    for item in started:
        item.wait_send()
    for item in stores:
        item.wait()


def deliver(*refs):
    sources, results, kept, sems = refs[:5], refs[5:10], refs[10:15], refs[15]
    loads = [pltpu.make_async_copy(a, b, sems.at[n]) for n, (a, b) in enumerate(zip(sources, kept))]
    stores = [pltpu.make_async_copy(a, b, sems.at[5 + n]) for n, (a, b) in enumerate(zip(kept, results))]
    for item in loads:
        item.start()
    for first, then in zip(loads, stores):
        first.wait()
        then.start()
    for item in stores:
        item.wait()


def on_device(inputs, lengths, kernel, norm_gain, weight, cotangent):
    vmem = pl.BlockSpec(memory_space=pltpu.VMEM)
    dma = pltpu.SemaphoreType.DMA
    scratch = [
        pltpu.VMEM((T, D), BF16),
        pltpu.VMEM((TAPS, D), F32),
        pltpu.VMEM((D,), F32),
        pltpu.VMEM((T, D), BF16),
        pltpu.VMEM((T, D), BF16),
        pltpu.VMEM((T, D), BF16),
        pltpu.VMEM((6, D), F32),
        pltpu.VMEM((TAPS, D), F32),
        pltpu.VMEM((1, D), F32),
        pltpu.VMEM((T, D), BF16),
        pltpu.VMEM((2, PAD, D), BF16),
        pltpu.VMEM((T + 2 * PAD, D), F32),
        pltpu.VMEM((T, D), F32),
        pltpu.VMEM((T, D), F32),
        pltpu.VMEM((2 * T, D), BF16),
        pltpu.VMEM((D, 2 * T), BF16),
        pltpu.VMEM((T, D), BF16),
        pltpu.VMEM((2 * T, H), BF16),
        pltpu.VMEM((D, H), BF16),
        pltpu.VMEM((4, 4, 96, CX), BF16),
        pltpu.VMEM((4, 4, 96, CY), BF16),
        pltpu.VMEM((3, 4, 96, CX), BF16),
        pltpu.VMEM((3, 4, 96, CY), BF16),
        pltpu.VMEM((4, 96, CX), BF16),
        pltpu.VMEM((4, 96, CY), BF16),
        pltpu.VMEM((3, 96, CX), BF16),
        pltpu.VMEM((3, 96, CY), BF16),
        pltpu.VMEM((104, H), F32),
        pltpu.VMEM((8, 16, H), BF16),
        pltpu.VMEM((7, 16, H), BF16),
        pltpu.VMEM((2, 8, H), F32),
        pltpu.VMEM((8, H), F32),
        pltpu.VMEM((2, T, D), F32),
        pltpu.VMEM((T, D), F32),
        pltpu.VMEM((2, T, H), BF16),
        pltpu.VMEM((T, H), BF16),
        pltpu.VMEM((T + 2 * PAD, D), F32),
        pltpu.VMEM((32, D), F32),
        pltpu.VMEM((32, H), F32),
        pltpu.VMEM((32, H), F32),
        pltpu.VMEM((7, 8, 384), F32),
        pltpu.VMEM((4, 8, 384), F32),
        pltpu.VMEM((4, 8, 384), F32),
        pltpu.VMEM((32, H), F32),
        pltpu.VMEM((32, H), F32),
        dma((4,)), dma((4,)),
        dma((14,)), dma((14,)),
        dma((12,)), dma((12,)),
        dma((12,)), dma((12,)),
        dma((8,)), dma((8,)),
        dma((22,)), dma((22,)),
        dma((5,)), dma((5,)),
    ]
    hbm = pl.BlockSpec(memory_space=pl.ANY)
    shapes = (
        jax.ShapeDtypeStruct((T, D), BF16),
        jax.ShapeDtypeStruct((T, D), BF16),
        jax.ShapeDtypeStruct((6, D), F32),
        jax.ShapeDtypeStruct((TAPS, D), F32),
        jax.ShapeDtypeStruct((1, D), F32),
    )
    results = pl.pallas_call(
        fused,
        out_shape=shapes,
        in_specs=[hbm, pl.BlockSpec(memory_space=pltpu.SMEM), hbm, hbm, hbm, hbm],
        out_specs=[hbm] * 5,
        scratch_shapes=scratch,
        compiler_params=pltpu.CompilerParams(
            collective_id=0, has_side_effects=True, vmem_limit_bytes=60 << 20
        ),
        name="conv_module",
    )(inputs[0], lengths, kernel, norm_gain, weight, cotangent[0])
    projected, grad_input, grad_weight, grad_kernel, grad_gain = pl.pallas_call(
        deliver,
        out_shape=shapes,
        in_specs=[hbm] * 5,
        out_specs=[hbm] * 5,
        scratch_shapes=[pltpu.VMEM(r.shape, r.dtype) for r in shapes] + [dma((10,))],
        compiler_params=pltpu.CompilerParams(vmem_limit_bytes=60 << 20),
        name="deliver",
    )(*results)
    return (projected[None], grad_input[None], grad_weight, grad_kernel, grad_gain[0])


def solution(mesh):
    in_specs = (
        P("batch", "tm", None),
        P("batch"),
        P(),
        P(),
        P("batch", None),
        P("batch", "tm", None),
    )
    out_specs = (P("batch", "tm", None), P("batch", "tm", None), P(("batch", "tm"), None), P(), P())
    return jax.shard_map(
        on_device, mesh=mesh, in_specs=in_specs, out_specs=out_specs, check_vma=False
    )
```

```python
import jax
import jax.numpy as jnp
from jax import lax
from jax.experimental import pallas as pl
from jax.experimental.pallas import tpu as pltpu
from jax.sharding import PartitionSpec as P

F32, BF16 = jnp.float32, jnp.bfloat16
MESH = pl.DeviceIdType.MESH
D, T, H, TAPS = 1536, 128, 768, 31
PAD = 16
CX, CY = 256, 512
LANES = 128
CHUNKS = D // LANES


def lanes_of(k):
    return pl.ds(pl.multiple_of(k * LANES, LANES), LANES)


def fused(
    x_hbm, len_hbm, kern_hbm, gain_hbm, w_hbm, cot_hbm,
    proj_hbm, gin_hbm, gw_hbm, gk_hbm, gg_hbm,
    len_ref, x_ref, kern_ref, gain_ref, cot_ref, proj_ref, gin_ref, gw_ref, gk_ref, gg_ref,
    xm, hx, xf, cv, ds, rs_sum, ab, tf, tp, at2, atm, us, ub, wb, px, py, rx, ry, s2x, s2y, r2x, r2y,
    facc, zs, rz, fin, cr, agp, agr, pj, pjr, cg, gkb, gcr, gh, zr, xs, ys, fg, fgr,
    sem_halo_s, sem_halo_r, sem_w_s, sem_w_r, sem_c_s, sem_c_r, sem_p_s, sem_p_r,
    sem_z_s, sem_z_r, sem_t_s, sem_t_r, sem_a_s, sem_a_r, sem_in, sem_out,
):
    b = lax.axis_index("batch")
    t = lax.axis_index("tm")
    y, xl = b // 2, b % 2
    xh, z, c = t // 16, (t // 2) % 8, t % 2
    x = xh * 2 + xl
    oc = 1 - c

    def dev(y_, x_, z_, c_):
        return (y_ * 2 + x_ % 2, (x_ // 2) * 16 + z_ * 2 + c_)

    def along_y(i):
        return dev((y + i) % 4, x, z, c)

    def along_x(i):
        return dev(y, (x + i) % 4, z, c)

    def along_z(i):
        return dev(y, x, (z + i) % 8, c)

    mate = dev(y, x, z, oc)
    zp = z % 2
    z_mate = z + 1 - 2 * zp
    across, diagonal = dev(y, x, z_mate, c), dev(y, x, z_mate, oc)
    before, after = (b, t - 1), (b, t + 1)

    def block_of(x_):
        return (x_ % 2) * 2 + x_ // 2

    q = block_of(x)

    def half(c_):
        return pl.ds(pl.multiple_of(c_ * H, H), H)

    def frames_of(c_):
        return pl.ds(pl.multiple_of(c_ * T, T), T)

    started = []

    def copy(src, dst, ss, rs, to):
        return pltpu.make_async_remote_copy(
            src_ref=src, dst_ref=dst, send_sem=ss, recv_sem=rs, device_id=to, device_id_type=MESH
        )

    def send(*args):
        item = copy(*args)
        item.start()
        started.append(item)
        return item

    barrier = pltpu.get_barrier_semaphore()

    def greet(to):
        pl.semaphore_signal(barrier, inc=1, device_id=to, device_id_type=MESH)

    greet(mate)
    greet(diagonal)
    for i in range(1, 4):
        greet(along_y(i))
        greet(along_x(i))
    for i in range(1, 8):
        greet(along_z(i))

    @pl.when(t > 0)
    def _():
        greet(before)

    @pl.when(t < 31)
    def _():
        greet(after)

    w_own = pl.ds(pl.multiple_of((y * 2 + xl) * 192, 192), 192)
    loads = [
        pltpu.make_async_copy(src, dst, sem_in.at[n])
        for n, (src, dst) in enumerate((
            (x_hbm, x_ref), (cot_hbm, cot_ref), (w_hbm.at[:, half(c)], wb.at[w_own]),
            (kern_hbm, kern_ref), (gain_hbm, gain_ref), (len_hbm, len_ref),
        ))
    ]
    for item in loads:
        item.start()
    loads[5].wait()
    position = t * T + lax.broadcasted_iota(jnp.int32, (T, LANES), 0)
    live = jnp.where(position < len_ref[0], 1.0, 0.0).astype(F32)
    for item in loads[:2]:
        item.wait()

    def mask_chunk(k, _):
        at_lanes = lanes_of(k)
        masked = x_ref[:, at_lanes].astype(F32) * live
        xm[:, at_lanes] = masked.astype(BF16)
        xf[PAD:PAD + T, at_lanes] = masked
        us[:, at_lanes] = (cot_ref[:, at_lanes].astype(F32) * live).astype(BF16)
        return 0

    lax.fori_loop(0, CHUNKS, mask_chunk, 0)

    others = 15 + jnp.where(t > 0, 1, 0) + jnp.where(t < 31, 1, 0)
    pl.semaphore_wait(barrier, others)

    to_before = copy(xm.at[pl.ds(0, PAD)], hx.at[1], sem_halo_s.at[0], sem_halo_r.at[1], before)
    to_after = copy(xm.at[pl.ds(T - PAD, PAD)], hx.at[0], sem_halo_s.at[1], sem_halo_r.at[0], after)

    @pl.when(t > 0)
    def _():
        to_before.start()

    @pl.when(t < 31)
    def _():
        to_after.start()

    mine = zp * 2 + c
    u_swaps = [send(us.at[:, half(oc)], ub.at[frames_of(mine)], sem_c_s.at[0], sem_c_r.at[0], mate)]

    def rows_of(y_, xl_, side):
        return wb.at[pl.ds(pl.multiple_of((y_ * 2 + xl_) * 192 + side * 96, 96), 96)]

    y_up, y_down, y_far = (y + 1) % 4, (y + 3) % 4, (y + 2) % 4
    x_step = (1, 3)

    def push(here, n, to):
        send(here, here, sem_w_s.at[n], sem_w_r.at[n], to)

    def landed(here, n):
        copy(here, here, sem_w_s.at[n], sem_w_r.at[n], mate).wait_recv()

    loads[2].wait()
    for side in range(2):
        own = rows_of(y, xl, side)
        push(own, side, along_y(1))
        push(own, 2 + side, along_y(3))
        push(own, 6 + side, along_x(x_step[side]))
    u_swaps += [
        send(us.at[:, half(c_)], ub.at[frames_of(mine)], sem_a_s.at[n], sem_a_r.at[n], to)
        for n, c_, to in ((0, c, across), (1, oc, diagonal))
    ]
    ub[frames_of(mine), :] = us[:, half(c)]

    for item in loads[3:5]:
        item.wait()

    def conv(source, taps, forward):
        count = source.shape[0] - 32
        total = jnp.zeros((count, LANES), F32)
        for r in range(8):
            shifted = source[r:r + count + 24]
            for k in range(4):
                offset = 8 * k + r
                tap = offset - 1 if forward else TAPS - offset
                if 0 <= tap < TAPS:
                    total = total + taps[tap:tap + 1] * shifted[8 * k:8 * k + count]
        return total

    def conv_chunk(start, count):
        def body(k, total):
            at_lanes = lanes_of(k)
            value = conv(xf[start:start + count + 32, at_lanes], kern_ref[:, at_lanes], True)
            value = value * live[start:start + count]
            cv[start:start + count, at_lanes] = value
            return total + value
        rs_sum[start:start + count, :] = lax.fori_loop(0, CHUNKS, body, jnp.zeros((count, LANES), F32))

    conv_chunk(PAD, T - 2 * PAD)

    @pl.when(t > 0)
    def _():
        to_after.wait_recv()
        xf[0:PAD, :] = hx[0].astype(F32)

    @pl.when(t == 0)
    def _():
        xf[0:PAD, :] = jnp.zeros((PAD, D), F32)

    @pl.when(t < 31)
    def _():
        to_before.wait_recv()
        xf[PAD + T:, :] = hx[1].astype(F32)

    @pl.when(t == 31)
    def _():
        xf[PAD + T:, :] = jnp.zeros((PAD, D), F32)

    conv_chunk(0, PAD)
    conv_chunk(T - PAD, PAD)

    zero = jnp.zeros((T, LANES), F32)
    total = rs_sum[...]
    average = jnp.broadcast_to(jnp.sum(total, axis=1, keepdims=True) * (1.0 / D), (T, LANES))

    def variance_chunk(k, total):
        centred = cv[:, lanes_of(k)] - average
        return total + centred * centred

    total = lax.fori_loop(0, CHUNKS, variance_chunk, zero)
    variance = jnp.sum(total, axis=1, keepdims=True) * (1.0 / D)
    inv = jnp.broadcast_to(lax.rsqrt(variance + 1e-05), (T, LANES))

    def act_chunk(k, _):
        at_lanes = lanes_of(k)
        normed = (cv[:, at_lanes] - average) * inv
        scaled = normed * gain_ref[at_lanes][None]
        gate = 1.0 / (1.0 + jnp.exp(-scaled))
        act = scaled * gate
        cv[:, at_lanes] = normed
        ds[:, at_lanes] = gate * (1.0 + scaled * (1.0 - gate))
        ab[frames_of(c), at_lanes] = act.astype(BF16)
        tf[pl.ds(pl.multiple_of((k % 3) * LANES, LANES), LANES), :] = act.T
        return 0

    swaps, z_swaps, a_swaps = [], [], []
    for part in range(4):
        lax.fori_loop(part * 3, part * 3 + 3, act_chunk, 0)
        for parity in range(2):
            for g in range(16):
                tp[12 * g:12 * g + 12, :] = tf[24 * g + 12 * parity:24 * g + 12 * parity + 12, :]
            at2[parity, part * 192:part * 192 + 192, :] = tp[...].astype(BF16)
        rows = pl.ds(part * 192, 192)
        there = atm.at[rows, frames_of(mine)]
        z_swaps.append(send(at2.at[1 - zp, rows], there, sem_a_s.at[2 + part], sem_a_r.at[2 + part], across))
        swaps.append(send(at2.at[zp, rows], there, sem_c_s.at[1 + part], sem_c_r.at[1 + part], mate))
        atm[rows, frames_of(mine)] = at2[zp, part * 192:part * 192 + 192, :]
    here = ab.at[frames_of(c)]
    a_swaps.append(send(here, here, sem_c_s.at[5], sem_c_r.at[5], mate))

    for side in range(2):
        for n, from_y in ((0, y_down), (2, y_up)):
            here = rows_of(from_y, xl, side)
            landed(here, n + side)
            push(here, 8 + n + side, along_x(x_step[side]))
            if n == 0 and side == 0:
                push(here, 4, along_y(1))
            if n == 2 and side == 1:
                push(here, 5, along_y(3))

    theirs = (1 - zp) * 2 + c
    for part in range(4):
        z_swaps[part].wait_recv()
        here = atm.at[pl.ds(part * 192, 192), frames_of(theirs)]
        swaps.append(send(here, here, sem_a_s.at[6 + part], sem_a_r.at[6 + part], mate))

    for side in range(2):
        here = rows_of(y_far, xl, side)
        landed(here, 4 + side)
        push(here, 12 + side, along_x(x_step[side]))

    for item in u_swaps + swaps:
        item.wait_recv()

    def partial(n, start, width):
        rows = pl.ds(pl.multiple_of(n * 192, 192), 192)
        value = jnp.dot(atm[rows, :], ub[:, start:start + width], preferred_element_type=F32)
        return value.reshape(4, 48, width).astype(BF16)

    y_first = []
    for i in (1, 3, 2, 0):
        to_y = (y + i) % 4
        py[to_y] = partial(to_y, CX, CY)
        if i:
            y_first.append(send(py.at[to_y], ry.at[i - 1], sem_p_s.at[2 + i], sem_p_r.at[2 + i], along_y(i)))

    def partial_x(n, _):
        px[n] = partial(n, 0, CX)
        return 0

    lax.fori_loop(0, 4, partial_x, 0)
    x_first = [
        send(px.at[:, block_of((x + i) % 4)], rx.at[i - 1], sem_p_s.at[i - 1], sem_p_r.at[i - 1], along_x(i))
        for i in (1, 3, 2)
    ]

    ag_swaps = []
    chip_rows = pl.ds(pl.multiple_of(zp * 2 * T, 2 * T), 2 * T)
    for n, from_y in ((6, y), (8, y_down), (10, y_up), (12, y_far)):
        for side in range(2):
            landed(rows_of(from_y, 1 - xl, side), n + side)
        cols = pl.ds(pl.multiple_of(from_y * 384, 384), 384)
        value = lax.dot_general(
            ub[chip_rows, :], wb[cols, :], (((1,), (1,)), ((), ())), preferred_element_type=F32
        )
        agp[0, :, cols] = value[:T]
        agp[1, :, cols] = value[T:]
        k = len(ag_swaps)
        ag_swaps.append(
            send(agp.at[oc, :, cols], agr.at[:, cols], sem_c_s.at[6 + k], sem_c_r.at[6 + k], mate)
        )

    for item in a_swaps:
        item.wait_recv()

    def project_chunk(n, _):
        cols = pl.ds(pl.multiple_of(n * 256, 256), 256)
        value = jnp.dot(ab[...], wb[:, cols], preferred_element_type=F32).astype(BF16)
        pj[0, :, cols] = value[:T]
        pj[1, :, cols] = value[T:]
        return 0

    lax.fori_loop(0, 3, project_chunk, 0)
    pj_swap = send(pj.at[oc], pjr, sem_c_s.at[10], sem_c_r.at[10], mate)
    proj_ref[:, half(c)] = pj[c]

    for item in ag_swaps:
        item.wait_recv()

    def back_chunk(k, sums):
        at_lanes = lanes_of(k)
        normed = cv[:, at_lanes]
        scaled_grad = (agp[c, :, at_lanes] + agr[:, at_lanes]) * ds[:, at_lanes]
        gkb[TAPS:TAPS + 1, at_lanes] = jnp.sum(scaled_grad * normed, axis=0, keepdims=True)
        normed_grad = scaled_grad * gain_ref[at_lanes][None]
        ds[:, at_lanes] = normed_grad
        return (sums[0] + normed_grad, sums[1] + normed_grad * normed)

    sums = lax.fori_loop(0, CHUNKS, back_chunk, (zero, zero))
    first, second = [
        jnp.broadcast_to(jnp.sum(s, axis=1, keepdims=True) * (1.0 / D), (T, LANES)) for s in sums
    ]
    inv_live = inv * live

    def conv_grad_chunk(k, _):
        at_lanes = lanes_of(k)
        cg[PAD:PAD + T, at_lanes] = inv_live * (ds[:, at_lanes] - first - cv[:, at_lanes] * second)
        return 0

    lax.fori_loop(0, CHUNKS, conv_grad_chunk, 0)

    g_before = copy(cg.at[pl.ds(PAD, PAD)], cg.at[pl.ds(PAD + T, PAD)], sem_halo_s.at[2], sem_halo_r.at[3], before)
    g_after = copy(cg.at[pl.ds(T, PAD)], cg.at[pl.ds(0, PAD)], sem_halo_s.at[3], sem_halo_r.at[2], after)

    @pl.when(t > 0)
    def _():
        g_before.start()

    @pl.when(t < 31)
    def _():
        g_after.start()

    def taps_chunk(k, _):
        at_lanes = lanes_of(k)
        source = xf[:, at_lanes]
        grad = cg[PAD:PAD + T, at_lanes]
        for r in range(8):
            shifted = source[r:r + T + 24]
            for j in range(4):
                tap = 8 * j + r - 1
                if 0 <= tap < TAPS:
                    gkb[tap:tap + 1, at_lanes] = jnp.sum(grad * shifted[8 * j:8 * j + T], axis=0, keepdims=True)
        return 0

    lax.fori_loop(oc * 6, oc * 6 + 6, taps_chunk, 0)
    gk_swap = send(gkb.at[:, half(oc)], gcr, sem_t_s.at[0], sem_t_r.at[0], mate)
    lax.fori_loop(c * 6, c * 6 + 6, taps_chunk, 0)

    def piece(z_):
        return (
            pl.ds(pl.multiple_of((z_ // 2) * 8, 8), 8),
            pl.ds(pl.multiple_of((z_ % 2) * 384, 384), 384),
        )

    gk_swap.wait_recv()
    gh[...] = gkb[:, half(c)] + gcr[...]
    t_z = [
        send(gh.at[piece((z + i) % 8)], zr.at[i - 1], sem_t_s.at[i], sem_t_r.at[i], along_z(i))
        for i in (4, 3, 5, 2, 6, 1, 7)
    ]

    def add(first, own, came, out):
        for item in first:
            item.wait_recv()

        def body(n, _):
            value = own(n).astype(F32)
            for i in range(3):
                value = value + came[i, n].astype(F32)
            out[n] = value.astype(BF16)
            return 0

        lax.fori_loop(0, 4, body, 0)

    add(x_first, lambda n: px[n, q], rx, s2x)
    x_second = [
        send(s2x.at[(y + i) % 4], r2x.at[i - 1], sem_p_s.at[5 + i], sem_p_r.at[5 + i], along_y(i))
        for i in (2, 1, 3)
    ]
    add(y_first, lambda n: py[y, n], ry, s2y)
    y_second = [
        send(s2y.at[block_of((x + i) % 4)], r2y.at[i - 1], sem_p_s.at[8 + i], sem_p_r.at[8 + i], along_x(i))
        for i in (2, 1, 3)
    ]

    @pl.when(t > 0)
    def _():
        g_after.wait_recv()

    @pl.when(t == 0)
    def _():
        cg[0:PAD, :] = jnp.zeros((PAD, D), F32)

    @pl.when(t < 31)
    def _():
        g_before.wait_recv()

    @pl.when(t == 31)
    def _():
        cg[PAD + T:, :] = jnp.zeros((PAD, D), F32)

    def input_chunk(k, _):
        at_lanes = lanes_of(k)
        value = conv(cg[:, at_lanes], kern_ref[:, at_lanes], False) * live
        gin_ref[:, at_lanes] = value.astype(BF16)
        return 0

    lax.fori_loop(0, 6, input_chunk, 0)

    for item in t_z:
        item.wait_recv()
    mine_t = gh[piece(z)]
    for i in range(7):
        mine_t = mine_t + zr[i]
    xs[x] = mine_t
    for i in (2, 1, 3):
        send(xs.at[x], xs.at[x], sem_t_s.at[7 + i], sem_t_r.at[7 + i], along_x(i))

    def wait_slots(slots, me, base):
        for i in range(1, 4):
            slot = slots.at[(me + 4 - i) % 4]
            copy(slot, slot, sem_t_s.at[base + i], sem_t_r.at[base + i], mate).wait_recv()

    for item in x_second + y_second:
        item.wait_recv()
    left, right = s2x[y].astype(F32), s2y[q].astype(F32)
    for i in range(3):
        left = left + r2x[i].astype(F32)
        right = right + r2y[i].astype(F32)
    facc[0:48, 0:CX] = left
    facc[0:48, CX:H] = right
    facc[48:56, :] = jnp.zeros((8, H), F32)
    for n in range(4):
        zs[n] = facc[12 * n:12 * n + 16, :].astype(BF16)
    w_z = [
        send(zs.at[(z // 2 + i) % 4], rz.at[i - 1], sem_z_s.at[i - 1], sem_z_r.at[i - 1], along_z(2 * i))
        for i in (2, 1, 3)
    ]

    wait_slots(xs, x, 7)
    ys[y] = xs[0] + xs[1] + xs[2] + xs[3]
    for i in (2, 1, 3):
        send(ys.at[y], ys.at[y], sem_t_s.at[10 + i], sem_t_r.at[10 + i], along_y(i))
    lax.fori_loop(6, CHUNKS, input_chunk, 0)
    wait_slots(ys, y, 10)
    fg[piece(z)] = ys[0] + ys[1] + ys[2] + ys[3]
    for i in (4, 3, 5, 2, 6, 1, 7):
        here = fg.at[piece(z)]
        send(here, here, sem_t_s.at[13 + i], sem_t_r.at[13 + i], along_z(i))

    stores = [pltpu.make_async_copy(gin_ref, gin_hbm, sem_out.at[0])]
    stores[0].start()
    pj_swap.wait_recv()
    proj_ref[:, half(oc)] = pjr[...]
    stores.append(pltpu.make_async_copy(proj_ref, proj_hbm, sem_out.at[1]))
    stores[1].start()

    for item in w_z:
        item.wait_recv()
    rows = zs[z // 2].astype(F32)
    for i in range(3):
        rows = rows + rz[i].astype(F32)
    fin[...] = jnp.zeros((2, 8, H), F32)
    fin[0, 0:6, :] = rows[0:6]
    fin[1, 0:6, :] = rows[6:12]
    w_swap = send(fin.at[oc], cr, sem_z_s.at[3], sem_z_r.at[3], mate)

    for i in range(1, 8):
        slot = fg.at[piece((z + 8 - i) % 8)]
        copy(slot, slot, sem_t_s.at[13 + i], sem_t_r.at[13 + i], mate).wait_recv()
    t_swap = send(fg, fgr, sem_t_s.at[21], sem_t_r.at[21], mate)

    def put_taps(cols, value):
        gk_ref[:, cols] = value[0:TAPS]
        gg_ref[:, cols] = value[TAPS:TAPS + 1]

    put_taps(half(c), fg[...])
    gw_ref[:, half(c)] = fin[c][0:6]
    t_swap.wait_recv()
    put_taps(half(oc), fgr[...])
    w_swap.wait_recv()
    gw_ref[:, half(oc)] = cr[0:6, :]
    for n, (src, dst) in enumerate(((gw_ref, gw_hbm), (gk_ref, gk_hbm), (gg_ref, gg_hbm))):
        stores.append(pltpu.make_async_copy(src, dst, sem_out.at[2 + n]))
        stores[-1].start()

    @pl.when(t > 0)
    def _():
        to_before.wait_send()
        g_before.wait_send()

    @pl.when(t < 31)
    def _():
        to_after.wait_send()
        g_after.wait_send()

    for item in started:
        item.wait_send()
    for item in stores:
        item.wait()


def deliver(*refs):
    sources, results, kept, sems = refs[:5], refs[5:10], refs[10:15], refs[15]
    loads = [pltpu.make_async_copy(a, b, sems.at[n]) for n, (a, b) in enumerate(zip(sources, kept))]
    stores = [pltpu.make_async_copy(a, b, sems.at[5 + n]) for n, (a, b) in enumerate(zip(kept, results))]
    for item in loads:
        item.start()
    for first, then in zip(loads, stores):
        first.wait()
        then.start()
    for item in stores:
        item.wait()


def on_device(inputs, lengths, kernel, norm_gain, weight, cotangent):
    vmem = pl.BlockSpec(memory_space=pltpu.VMEM)
    dma = pltpu.SemaphoreType.DMA
    scratch = [
        pltpu.SMEM((1,), jnp.int32),
        pltpu.VMEM((T, D), BF16),
        pltpu.VMEM((TAPS, D), F32),
        pltpu.VMEM((D,), F32),
        pltpu.VMEM((T, D), BF16),
        pltpu.VMEM((T, D), BF16),
        pltpu.VMEM((T, D), BF16),
        pltpu.VMEM((6, D), F32),
        pltpu.VMEM((TAPS, D), F32),
        pltpu.VMEM((1, D), F32),
        pltpu.VMEM((T, D), BF16),
        pltpu.VMEM((2, PAD, D), BF16),
        pltpu.VMEM((T + 2 * PAD, D), F32),
        pltpu.VMEM((T, D), F32),
        pltpu.VMEM((T, D), F32),
        pltpu.VMEM((T, LANES), F32),
        pltpu.VMEM((2 * T, D), BF16),
        pltpu.VMEM((3 * LANES, T), F32),
        pltpu.VMEM((192, T), F32),
        pltpu.VMEM((2, H, T), BF16),
        pltpu.VMEM((H, 4 * T), BF16),
        pltpu.VMEM((T, D), BF16),
        pltpu.VMEM((4 * T, H), BF16),
        pltpu.VMEM((D, H), BF16),
        pltpu.VMEM((4, 4, 48, CX), BF16),
        pltpu.VMEM((4, 4, 48, CY), BF16),
        pltpu.VMEM((3, 4, 48, CX), BF16),
        pltpu.VMEM((3, 4, 48, CY), BF16),
        pltpu.VMEM((4, 48, CX), BF16),
        pltpu.VMEM((4, 48, CY), BF16),
        pltpu.VMEM((3, 48, CX), BF16),
        pltpu.VMEM((3, 48, CY), BF16),
        pltpu.VMEM((56, H), F32),
        pltpu.VMEM((4, 16, H), BF16),
        pltpu.VMEM((3, 16, H), BF16),
        pltpu.VMEM((2, 8, H), F32),
        pltpu.VMEM((8, H), F32),
        pltpu.VMEM((2, T, D), F32),
        pltpu.VMEM((T, D), F32),
        pltpu.VMEM((2, T, H), BF16),
        pltpu.VMEM((T, H), BF16),
        pltpu.VMEM((T + 2 * PAD, D), F32),
        pltpu.VMEM((32, D), F32),
        pltpu.VMEM((32, H), F32),
        pltpu.VMEM((32, H), F32),
        pltpu.VMEM((7, 8, 384), F32),
        pltpu.VMEM((4, 8, 384), F32),
        pltpu.VMEM((4, 8, 384), F32),
        pltpu.VMEM((32, H), F32),
        pltpu.VMEM((32, H), F32),
        dma((4,)), dma((4,)),
        dma((14,)), dma((14,)),
        dma((12,)), dma((12,)),
        dma((12,)), dma((12,)),
        dma((8,)), dma((8,)),
        dma((22,)), dma((22,)),
        dma((10,)), dma((10,)),
        dma((6,)), dma((5,)),
    ]
    hbm = pl.BlockSpec(memory_space=pl.ANY)
    shapes = (
        jax.ShapeDtypeStruct((T, D), BF16),
        jax.ShapeDtypeStruct((T, D), BF16),
        jax.ShapeDtypeStruct((6, D), F32),
        jax.ShapeDtypeStruct((TAPS, D), F32),
        jax.ShapeDtypeStruct((1, D), F32),
    )
    results = pl.pallas_call(
        fused,
        out_shape=shapes,
        in_specs=[hbm] * 6,
        out_specs=[hbm] * 5,
        scratch_shapes=scratch,
        compiler_params=pltpu.CompilerParams(
            collective_id=0, has_side_effects=True, vmem_limit_bytes=60 << 20
        ),
        name="conv_module",
    )(inputs[0], lengths, kernel, norm_gain, weight, cotangent[0])
    projected, grad_input, grad_weight, grad_kernel, grad_gain = pl.pallas_call(
        deliver,
        out_shape=shapes,
        in_specs=[hbm] * 5,
        out_specs=[hbm] * 5,
        scratch_shapes=[pltpu.VMEM(r.shape, r.dtype) for r in shapes] + [dma((10,))],
        compiler_params=pltpu.CompilerParams(vmem_limit_bytes=60 << 20),
        name="deliver",
    )(*results)
    return (projected[None], grad_input[None], grad_weight, grad_kernel, grad_gain[0])


def solution(mesh):
    in_specs = (
        P("batch", "tm", None),
        P("batch"),
        P(),
        P(),
        P("batch", None),
        P("batch", "tm", None),
    )
    out_specs = (P("batch", "tm", None), P("batch", "tm", None), P(("batch", "tm"), None), P(), P())
    return jax.shard_map(
        on_device, mesh=mesh, in_specs=in_specs, out_specs=out_specs, check_vma=False
    )
```

```python
import jax
import jax.numpy as jnp
from jax import lax
from jax.experimental import pallas as pl
from jax.experimental.pallas import tpu as pltpu
from jax.sharding import PartitionSpec as P

F32, BF16 = jnp.float32, jnp.bfloat16
MESH = pl.DeviceIdType.MESH
D, T, H, TAPS = 1536, 128, 768, 31
PAD = 16
CX, CY = 384, 384
LANES = 128
CHUNKS = D // LANES


def lanes_of(k):
    return pl.ds(pl.multiple_of(k * LANES, LANES), LANES)


def fused(
    x_hbm, len_hbm, kern_hbm, gain_hbm, w_hbm, cot_hbm,
    proj_hbm, gin_hbm, gw_hbm, gk_hbm, gg_hbm,
    len_ref, x_ref, kern_ref, gain_ref, cot_ref, proj_ref, gin_ref, gw_ref, gk_ref, gg_ref,
    xm, hx, xf, cv, ds, rs_sum, ab, tf, tp, at2, atm, us, ub, wb, px, py, rx, ry, s2x, s2y, r2x, r2y,
    facc, zs, rz, fin, cr, agp, agr, pj, pjr, cg, gkb, gcr, gh, zr, xs, fg, fgr,
    sem_halo_s, sem_halo_r, sem_w_s, sem_w_r, sem_c_s, sem_c_r, sem_p_s, sem_p_r,
    sem_z_s, sem_z_r, sem_t_s, sem_t_r, sem_a_s, sem_a_r, sem_in, sem_out,
):
    b = lax.axis_index("batch")
    t = lax.axis_index("tm")
    y, xl = b // 2, b % 2
    xh, z, c = t // 16, (t // 2) % 8, t % 2
    x = xh * 2 + xl
    oc = 1 - c

    def dev(y_, x_, z_, c_):
        return (y_ * 2 + x_ % 2, (x_ // 2) * 16 + z_ * 2 + c_)

    def along_y(i):
        return dev((y + i) % 4, x, z, c)

    def along_x(i):
        return dev(y, (x + i) % 4, z, c)

    def along_z(i):
        return dev(y, x, (z + i) % 8, c)

    mate = dev(y, x, z, oc)
    zp = z % 2
    z_mate = z + 1 - 2 * zp
    across, diagonal = dev(y, x, z_mate, c), dev(y, x, z_mate, oc)
    before, after = (b, t - 1), (b, t + 1)

    def block_of(x_):
        return (x_ % 2) * 2 + x_ // 2

    q = block_of(x)

    def half(c_):
        return pl.ds(pl.multiple_of(c_ * H, H), H)

    def frames_of(c_):
        return pl.ds(pl.multiple_of(c_ * T, T), T)

    started = []

    def copy(src, dst, ss, rs, to):
        return pltpu.make_async_remote_copy(
            src_ref=src, dst_ref=dst, send_sem=ss, recv_sem=rs, device_id=to, device_id_type=MESH
        )

    def send(*args):
        item = copy(*args)
        item.start()
        started.append(item)
        return item

    barrier = pltpu.get_barrier_semaphore()

    def greet(to):
        pl.semaphore_signal(barrier, inc=1, device_id=to, device_id_type=MESH)

    greet(mate)
    greet(diagonal)
    for i in range(1, 16):
        greet(dev((y + i // 4) % 4, (x + i % 4) % 4, z, c))
    for i in range(1, 8):
        greet(along_z(i))

    @pl.when(t > 0)
    def _():
        greet(before)

    @pl.when(t < 31)
    def _():
        greet(after)

    w_own = pl.ds(pl.multiple_of((y * 2 + xl) * 192, 192), 192)
    loads = [
        pltpu.make_async_copy(src, dst, sem_in.at[n])
        for n, (src, dst) in enumerate((
            (x_hbm, x_ref), (cot_hbm, cot_ref), (w_hbm.at[:, half(c)], wb.at[w_own]),
            (kern_hbm, kern_ref), (gain_hbm, gain_ref), (len_hbm, len_ref),
        ))
    ]
    for item in loads:
        item.start()
    others = 24 + jnp.where(t > 0, 1, 0) + jnp.where(t < 31, 1, 0)
    pl.semaphore_wait(barrier, others)

    def rows_of(y_, xl_, side):
        return wb.at[pl.ds(pl.multiple_of((y_ * 2 + xl_) * 192 + side * 96, 96), 96)]

    y_up, y_down, y_far = (y + 1) % 4, (y + 3) % 4, (y + 2) % 4
    x_step = (1, 3)

    def push(here, n, to):
        send(here, here, sem_w_s.at[n], sem_w_r.at[n], to)

    def landed(here, n):
        copy(here, here, sem_w_s.at[n], sem_w_r.at[n], mate).wait_recv()

    def push_own(side, n, to):
        send(w_hbm.at[pl.ds(side * 96, 96), half(c)], rows_of(y, xl, side), sem_w_s.at[n], sem_w_r.at[n], to)

    push_own(0, 0, along_y(1))
    push_own(1, 3, along_y(3))
    for side in range(2):
        push_own(side, 6 + side, along_x(x_step[side]))
    push_own(1, 1, along_y(1))
    push_own(0, 2, along_y(3))

    loads[5].wait()
    position = t * T + lax.broadcasted_iota(jnp.int32, (T, LANES), 0)
    live = jnp.where(position < len_ref[0], 1.0, 0.0).astype(F32)
    for item in loads[:2]:
        item.wait()

    def mask_chunk(k, _):
        at_lanes = lanes_of(k)
        masked = x_ref[:, at_lanes].astype(F32) * live
        xm[:, at_lanes] = masked.astype(BF16)
        xf[PAD:PAD + T, at_lanes] = masked
        us[:, at_lanes] = (cot_ref[:, at_lanes].astype(F32) * live).astype(BF16)
        return 0

    lax.fori_loop(0, CHUNKS, mask_chunk, 0)

    to_before = copy(xm.at[pl.ds(0, PAD)], hx.at[1], sem_halo_s.at[0], sem_halo_r.at[1], before)
    to_after = copy(xm.at[pl.ds(T - PAD, PAD)], hx.at[0], sem_halo_s.at[1], sem_halo_r.at[0], after)

    @pl.when(t > 0)
    def _():
        to_before.start()

    @pl.when(t < 31)
    def _():
        to_after.start()

    mine = zp * 2 + c
    u_swaps = [send(us.at[:, half(oc)], ub.at[frames_of(mine)], sem_c_s.at[0], sem_c_r.at[0], mate)]

    u_swaps += [
        send(us.at[:, half(c_)], ub.at[frames_of(mine)], sem_a_s.at[n], sem_a_r.at[n], to)
        for n, c_, to in ((0, c, across), (1, oc, diagonal))
    ]
    ub[frames_of(mine), :] = us[:, half(c)]

    for item in loads[3:5]:
        item.wait()

    def conv(source, taps, forward):
        count = source.shape[0] - 32
        total = None
        for r in range(8):
            part = None
            for k in range(4):
                offset = 8 * k + r
                tap = offset - 1 if forward else TAPS - offset
                if 0 <= tap < TAPS:
                    value = taps[tap:tap + 1] * source[8 * k:8 * k + count + 8]
                    part = value if part is None else part + value
            part = part[r:r + count]
            total = part if total is None else total + part
        return total

    def conv_chunk(start, count):
        def body(k, total):
            at_lanes = lanes_of(k)
            value = conv(xf[start:start + count + 32, at_lanes], kern_ref[:, at_lanes], True)
            value = value * live[start:start + count]
            cv[start:start + count, at_lanes] = value
            return total + value
        rs_sum[start:start + count, :] = lax.fori_loop(0, CHUNKS, body, jnp.zeros((count, LANES), F32))

    conv_chunk(PAD, T - 2 * PAD)

    @pl.when(t > 0)
    def _():
        to_after.wait_recv()
        xf[0:PAD, :] = hx[0].astype(F32)

    @pl.when(t == 0)
    def _():
        xf[0:PAD, :] = jnp.zeros((PAD, D), F32)

    @pl.when(t < 31)
    def _():
        to_before.wait_recv()
        xf[PAD + T:, :] = hx[1].astype(F32)

    @pl.when(t == 31)
    def _():
        xf[PAD + T:, :] = jnp.zeros((PAD, D), F32)

    conv_chunk(0, PAD)
    conv_chunk(T - PAD, PAD)

    zero = jnp.zeros((T, LANES), F32)
    total = rs_sum[...]
    average = jnp.broadcast_to(jnp.sum(total, axis=1, keepdims=True) * (1.0 / D), (T, LANES))

    def variance_chunk(k, total):
        centred = cv[:, lanes_of(k)] - average
        return total + centred * centred

    total = lax.fori_loop(0, CHUNKS, variance_chunk, zero)
    variance = jnp.sum(total, axis=1, keepdims=True) * (1.0 / D)
    inv = jnp.broadcast_to(lax.rsqrt(variance + 1e-05), (T, LANES))

    def act_chunk(k, _):
        at_lanes = lanes_of(k)
        normed = (cv[:, at_lanes] - average) * inv
        scaled = normed * gain_ref[at_lanes][None]
        gate = 1.0 / (1.0 + jnp.exp(-scaled))
        act = scaled * gate
        cv[:, at_lanes] = normed
        ds[:, at_lanes] = gate * (1.0 + scaled * (1.0 - gate))
        ab[frames_of(c), at_lanes] = act.astype(BF16)
        tf[pl.ds(pl.multiple_of((k % 3) * LANES, LANES), LANES), :] = act.T
        return 0

    def pass_on(*pieces):
        for n, from_y, side in pieces:
            here = rows_of(from_y, xl, side)
            landed(here, n + side)
            push(here, 8 + n + side, along_x(x_step[side]))

    pass_on((0, y_down, 0), (2, y_up, 1))
    push(rows_of(y_down, xl, 0), 4, along_y(1))
    push(rows_of(y_up, xl, 1), 5, along_y(3))

    swaps, z_swaps, a_swaps = [], [], []
    for part in range(4):
        lax.fori_loop(part * 3, part * 3 + 3, act_chunk, 0)
        for parity in range(2):
            for g in range(16):
                tp[12 * g:12 * g + 12, :] = tf[24 * g + 12 * parity:24 * g + 12 * parity + 12, :]
            at2[parity, part * 192:part * 192 + 192, :] = tp[...].astype(BF16)
        rows = pl.ds(part * 192, 192)
        there = atm.at[rows, frames_of(mine)]
        z_swaps.append(send(at2.at[1 - zp, rows], there, sem_a_s.at[2 + part], sem_a_r.at[2 + part], across))
        swaps.append(send(at2.at[zp, rows], there, sem_c_s.at[1 + part], sem_c_r.at[1 + part], mate))
        atm[rows, frames_of(mine)] = at2[zp, part * 192:part * 192 + 192, :]
    here = ab.at[frames_of(c)]
    a_swaps.append(send(here, here, sem_c_s.at[5], sem_c_r.at[5], mate))

    pass_on((2, y_up, 0), (0, y_down, 1))
    for side in range(2):
        here = rows_of(y_far, xl, side)
        landed(here, 4 + side)
        push(here, 12 + side, along_x(x_step[side]))

    theirs = (1 - zp) * 2 + c
    for part in range(4):
        z_swaps[part].wait_recv()
        here = atm.at[pl.ds(part * 192, 192), frames_of(theirs)]
        swaps.append(send(here, here, sem_a_s.at[6 + part], sem_a_r.at[6 + part], mate))

    for item in u_swaps + swaps:
        item.wait_recv()

    def partial(n, start, width):
        rows = pl.ds(pl.multiple_of(n * 192, 192), 192)
        value = jnp.dot(atm[rows, :], ub[:, start:start + width], preferred_element_type=F32)
        return value.reshape(4, 48, width).astype(BF16)

    loads[2].wait()
    y_first = []
    for i in (1, 3, 2, 0):
        to_y = (y + i) % 4
        py[to_y] = partial(to_y, CX, CY)
        if i:
            y_first.append(send(py.at[to_y], ry.at[i - 1], sem_p_s.at[2 + i], sem_p_r.at[2 + i], along_y(i)))

    def partial_x(n, _):
        px[n] = partial(n, 0, CX)
        return 0

    lax.fori_loop(0, 4, partial_x, 0)
    x_first = [
        send(px.at[:, block_of((x + i) % 4)], rx.at[i - 1], sem_p_s.at[i - 1], sem_p_r.at[i - 1], along_x(i))
        for i in (1, 3, 2)
    ]

    ag_swaps = []
    chip_rows = pl.ds(pl.multiple_of(zp * 2 * T, 2 * T), 2 * T)
    for n, from_y in ((6, y), (8, y_down), (10, y_up), (12, y_far)):
        for side in range(2):
            landed(rows_of(from_y, 1 - xl, side), n + side)
        cols = pl.ds(pl.multiple_of(from_y * 384, 384), 384)
        value = lax.dot_general(
            ub[chip_rows, :], wb[cols, :], (((1,), (1,)), ((), ())), preferred_element_type=F32
        )
        agp[0, :, cols] = value[:T]
        agp[1, :, cols] = value[T:]
        k = len(ag_swaps)
        ag_swaps.append(
            send(agp.at[oc, :, cols], agr.at[:, cols], sem_c_s.at[6 + k], sem_c_r.at[6 + k], mate)
        )

    for item in ag_swaps:
        item.wait_recv()

    def back_chunk(k, sums):
        at_lanes = lanes_of(k)
        normed = cv[:, at_lanes]
        scaled_grad = (agp[c, :, at_lanes] + agr[:, at_lanes]) * ds[:, at_lanes]
        gkb[TAPS:TAPS + 1, at_lanes] = jnp.sum(scaled_grad * normed, axis=0, keepdims=True)
        normed_grad = scaled_grad * gain_ref[at_lanes][None]
        ds[:, at_lanes] = normed_grad
        return (sums[0] + normed_grad, sums[1] + normed_grad * normed)

    sums = lax.fori_loop(0, CHUNKS, back_chunk, (zero, zero))
    first, second = [
        jnp.broadcast_to(jnp.sum(s, axis=1, keepdims=True) * (1.0 / D), (T, LANES)) for s in sums
    ]
    inv_live = inv * live

    def taps_chunk(k, _):
        at_lanes = lanes_of(k)
        source = xf[:, at_lanes]
        grad = inv_live * (ds[:, at_lanes] - first - cv[:, at_lanes] * second)
        cg[PAD:PAD + T, at_lanes] = grad
        for r in range(8):
            shifted = source[r:r + T + 24]
            for j in range(4):
                tap = 8 * j + r - 1
                if 0 <= tap < TAPS:
                    gkb[tap:tap + 1, at_lanes] = jnp.sum(grad * shifted[8 * j:8 * j + T], axis=0, keepdims=True)
        return 0

    lax.fori_loop(oc * 6, oc * 6 + 6, taps_chunk, 0)
    gk_swap = send(gkb.at[:, half(oc)], gcr, sem_t_s.at[0], sem_t_r.at[0], mate)
    lax.fori_loop(c * 6, c * 6 + 6, taps_chunk, 0)
    g_before = copy(cg.at[pl.ds(PAD, PAD)], cg.at[pl.ds(PAD + T, PAD)], sem_halo_s.at[2], sem_halo_r.at[3], before)
    g_after = copy(cg.at[pl.ds(T, PAD)], cg.at[pl.ds(0, PAD)], sem_halo_s.at[3], sem_halo_r.at[2], after)

    @pl.when(t > 0)
    def _():
        g_before.start()

    @pl.when(t < 31)
    def _():
        g_after.start()

    def piece(z_):
        return (
            pl.ds(pl.multiple_of((z_ // 2) * 8, 8), 8),
            pl.ds(pl.multiple_of((z_ % 2) * 384, 384), 384),
        )

    gk_swap.wait_recv()
    gh[...] = gkb[:, half(c)] + gcr[...]
    t_z = [
        send(gh.at[piece((z + i) % 8)], zr.at[i - 1], sem_t_s.at[i], sem_t_r.at[i], along_z(i))
        for i in (4, 3, 5, 2, 6, 1, 7)
    ]

    def add(first, own, came, out):
        for item in first:
            item.wait_recv()

        def body(n, _):
            value = own(n).astype(F32)
            for i in range(3):
                value = value + came[i, n].astype(F32)
            out[n] = value.astype(BF16)
            return 0

        lax.fori_loop(0, 4, body, 0)

    add(x_first, lambda n: px[n, q], rx, s2x)
    x_second = [
        send(s2x.at[(y + i) % 4], r2x.at[i - 1], sem_p_s.at[5 + i], sem_p_r.at[5 + i], along_y(i))
        for i in (2, 1, 3)
    ]
    add(y_first, lambda n: py[y, n], ry, s2y)
    y_second = [
        send(s2y.at[block_of((x + i) % 4)], r2y.at[i - 1], sem_p_s.at[8 + i], sem_p_r.at[8 + i], along_x(i))
        for i in (2, 1, 3)
    ]

    for item in a_swaps:
        item.wait_recv()

    def project_chunk(n, _):
        cols = pl.ds(pl.multiple_of(n * 256, 256), 256)
        value = jnp.dot(ab[...], wb[:, cols], preferred_element_type=F32).astype(BF16)
        pj[0, :, cols] = value[:T]
        pj[1, :, cols] = value[T:]
        return 0

    lax.fori_loop(0, 3, project_chunk, 0)
    pj_swap = send(pj.at[oc], pjr, sem_c_s.at[10], sem_c_r.at[10], mate)
    proj_ref[:, half(c)] = pj[c]

    @pl.when(t > 0)
    def _():
        g_after.wait_recv()

    @pl.when(t == 0)
    def _():
        cg[0:PAD, :] = jnp.zeros((PAD, D), F32)

    @pl.when(t < 31)
    def _():
        g_before.wait_recv()

    @pl.when(t == 31)
    def _():
        cg[PAD + T:, :] = jnp.zeros((PAD, D), F32)

    def input_chunk(k, _):
        at_lanes = lanes_of(k)
        value = conv(cg[:, at_lanes], kern_ref[:, at_lanes], False) * live
        gin_ref[:, at_lanes] = value.astype(BF16)
        return 0

    lax.fori_loop(0, 6, input_chunk, 0)

    for item in t_z:
        item.wait_recv()
    mine_t = gh[piece(z)]
    for i in range(7):
        mine_t = mine_t + zr[i]
    xs[y * 4 + x] = mine_t
    for i in (10, 9, 11, 6, 14, 2, 8, 5, 7, 13, 15, 1, 3, 4, 12):
        here = xs.at[y * 4 + x]
        to = dev((y + i // 4) % 4, (x + i % 4) % 4, z, c)
        send(here, here, sem_t_s.at[7 + i], sem_t_r.at[7 + i], to)

    for item in x_second + y_second:
        item.wait_recv()
    left, right = s2x[y].astype(F32), s2y[q].astype(F32)
    for i in range(3):
        left = left + r2x[i].astype(F32)
        right = right + r2y[i].astype(F32)
    facc[0:48, 0:CX] = left
    facc[0:48, CX:H] = right
    facc[48:56, :] = jnp.zeros((8, H), F32)
    for n in range(4):
        zs[n] = facc[12 * n:12 * n + 16, :].astype(BF16)
    w_z = [
        send(zs.at[(z // 2 + i) % 4], rz.at[i - 1], sem_z_s.at[i - 1], sem_z_r.at[i - 1], along_z(2 * i))
        for i in (2, 1, 3)
    ]

    lax.fori_loop(6, CHUNKS, input_chunk, 0)
    for i in range(1, 16):
        slot = xs.at[(y + 4 - i // 4) % 4 * 4 + (x + 4 - i % 4) % 4]
        copy(slot, slot, sem_t_s.at[7 + i], sem_t_r.at[7 + i], mate).wait_recv()
    total = xs[0]
    for i in range(1, 16):
        total = total + xs[i]
    fg[piece(z)] = total
    for i in (4, 3, 5, 2, 6, 1, 7):
        here = fg.at[piece(z)]
        send(here, here, sem_t_s.at[22 + i], sem_t_r.at[22 + i], along_z(i))

    stores = [pltpu.make_async_copy(gin_ref, gin_hbm, sem_out.at[0])]
    stores[0].start()
    pj_swap.wait_recv()
    proj_ref[:, half(oc)] = pjr[...]
    stores.append(pltpu.make_async_copy(proj_ref, proj_hbm, sem_out.at[1]))
    stores[1].start()

    for item in w_z:
        item.wait_recv()
    rows = zs[z // 2].astype(F32)
    for i in range(3):
        rows = rows + rz[i].astype(F32)
    fin[...] = jnp.zeros((2, 8, H), F32)
    fin[0, 0:6, :] = rows[0:6]
    fin[1, 0:6, :] = rows[6:12]
    w_swap = send(fin.at[oc], cr, sem_z_s.at[3], sem_z_r.at[3], mate)

    for i in range(1, 8):
        slot = fg.at[piece((z + 8 - i) % 8)]
        copy(slot, slot, sem_t_s.at[22 + i], sem_t_r.at[22 + i], mate).wait_recv()
    t_swap = send(fg, fgr, sem_t_s.at[30], sem_t_r.at[30], mate)

    def put_taps(cols, value):
        gk_ref[:, cols] = value[0:TAPS]
        gg_ref[:, cols] = value[TAPS:TAPS + 1]

    put_taps(half(c), fg[...])
    gw_ref[:, half(c)] = fin[c][0:6]
    t_swap.wait_recv()
    put_taps(half(oc), fgr[...])
    w_swap.wait_recv()
    gw_ref[:, half(oc)] = cr[0:6, :]
    for n, (src, dst) in enumerate(((gw_ref, gw_hbm), (gk_ref, gk_hbm), (gg_ref, gg_hbm))):
        stores.append(pltpu.make_async_copy(src, dst, sem_out.at[2 + n]))
        stores[-1].start()

    @pl.when(t > 0)
    def _():
        to_before.wait_send()
        g_before.wait_send()

    @pl.when(t < 31)
    def _():
        to_after.wait_send()
        g_after.wait_send()

    for item in started:
        item.wait_send()
    for item in stores:
        item.wait()


def deliver(*refs):
    sources, results, kept, flat, sems = refs[:5], refs[5:10], refs[10:15], refs[15], refs[16]
    loads = [pltpu.make_async_copy(a, b, sems.at[n]) for n, (a, b) in enumerate(zip(sources, kept))]
    stores = [pltpu.make_async_copy(a, b, sems.at[5 + n]) for n, (a, b) in enumerate(zip(kept[:4] + (flat,), results))]
    for item in loads:
        item.start()
    for first, then in zip(loads[:4], stores):
        first.wait()
        then.start()
    loads[4].wait()
    flat[...] = kept[4][0]
    stores[4].start()
    for item in stores:
        item.wait()


def on_device(inputs, lengths, kernel, norm_gain, weight, cotangent):
    vmem = pl.BlockSpec(memory_space=pltpu.VMEM)
    dma = pltpu.SemaphoreType.DMA
    scratch = [
        pltpu.SMEM((1,), jnp.int32),
        pltpu.VMEM((T, D), BF16),
        pltpu.VMEM((TAPS, D), F32),
        pltpu.VMEM((D,), F32),
        pltpu.VMEM((T, D), BF16),
        pltpu.VMEM((T, D), BF16),
        pltpu.VMEM((T, D), BF16),
        pltpu.VMEM((6, D), F32),
        pltpu.VMEM((TAPS, D), F32),
        pltpu.VMEM((1, D), F32),
        pltpu.VMEM((T, D), BF16),
        pltpu.VMEM((2, PAD, D), BF16),
        pltpu.VMEM((T + 2 * PAD, D), F32),
        pltpu.VMEM((T, D), F32),
        pltpu.VMEM((T, D), F32),
        pltpu.VMEM((T, LANES), F32),
        pltpu.VMEM((2 * T, D), BF16),
        pltpu.VMEM((3 * LANES, T), F32),
        pltpu.VMEM((192, T), F32),
        pltpu.VMEM((2, H, T), BF16),
        pltpu.VMEM((H, 4 * T), BF16),
        pltpu.VMEM((T, D), BF16),
        pltpu.VMEM((4 * T, H), BF16),
        pltpu.VMEM((D, H), BF16),
        pltpu.VMEM((4, 4, 48, CX), BF16),
        pltpu.VMEM((4, 4, 48, CY), BF16),
        pltpu.VMEM((3, 4, 48, CX), BF16),
        pltpu.VMEM((3, 4, 48, CY), BF16),
        pltpu.VMEM((4, 48, CX), BF16),
        pltpu.VMEM((4, 48, CY), BF16),
        pltpu.VMEM((3, 48, CX), BF16),
        pltpu.VMEM((3, 48, CY), BF16),
        pltpu.VMEM((56, H), F32),
        pltpu.VMEM((4, 16, H), BF16),
        pltpu.VMEM((3, 16, H), BF16),
        pltpu.VMEM((2, 8, H), F32),
        pltpu.VMEM((8, H), F32),
        pltpu.VMEM((2, T, D), F32),
        pltpu.VMEM((T, D), F32),
        pltpu.VMEM((2, T, H), BF16),
        pltpu.VMEM((T, H), BF16),
        pltpu.VMEM((T + 2 * PAD, D), F32),
        pltpu.VMEM((32, D), F32),
        pltpu.VMEM((32, H), F32),
        pltpu.VMEM((32, H), F32),
        pltpu.VMEM((7, 8, 384), F32),
        pltpu.VMEM((16, 8, 384), F32),
        pltpu.VMEM((32, H), F32),
        pltpu.VMEM((32, H), F32),
        dma((4,)), dma((4,)),
        dma((14,)), dma((14,)),
        dma((12,)), dma((12,)),
        dma((12,)), dma((12,)),
        dma((8,)), dma((8,)),
        dma((31,)), dma((31,)),
        dma((10,)), dma((10,)),
        dma((6,)), dma((5,)),
    ]
    hbm = pl.BlockSpec(memory_space=pl.ANY)
    shapes = (
        jax.ShapeDtypeStruct((T, D), BF16),
        jax.ShapeDtypeStruct((T, D), BF16),
        jax.ShapeDtypeStruct((6, D), F32),
        jax.ShapeDtypeStruct((TAPS, D), F32),
        jax.ShapeDtypeStruct((1, D), F32),
    )
    results = pl.pallas_call(
        fused,
        out_shape=shapes,
        in_specs=[hbm] * 6,
        out_specs=[hbm] * 5,
        scratch_shapes=scratch,
        compiler_params=pltpu.CompilerParams(
            collective_id=0, has_side_effects=True, vmem_limit_bytes=60 << 20
        ),
        name="conv_module",
    )(inputs[0], lengths, kernel, norm_gain, weight, cotangent[0])
    projected, grad_input, grad_weight, grad_kernel, grad_gain = pl.pallas_call(
        deliver,
        out_shape=shapes[:4] + (jax.ShapeDtypeStruct((D,), F32),),
        in_specs=[hbm] * 5,
        out_specs=[hbm] * 5,
        scratch_shapes=[pltpu.VMEM(r.shape, r.dtype) for r in shapes] + [pltpu.VMEM((D,), F32), dma((10,))],
        compiler_params=pltpu.CompilerParams(vmem_limit_bytes=60 << 20),
        name="deliver",
    )(*results)
    return (projected[None], grad_input[None], grad_weight, grad_kernel, grad_gain)


def solution(mesh):
    in_specs = (
        P("batch", "tm", None),
        P("batch"),
        P(),
        P(),
        P("batch", None),
        P("batch", "tm", None),
    )
    out_specs = (P("batch", "tm", None), P("batch", "tm", None), P(("batch", "tm"), None), P(), P())
    return jax.shard_map(
        on_device, mesh=mesh, in_specs=in_specs, out_specs=out_specs, check_vma=False
    )
```

```python
import jax
import jax.numpy as jnp
from jax import lax
from jax.experimental import pallas as pl
from jax.experimental.pallas import tpu as pltpu
from jax.sharding import PartitionSpec as P

F32, BF16 = jnp.float32, jnp.bfloat16
MESH = pl.DeviceIdType.MESH
D, T, H, TAPS = 1536, 128, 768, 31
PAD = 16
CX, CY = 256, 512
LANES = 128
CHUNKS = D // LANES


def lanes_of(k):
    return pl.ds(pl.multiple_of(k * LANES, LANES), LANES)


def fused(
    x_hbm, len_hbm, kern_hbm, gain_hbm, w_hbm, cot_hbm,
    proj_hbm, gin_hbm, gw_hbm, gk_hbm, gg_hbm,
    len_ref, x_ref, kern_ref, gain_ref, proj_ref, gin_ref, gw_ref, gk_ref, gg_ref,
    hx, xf, cv, ds, rs_sum, ab, tf, tp, at2, atm, ub, wb, px, py, rx, ry, s2x, s2y, r2x, r2y,
    facc, zs, rz, fin, cr, agp, agr, pj, pjr, cg, gkb, gcr, gh, gp, zr, xs, fg, fgr,
    sem_halo_s, sem_halo_r, sem_w_s, sem_w_r, sem_c_s, sem_c_r, sem_p_s, sem_p_r,
    sem_z_s, sem_z_r, sem_t_s, sem_t_r, sem_a_s, sem_a_r, sem_in, sem_out,
):
    b = lax.axis_index("batch")
    t = lax.axis_index("tm")
    y, xl = lax.div(b, 2), lax.rem(b, 2)
    xh, z, c = lax.div(t, 16), lax.rem(lax.div(t, 2), 8), lax.rem(t, 2)
    x = xh * 2 + xl
    oc = 1 - c

    ys = [y] + [lax.rem(y + i, 4) for i in range(1, 4)]
    xr = [x] + [lax.rem(x + i, 4) for i in range(1, 4)]
    zr_ = [z] + [lax.rem(z + i, 8) for i in range(1, 8)]
    low, high = [lax.rem(v, 2) for v in xr], [lax.div(v, 2) for v in xr]
    blocks = [l * 2 + h for l, h in zip(low, high)]

    def dev(dy, dx, z_, c_):
        return (ys[dy] * 2 + low[dx], high[dx] * 16 + z_ * 2 + c_)

    def along_y(i):
        return dev(i, 0, z, c)

    def along_x(i):
        return dev(0, i, z, c)

    def along_z(i):
        return dev(0, 0, zr_[i], c)

    mate = dev(0, 0, z, oc)
    zp = lax.rem(z, 2)
    zh = lax.div(z, 2)
    zhs = [zh] + [lax.rem(zh + i, 4) for i in range(1, 4)]
    z_mate = z + 1 - 2 * zp
    across, diagonal = dev(0, 0, z_mate, c), dev(0, 0, z_mate, oc)
    before, after = (b, t - 1), (b, t + 1)

    q = blocks[0]

    def half(c_):
        return pl.ds(pl.multiple_of(c_ * H, H), H)

    def frames_of(c_):
        return pl.ds(pl.multiple_of(c_ * T, T), T)

    started = []

    def copy(src, dst, ss, rs, to):
        return pltpu.make_async_remote_copy(
            src_ref=src, dst_ref=dst, send_sem=ss, recv_sem=rs, device_id=to, device_id_type=MESH
        )

    def send(*args):
        item = copy(*args)
        item.start()
        started.append(item)
        return item

    barrier = pltpu.get_barrier_semaphore()

    def greet(to):
        pl.semaphore_signal(barrier, inc=1, device_id=to, device_id_type=MESH)

    greet(mate)
    greet(diagonal)
    for i in range(1, 16):
        greet(dev(i // 4, i % 4, z, c))
    for i in range(1, 8):
        greet(along_z(i))

    @pl.when(t > 0)
    def _():
        greet(before)

    @pl.when(t < 31)
    def _():
        greet(after)

    mine = zp * 2 + c
    w_own = pl.ds(pl.multiple_of((y * 2 + xl) * 192, 192), 192)
    loads = [
        pltpu.make_async_copy(src, dst, sem_in.at[n])
        for n, (src, dst) in enumerate((
            (x_hbm, x_ref), (cot_hbm.at[:, half(c)], ub.at[frames_of(mine)]), (w_hbm.at[:, half(c)], wb.at[w_own]),
            (kern_hbm, kern_ref), (gain_hbm, gain_ref), (len_hbm, len_ref),
        ))
    ]
    for item in loads:
        item.start()
    others = 24 + jnp.where(t > 0, 1, 0) + jnp.where(t < 31, 1, 0)
    pl.semaphore_wait(barrier, others)

    to_before = copy(x_hbm.at[pl.ds(0, PAD)], hx.at[1], sem_halo_s.at[0], sem_halo_r.at[1], before)
    to_after = copy(x_hbm.at[pl.ds(T - PAD, PAD)], hx.at[0], sem_halo_s.at[1], sem_halo_r.at[0], after)

    @pl.when(t > 0)
    def _():
        to_before.start()

    @pl.when(t < 31)
    def _():
        to_after.start()

    u_swaps = [
        send(cot_hbm.at[:, half(c_)], ub.at[frames_of(mine)], ss, rs, to)
        for c_, ss, rs, to in (
            (oc, sem_c_s.at[0], sem_c_r.at[0], mate),
            (c, sem_a_s.at[0], sem_a_r.at[0], across),
            (oc, sem_a_s.at[1], sem_a_r.at[1], diagonal),
        )
    ]

    def rows_of(y_, xl_, side):
        return wb.at[pl.ds(pl.multiple_of((y_ * 2 + xl_) * 192 + side * 96, 96), 96)]

    y_up, y_down, y_far = ys[1], ys[3], ys[2]
    x_step = (1, 3)

    def push(here, n, to):
        send(here, here, sem_w_s.at[n], sem_w_r.at[n], to)

    def landed(here, n):
        copy(here, here, sem_w_s.at[n], sem_w_r.at[n], mate).wait_recv()

    def push_own(side, n, to):
        send(w_hbm.at[pl.ds(side * 96, 96), half(c)], rows_of(y, xl, side), sem_w_s.at[n], sem_w_r.at[n], to)

    push_own(0, 0, along_y(1))
    push_own(1, 3, along_y(3))
    for side in range(2):
        push_own(side, 6 + side, along_x(x_step[side]))
    push_own(1, 1, along_y(1))
    push_own(0, 2, along_y(3))

    loads[5].wait()
    position = t * T + lax.broadcasted_iota(jnp.int32, (T, LANES), 0)
    live = jnp.where(position < len_ref[0], 1.0, 0.0).astype(F32)
    loads[0].wait()

    def mask_chunk(k, _):
        at_lanes = lanes_of(k)
        masked = x_ref[:, at_lanes].astype(F32) * live
        xf[PAD:PAD + T, at_lanes] = masked
        return 0

    lax.fori_loop(0, CHUNKS, mask_chunk, 0)

    for item in loads[3:5]:
        item.wait()

    def conv(source, taps, forward):
        count = source.shape[0] - 32
        total = None
        for r in range(8):
            part = None
            for k in range(4):
                offset = 8 * k + r
                tap = offset - 1 if forward else TAPS - offset
                if 0 <= tap < TAPS:
                    value = taps[tap:tap + 1] * source[8 * k:8 * k + count + 8]
                    part = value if part is None else part + value
            part = part[r:r + count]
            total = part if total is None else total + part
        return total

    def conv_chunk(start, count):
        def body(k, total):
            at_lanes = lanes_of(k)
            value = conv(xf[start:start + count + 32, at_lanes], kern_ref[:, at_lanes], True)
            value = value * live[start:start + count]
            cv[start:start + count, at_lanes] = value
            return total + value
        rs_sum[start:start + count, :] = lax.fori_loop(0, CHUNKS, body, jnp.zeros((count, LANES), F32))

    conv_chunk(PAD, T - 2 * PAD)

    def alive_halo(side, row, frame):
        frames = frame + lax.broadcasted_iota(jnp.int32, (PAD, D), 0)
        alive = jnp.where(frames < len_ref[0], 1.0, 0.0).astype(F32)
        xf[row:row + PAD, :] = hx[side].astype(F32) * alive

    @pl.when(t > 0)
    def _():
        to_after.wait_recv()
        alive_halo(0, 0, t * T - PAD)

    @pl.when(t == 0)
    def _():
        xf[0:PAD, :] = jnp.zeros((PAD, D), F32)

    @pl.when(t < 31)
    def _():
        to_before.wait_recv()
        alive_halo(1, PAD + T, t * T + T)

    @pl.when(t == 31)
    def _():
        xf[PAD + T:, :] = jnp.zeros((PAD, D), F32)

    conv_chunk(0, PAD)
    conv_chunk(T - PAD, PAD)

    zero = jnp.zeros((T, LANES), F32)
    total = rs_sum[...]
    average = jnp.broadcast_to(jnp.sum(total, axis=1, keepdims=True) * (1.0 / D), (T, LANES))

    def variance_chunk(k, total):
        centred = cv[:, lanes_of(k)] - average
        return total + centred * centred

    total = lax.fori_loop(0, CHUNKS, variance_chunk, zero)
    variance = jnp.sum(total, axis=1, keepdims=True) * (1.0 / D)
    inv = jnp.broadcast_to(lax.rsqrt(variance + 1e-05), (T, LANES))

    def act_chunk(k, _):
        at_lanes = lanes_of(k)
        normed = (cv[:, at_lanes] - average) * inv
        scaled = normed * gain_ref[at_lanes][None]
        gate = 1.0 / (1.0 + jnp.exp(-scaled))
        act = scaled * gate
        cv[:, at_lanes] = normed
        ds[:, at_lanes] = gate * (1.0 + scaled * (1.0 - gate))
        ab[frames_of(c), at_lanes] = act.astype(BF16)
        tf[pl.ds(pl.multiple_of(lax.rem(k, 3) * LANES, LANES), LANES), :] = act.T
        return 0

    def pass_on(*pieces):
        for n, from_y, side in pieces:
            here = rows_of(from_y, xl, side)
            landed(here, n + side)
            push(here, 8 + n + side, along_x(x_step[side]))

    pass_on((0, y_down, 0), (2, y_up, 1))
    push(rows_of(y_down, xl, 0), 4, along_y(1))
    push(rows_of(y_up, xl, 1), 5, along_y(3))

    swaps, z_swaps, a_swaps = [], [], []
    for part in range(4):
        lax.fori_loop(part * 3, part * 3 + 3, act_chunk, 0)
        for parity in range(2):
            for g in range(16):
                tp[12 * g:12 * g + 12, :] = tf[24 * g + 12 * parity:24 * g + 12 * parity + 12, :]
            at2[parity, part * 192:part * 192 + 192, :] = tp[...].astype(BF16)
        rows = pl.ds(part * 192, 192)
        there = atm.at[rows, frames_of(mine)]
        z_swaps.append(send(at2.at[1 - zp, rows], there, sem_a_s.at[2 + part], sem_a_r.at[2 + part], across))
        swaps.append(send(at2.at[zp, rows], there, sem_c_s.at[1 + part], sem_c_r.at[1 + part], mate))
        atm[rows, frames_of(mine)] = at2[zp, part * 192:part * 192 + 192, :]
    here = ab.at[frames_of(c)]
    a_swaps.append(send(here, here, sem_c_s.at[5], sem_c_r.at[5], mate))

    pass_on((2, y_up, 0), (0, y_down, 1))
    for side in range(2):
        here = rows_of(y_far, xl, side)
        landed(here, 4 + side)
        push(here, 12 + side, along_x(x_step[side]))

    loads[1].wait()
    loads[2].wait()
    for item in u_swaps:
        item.wait_recv()
    for slot in range(4):
        first_frame = (xh * 16 + (z - zp) * 2 + slot) * T
        alive = jnp.where(position - t * T + first_frame < len_ref[0], 1.0, 0.0).astype(F32)

        def mask_upstream(k, _):
            rows, at_lanes = slice(slot * T, slot * T + T), lanes_of(k)
            ub[rows, at_lanes] = (ub[rows, at_lanes].astype(F32) * alive).astype(BF16)
            return 0

        lax.fori_loop(0, H // LANES, mask_upstream, 0)

    theirs = (1 - zp) * 2 + c
    for part in range(4):
        z_swaps[part].wait_recv()
        here = atm.at[pl.ds(part * 192, 192), frames_of(theirs)]
        swaps.append(send(here, here, sem_a_s.at[6 + part], sem_a_r.at[6 + part], mate))

    for item in swaps:
        item.wait_recv()

    def partial(n, start, width):
        rows = pl.ds(pl.multiple_of(n * 192, 192), 192)
        value = jnp.dot(atm[rows, :], ub[:, start:start + width], preferred_element_type=F32)
        return value.reshape(4, 48, width).astype(BF16)

    y_first = []
    for i in (1, 3, 2, 0):
        to_y = ys[i]
        py[to_y] = partial(to_y, CX, CY)
        if i:
            y_first.append(send(py.at[to_y], ry.at[i - 1], sem_p_s.at[2 + i], sem_p_r.at[2 + i], along_y(i)))

    def partial_x(n, _):
        px[n] = partial(n, 0, CX)
        return 0

    lax.fori_loop(0, 4, partial_x, 0)
    x_first = [
        send(px.at[:, blocks[i]], rx.at[i - 1], sem_p_s.at[i - 1], sem_p_r.at[i - 1], along_x(i))
        for i in (1, 3, 2)
    ]

    ag_swaps = []
    chip_rows = pl.ds(pl.multiple_of(zp * 2 * T, 2 * T), 2 * T)
    for n, from_y in ((6, y), (8, y_down), (10, y_up), (12, y_far)):
        for side in range(2):
            landed(rows_of(from_y, 1 - xl, side), n + side)
        cols = pl.ds(pl.multiple_of(from_y * 384, 384), 384)
        value = lax.dot_general(
            ub[chip_rows, :], wb[cols, :], (((1,), (1,)), ((), ())), preferred_element_type=F32
        )
        agp[0, :, cols] = value[:T]
        agp[1, :, cols] = value[T:]
        k = len(ag_swaps)
        ag_swaps.append(
            send(agp.at[oc, :, cols], agr.at[:, cols], sem_c_s.at[6 + k], sem_c_r.at[6 + k], mate)
        )

    for item in ag_swaps:
        item.wait_recv()

    def back_chunk(k, sums):
        at_lanes = lanes_of(k)
        normed = cv[:, at_lanes]
        scaled_grad = (agp[c, :, at_lanes] + agr[:, at_lanes]) * ds[:, at_lanes]
        gkb[TAPS:TAPS + 1, at_lanes] = jnp.sum(scaled_grad * normed, axis=0, keepdims=True)
        normed_grad = scaled_grad * gain_ref[at_lanes][None]
        ds[:, at_lanes] = normed_grad
        return (sums[0] + normed_grad, sums[1] + normed_grad * normed)

    sums = lax.fori_loop(0, CHUNKS, back_chunk, (zero, zero))
    first, second = [
        jnp.broadcast_to(jnp.sum(s, axis=1, keepdims=True) * (1.0 / D), (T, LANES)) for s in sums
    ]
    inv_live = inv * live

    def taps_chunk(k, _):
        at_lanes = lanes_of(k)
        source = xf[:, at_lanes]
        grad = inv_live * (ds[:, at_lanes] - first - cv[:, at_lanes] * second)
        cg[PAD:PAD + T, at_lanes] = grad
        for r in range(8):
            shifted = source[r:r + T + 24]
            for j in range(4):
                tap = 8 * j + r - 1
                if 0 <= tap < TAPS:
                    gkb[tap:tap + 1, at_lanes] = jnp.sum(grad * shifted[8 * j:8 * j + T], axis=0, keepdims=True)
        return 0

    lax.fori_loop(oc * 6, oc * 6 + 6, taps_chunk, 0)
    gk_swap = send(gkb.at[:, half(oc)], gcr, sem_t_s.at[0], sem_t_r.at[0], mate)
    lax.fori_loop(c * 6, c * 6 + 6, taps_chunk, 0)
    g_before = copy(cg.at[pl.ds(PAD, PAD)], cg.at[pl.ds(PAD + T, PAD)], sem_halo_s.at[2], sem_halo_r.at[3], before)
    g_after = copy(cg.at[pl.ds(T, PAD)], cg.at[pl.ds(0, PAD)], sem_halo_s.at[3], sem_halo_r.at[2], after)

    @pl.when(t > 0)
    def _():
        g_before.start()

    @pl.when(t < 31)
    def _():
        g_after.start()

    def pieces():
        for n in range(16):
            yield n, slice(n // 4 * 8, n // 4 * 8 + 8), slice(n % 4 * 192, n % 4 * 192 + 192)

    plane = (10, 9, 11, 6, 14, 2, 8, 5, 7, 13, 15, 1, 3, 4, 12)
    line = (4, 3, 5, 2, 6, 1, 7)
    here = y * 4 + x

    def in_plane(i):
        return ys[i // 4] * 4 + xr[i % 4], dev(i // 4, i % 4, z, c)

    gk_swap.wait_recv()
    gh[...] = gkb[:, half(c)] + gcr[...]
    gp[...] = jnp.zeros((16, 8, 256), F32)
    for n, rows, cols in pieces():
        gp[n, :, 0:192] = gh[rows, cols]
    t_plane = []
    for i in plane:
        n, to = in_plane(i)
        t_plane.append(send(gp.at[n], zr.at[i - 1], sem_t_s.at[i], sem_t_r.at[i], to))

    def add(first, own, came, out):
        for item in first:
            item.wait_recv()

        def body(n, _):
            value = own(n).astype(F32)
            for i in range(3):
                value = value + came[i, n].astype(F32)
            out[n] = value.astype(BF16)
            return 0

        lax.fori_loop(0, 4, body, 0)

    add(x_first, lambda n: px[n, q], rx, s2x)
    x_second = [
        send(s2x.at[ys[i]], r2x.at[i - 1], sem_p_s.at[5 + i], sem_p_r.at[5 + i], along_y(i))
        for i in (2, 1, 3)
    ]
    add(y_first, lambda n: py[y, n], ry, s2y)
    y_second = [
        send(s2y.at[blocks[i]], r2y.at[i - 1], sem_p_s.at[8 + i], sem_p_r.at[8 + i], along_x(i))
        for i in (2, 1, 3)
    ]

    for item in a_swaps:
        item.wait_recv()

    def project_chunk(n, _):
        cols = pl.ds(pl.multiple_of(n * 256, 256), 256)
        value = jnp.dot(ab[...], wb[:, cols], preferred_element_type=F32).astype(BF16)
        pj[0, :, cols] = value[:T]
        pj[1, :, cols] = value[T:]
        return 0

    lax.fori_loop(0, 3, project_chunk, 0)
    pj_swap = send(pj.at[oc], pjr, sem_c_s.at[10], sem_c_r.at[10], mate)
    proj_ref[:, half(c)] = pj[c]

    @pl.when(t > 0)
    def _():
        g_after.wait_recv()

    @pl.when(t == 0)
    def _():
        cg[0:PAD, :] = jnp.zeros((PAD, D), F32)

    @pl.when(t < 31)
    def _():
        g_before.wait_recv()

    @pl.when(t == 31)
    def _():
        cg[PAD + T:, :] = jnp.zeros((PAD, D), F32)

    def input_chunk(k, _):
        at_lanes = lanes_of(k)
        value = conv(cg[:, at_lanes], kern_ref[:, at_lanes], False) * live
        gin_ref[:, at_lanes] = value.astype(BF16)
        return 0

    lax.fori_loop(0, 6, input_chunk, 0)

    for item in t_plane:
        item.wait_recv()
    total = gp[here]
    for i in range(15):
        total = total + zr[i]
    xs[z] = total
    for i in line:
        slot = xs.at[z]
        send(slot, slot, sem_t_s.at[15 + i], sem_t_r.at[15 + i], along_z(i))

    for item in x_second + y_second:
        item.wait_recv()
    left, right = s2x[y].astype(F32), s2y[q].astype(F32)
    for i in range(3):
        left = left + r2x[i].astype(F32)
        right = right + r2y[i].astype(F32)
    facc[0:48, 0:CX] = left
    facc[0:48, CX:H] = right
    facc[48:56, :] = jnp.zeros((8, H), F32)
    for n in range(4):
        zs[n] = facc[12 * n:12 * n + 16, :].astype(BF16)
    w_z = [
        send(zs.at[zhs[i]], rz.at[i - 1], sem_z_s.at[i - 1], sem_z_r.at[i - 1], along_z(2 * i))
        for i in (2, 1, 3)
    ]

    lax.fori_loop(6, CHUNKS, input_chunk, 0)
    for i in range(1, 8):
        slot = xs.at[zr_[8 - i]]
        copy(slot, slot, sem_t_s.at[15 + i], sem_t_r.at[15 + i], mate).wait_recv()
    total = xs[0]
    for i in range(1, 8):
        total = total + xs[i]
    fg[here] = total
    for i in plane:
        send(fg.at[here], fg.at[here], sem_t_s.at[22 + i], sem_t_r.at[22 + i], in_plane(i)[1])

    stores = [pltpu.make_async_copy(gin_ref, gin_hbm, sem_out.at[0])]
    stores[0].start()
    pj_swap.wait_recv()
    proj_ref[:, half(oc)] = pjr[...]
    stores.append(pltpu.make_async_copy(proj_ref, proj_hbm, sem_out.at[1]))
    stores[1].start()

    for item in w_z:
        item.wait_recv()
    rows = zs[zh].astype(F32)
    for i in range(3):
        rows = rows + rz[i].astype(F32)
    fin[...] = jnp.zeros((2, 8, H), F32)
    fin[0, 0:6, :] = rows[0:6]
    fin[1, 0:6, :] = rows[6:12]
    w_swap = send(fin.at[oc], cr, sem_z_s.at[3], sem_z_r.at[3], mate)

    for i in range(1, 16):
        slot = fg.at[ys[-(i // 4) % 4] * 4 + xr[-(i % 4) % 4]]
        copy(slot, slot, sem_t_s.at[22 + i], sem_t_r.at[22 + i], mate).wait_recv()
    t_swap = send(fg, fgr, sem_t_s.at[38], sem_t_r.at[38], mate)

    def put_taps(cols, source):
        for n, rows, part in pieces():
            gh[rows, part] = source[n, :, 0:192]
        gk_ref[:, cols] = gh[0:TAPS, :]
        gg_ref[:, cols] = gh[TAPS:TAPS + 1, :]

    put_taps(half(c), fg)
    gw_ref[:, half(c)] = fin[c][0:6]
    t_swap.wait_recv()
    put_taps(half(oc), fgr)
    w_swap.wait_recv()
    gw_ref[:, half(oc)] = cr[0:6, :]
    for n, (src, dst) in enumerate(((gw_ref, gw_hbm), (gk_ref, gk_hbm), (gg_ref, gg_hbm))):
        stores.append(pltpu.make_async_copy(src, dst, sem_out.at[2 + n]))
        stores[-1].start()

    @pl.when(t > 0)
    def _():
        to_before.wait_send()
        g_before.wait_send()

    @pl.when(t < 31)
    def _():
        to_after.wait_send()
        g_after.wait_send()

    for item in started:
        item.wait_send()
    for item in stores:
        item.wait()


def deliver(*refs):
    sources, results, kept, flat, sems = refs[:5], refs[5:10], refs[10:15], refs[15], refs[16]
    loads = [pltpu.make_async_copy(a, b, sems.at[n]) for n, (a, b) in enumerate(zip(sources, kept))]
    stores = [pltpu.make_async_copy(a, b, sems.at[5 + n]) for n, (a, b) in enumerate(zip(kept[:4] + (flat,), results))]
    for item in loads:
        item.start()
    for first, then in zip(loads[:4], stores):
        first.wait()
        then.start()
    loads[4].wait()
    flat[...] = kept[4][0]
    stores[4].start()
    for item in stores:
        item.wait()


def on_device(inputs, lengths, kernel, norm_gain, weight, cotangent):
    vmem = pl.BlockSpec(memory_space=pltpu.VMEM)
    dma = pltpu.SemaphoreType.DMA
    scratch = [
        pltpu.SMEM((1,), jnp.int32),
        pltpu.VMEM((T, D), BF16),
        pltpu.VMEM((TAPS, D), F32),
        pltpu.VMEM((D,), F32),
        pltpu.VMEM((T, D), BF16),
        pltpu.VMEM((T, D), BF16),
        pltpu.VMEM((6, D), F32),
        pltpu.VMEM((TAPS, D), F32),
        pltpu.VMEM((1, D), F32),
        pltpu.VMEM((2, PAD, D), BF16),
        pltpu.VMEM((T + 2 * PAD, D), F32),
        pltpu.VMEM((T, D), F32),
        pltpu.VMEM((T, D), F32),
        pltpu.VMEM((T, LANES), F32),
        pltpu.VMEM((2 * T, D), BF16),
        pltpu.VMEM((3 * LANES, T), F32),
        pltpu.VMEM((192, T), F32),
        pltpu.VMEM((2, H, T), BF16),
        pltpu.VMEM((H, 4 * T), BF16),
        pltpu.VMEM((4 * T, H), BF16),
        pltpu.VMEM((D, H), BF16),
        pltpu.VMEM((4, 4, 48, CX), BF16),
        pltpu.VMEM((4, 4, 48, CY), BF16),
        pltpu.VMEM((3, 4, 48, CX), BF16),
        pltpu.VMEM((3, 4, 48, CY), BF16),
        pltpu.VMEM((4, 48, CX), BF16),
        pltpu.VMEM((4, 48, CY), BF16),
        pltpu.VMEM((3, 48, CX), BF16),
        pltpu.VMEM((3, 48, CY), BF16),
        pltpu.VMEM((56, H), F32),
        pltpu.VMEM((4, 16, H), BF16),
        pltpu.VMEM((3, 16, H), BF16),
        pltpu.VMEM((2, 8, H), F32),
        pltpu.VMEM((8, H), F32),
        pltpu.VMEM((2, T, D), F32),
        pltpu.VMEM((T, D), F32),
        pltpu.VMEM((2, T, H), BF16),
        pltpu.VMEM((T, H), BF16),
        pltpu.VMEM((T + 2 * PAD, D), F32),
        pltpu.VMEM((32, D), F32),
        pltpu.VMEM((32, H), F32),
        pltpu.VMEM((32, H), F32),
        pltpu.VMEM((16, 8, 256), F32),
        pltpu.VMEM((15, 8, 256), F32),
        pltpu.VMEM((8, 8, 256), F32),
        pltpu.VMEM((16, 8, 256), F32),
        pltpu.VMEM((16, 8, 256), F32),
        dma((4,)), dma((4,)),
        dma((14,)), dma((14,)),
        dma((12,)), dma((12,)),
        dma((12,)), dma((12,)),
        dma((8,)), dma((8,)),
        dma((39,)), dma((39,)),
        dma((10,)), dma((10,)),
        dma((6,)), dma((5,)),
    ]
    hbm = pl.BlockSpec(memory_space=pl.ANY)
    shapes = (
        jax.ShapeDtypeStruct((T, D), BF16),
        jax.ShapeDtypeStruct((T, D), BF16),
        jax.ShapeDtypeStruct((6, D), F32),
        jax.ShapeDtypeStruct((TAPS, D), F32),
        jax.ShapeDtypeStruct((1, D), F32),
    )
    results = pl.pallas_call(
        fused,
        out_shape=shapes,
        in_specs=[hbm] * 6,
        out_specs=[hbm] * 5,
        scratch_shapes=scratch,
        compiler_params=pltpu.CompilerParams(
            collective_id=0, has_side_effects=True, vmem_limit_bytes=60 << 20
        ),
        name="conv_module",
    )(inputs[0], lengths, kernel, norm_gain, weight, cotangent[0])
    projected, grad_input, grad_weight, grad_kernel, grad_gain = pl.pallas_call(
        deliver,
        out_shape=shapes[:4] + (jax.ShapeDtypeStruct((D,), F32),),
        in_specs=[hbm] * 5,
        out_specs=[hbm] * 5,
        scratch_shapes=[pltpu.VMEM(r.shape, r.dtype) for r in shapes] + [pltpu.VMEM((D,), F32), dma((10,))],
        compiler_params=pltpu.CompilerParams(vmem_limit_bytes=60 << 20),
        name="deliver",
    )(*results)
    return (projected[None], grad_input[None], grad_weight, grad_kernel, grad_gain)


def solution(mesh):
    in_specs = (
        P("batch", "tm", None),
        P("batch"),
        P(),
        P(),
        P("batch", None),
        P("batch", "tm", None),
    )
    out_specs = (P("batch", "tm", None), P("batch", "tm", None), P(("batch", "tm"), None), P(), P())
    return jax.shard_map(
        on_device, mesh=mesh, in_specs=in_specs, out_specs=out_specs, check_vma=False
    )
```

```python
import jax
import jax.numpy as jnp
from jax import lax
from jax.experimental import pallas as pl
from jax.experimental.pallas import tpu as pltpu
from jax.sharding import PartitionSpec as P

F32, BF16 = jnp.float32, jnp.bfloat16
MESH = pl.DeviceIdType.MESH
D, T, H, TAPS = 1536, 128, 768, 31
PAD = 16
CX, CY = 256, 512
LANES = 128
CHUNKS = D // LANES


def lanes_of(k):
    return pl.ds(pl.multiple_of(k * LANES, LANES), LANES)


def fused(
    x_hbm, len_hbm, kern_hbm, gain_hbm, w_hbm, cot_hbm,
    proj_hbm, gin_hbm, gw_hbm, gk_hbm, gg_hbm,
    len_ref, x_ref, kern_ref, gain_ref, proj_ref, gin_ref, gw_ref, gk_ref, gg_ref,
    hx, xf, cv, ds, rs_sum, ab, tf, tp, at2, atm, ub, wb, px, py, rx, ry, s2x, s2y, r2x, r2y,
    facc, zs, rz, fin, cr, agp, agr, pj, pjr, cg, gkb, gcr, gh, gp, zr, xs, fg, fgr,
    sem_halo_s, sem_halo_r, sem_w_s, sem_w_r, sem_c_s, sem_c_r, sem_p_s, sem_p_r,
    sem_z_s, sem_z_r, sem_t_s, sem_t_r, sem_a_s, sem_a_r, sem_in, sem_out, sem_far,
):
    b = lax.axis_index("batch")
    t = lax.axis_index("tm")
    y, xl = lax.div(b, 2), lax.rem(b, 2)
    xh, z, c = lax.div(t, 16), lax.rem(lax.div(t, 2), 8), lax.rem(t, 2)
    x = xh * 2 + xl
    oc = 1 - c

    ys = [y] + [lax.rem(y + i, 4) for i in range(1, 4)]
    xr = [x] + [lax.rem(x + i, 4) for i in range(1, 4)]
    zr_ = [z] + [lax.rem(z + i, 8) for i in range(1, 8)]
    low, high = [lax.rem(v, 2) for v in xr], [lax.div(v, 2) for v in xr]
    blocks = [l * 2 + h for l, h in zip(low, high)]

    def dev(dy, dx, z_, c_):
        return (ys[dy] * 2 + low[dx], high[dx] * 16 + z_ * 2 + c_)

    def along_y(i):
        return dev(i, 0, z, c)

    def along_x(i):
        return dev(0, i, z, c)

    def along_z(i):
        return dev(0, 0, zr_[i], c)

    mate = dev(0, 0, z, oc)
    zp = lax.rem(z, 2)
    zh = lax.div(z, 2)
    zhs = [zh] + [lax.rem(zh + i, 4) for i in range(1, 4)]
    z_mate = z + 1 - 2 * zp
    across, diagonal = dev(0, 0, z_mate, c), dev(0, 0, z_mate, oc)
    before, after = (b, t - 1), (b, t + 1)

    q = blocks[0]

    def half(c_):
        return pl.ds(pl.multiple_of(c_ * H, H), H)

    def frames_of(c_):
        return pl.ds(pl.multiple_of(c_ * T, T), T)

    started = []

    def copy(src, dst, ss, rs, to):
        return pltpu.make_async_remote_copy(
            src_ref=src, dst_ref=dst, send_sem=ss, recv_sem=rs, device_id=to, device_id_type=MESH
        )

    def send(*args):
        item = copy(*args)
        item.start()
        started.append(item)
        return item

    def sent_so_far():
        items = list(started)
        started.clear()
        return items

    def all_sent(items):
        for item in items:
            item.wait_send()

    barrier = pltpu.get_barrier_semaphore()

    def greet(to):
        pl.semaphore_signal(barrier, inc=1, device_id=to, device_id_type=MESH)

    greet(mate)
    greet(diagonal)
    beside = [along_x(1), along_x(3), along_y(1), along_y(3), along_z(1), along_z(7)]
    for to in beside:
        greet(to)

    @pl.when(t > 0)
    def _():
        greet(before)

    @pl.when(t < 31)
    def _():
        greet(after)

    mine = zp * 2 + c
    w_own = pl.ds(pl.multiple_of((y * 2 + xl) * 192, 192), 192)
    loads = [
        pltpu.make_async_copy(src, dst, sem_in.at[n])
        for n, (src, dst) in enumerate((
            (x_hbm, x_ref), (cot_hbm.at[:, half(c)], ub.at[frames_of(mine)]), (w_hbm.at[:, half(c)], wb.at[w_own]),
            (kern_hbm, kern_ref), (gain_hbm, gain_ref), (len_hbm, len_ref),
        ))
    ]
    for item in loads:
        item.start()
    others = 8 + jnp.where(t > 0, 1, 0) + jnp.where(t < 31, 1, 0)
    pl.semaphore_wait(barrier, others)

    to_before = copy(x_hbm.at[pl.ds(0, PAD)], hx.at[1], sem_halo_s.at[0], sem_halo_r.at[1], before)
    to_after = copy(x_hbm.at[pl.ds(T - PAD, PAD)], hx.at[0], sem_halo_s.at[1], sem_halo_r.at[0], after)

    @pl.when(t > 0)
    def _():
        to_before.start()

    @pl.when(t < 31)
    def _():
        to_after.start()

    u_swaps = [
        send(cot_hbm.at[:, half(c_)], ub.at[frames_of(mine)], ss, rs, to)
        for c_, ss, rs, to in (
            (oc, sem_c_s.at[0], sem_c_r.at[0], mate),
            (c, sem_a_s.at[0], sem_a_r.at[0], across),
            (oc, sem_a_s.at[1], sem_a_r.at[1], diagonal),
        )
    ]

    def tell(n):
        for to in beside:
            pl.semaphore_signal(sem_far.at[n], inc=1, device_id=to, device_id_type=MESH)

    def told(n):
        pl.semaphore_wait(sem_far.at[n], len(beside))

    def rows_of(y_, xl_, side):
        return wb.at[pl.ds(pl.multiple_of((y_ * 2 + xl_) * 192 + side * 96, 96), 96)]

    y_up, y_down, y_far = ys[1], ys[3], ys[2]
    x_step = (1, 3)

    def push(here, n, to):
        send(here, here, sem_w_s.at[n], sem_w_r.at[n], to)

    def landed(here, n):
        copy(here, here, sem_w_s.at[n], sem_w_r.at[n], mate).wait_recv()

    def push_own(side, n, to):
        send(w_hbm.at[pl.ds(side * 96, 96), half(c)], rows_of(y, xl, side), sem_w_s.at[n], sem_w_r.at[n], to)

    push_own(0, 0, along_y(1))
    push_own(1, 3, along_y(3))
    for side in range(2):
        push_own(side, 6 + side, along_x(x_step[side]))
    push_own(1, 1, along_y(1))
    push_own(0, 2, along_y(3))

    tell(0)

    loads[5].wait()
    position = t * T + lax.broadcasted_iota(jnp.int32, (T, LANES), 0)
    live = jnp.where(position < len_ref[0], 1.0, 0.0).astype(F32)
    loads[0].wait()

    def mask_chunk(k, _):
        at_lanes = lanes_of(k)
        masked = x_ref[:, at_lanes].astype(F32) * live
        xf[PAD:PAD + T, at_lanes] = masked
        return 0

    lax.fori_loop(0, CHUNKS, mask_chunk, 0)

    for item in loads[3:5]:
        item.wait()

    def conv(source, taps, forward):
        count = source.shape[0] - 32
        total = None
        for r in range(8):
            part = None
            for k in range(4):
                offset = 8 * k + r
                tap = offset - 1 if forward else TAPS - offset
                if 0 <= tap < TAPS:
                    value = taps[tap:tap + 1] * source[8 * k:8 * k + count + 8]
                    part = value if part is None else part + value
            part = part[r:r + count]
            total = part if total is None else total + part
        return total

    def conv_chunk(start, count):
        def body(k, total):
            at_lanes = lanes_of(k)
            value = conv(xf[start:start + count + 32, at_lanes], kern_ref[:, at_lanes], True)
            value = value * live[start:start + count]
            cv[start:start + count, at_lanes] = value
            return total + value
        rs_sum[start:start + count, :] = lax.fori_loop(0, CHUNKS, body, jnp.zeros((count, LANES), F32))

    conv_chunk(PAD, T - 2 * PAD)

    def alive_halo(side, row, frame):
        frames = frame + lax.broadcasted_iota(jnp.int32, (PAD, D), 0)
        alive = jnp.where(frames < len_ref[0], 1.0, 0.0).astype(F32)
        xf[row:row + PAD, :] = hx[side].astype(F32) * alive

    @pl.when(t > 0)
    def _():
        to_after.wait_recv()
        alive_halo(0, 0, t * T - PAD)

    @pl.when(t == 0)
    def _():
        xf[0:PAD, :] = jnp.zeros((PAD, D), F32)

    @pl.when(t < 31)
    def _():
        to_before.wait_recv()
        alive_halo(1, PAD + T, t * T + T)

    @pl.when(t == 31)
    def _():
        xf[PAD + T:, :] = jnp.zeros((PAD, D), F32)

    conv_chunk(0, PAD)
    conv_chunk(T - PAD, PAD)

    told(0)
    tell(1)

    zero = jnp.zeros((T, LANES), F32)
    total = rs_sum[...]
    average = jnp.broadcast_to(jnp.sum(total, axis=1, keepdims=True) * (1.0 / D), (T, LANES))

    def variance_chunk(k, total):
        centred = cv[:, lanes_of(k)] - average
        return total + centred * centred

    total = lax.fori_loop(0, CHUNKS, variance_chunk, zero)
    variance = jnp.sum(total, axis=1, keepdims=True) * (1.0 / D)
    inv = jnp.broadcast_to(lax.rsqrt(variance + 1e-05), (T, LANES))

    def act_chunk(k, _):
        at_lanes = lanes_of(k)
        normed = (cv[:, at_lanes] - average) * inv
        scaled = normed * gain_ref[at_lanes][None]
        gate = 1.0 / (1.0 + jnp.exp(-scaled))
        act = scaled * gate
        cv[:, at_lanes] = normed
        ds[:, at_lanes] = gate * (1.0 + scaled * (1.0 - gate))
        ab[frames_of(c), at_lanes] = act.astype(BF16)
        tf[pl.ds(pl.multiple_of(lax.rem(k, 3) * LANES, LANES), LANES), :] = act.T
        return 0

    def pass_on(*pieces):
        for n, from_y, side in pieces:
            here = rows_of(from_y, xl, side)
            landed(here, n + side)
            push(here, 8 + n + side, along_x(x_step[side]))

    pass_on((0, y_down, 0), (2, y_up, 1))
    push(rows_of(y_down, xl, 0), 4, along_y(1))
    push(rows_of(y_up, xl, 1), 5, along_y(3))

    swaps, z_swaps, a_swaps = [], [], []
    for part in range(4):
        lax.fori_loop(part * 3, part * 3 + 3, act_chunk, 0)
        for parity in range(2):
            for g in range(16):
                tp[12 * g:12 * g + 12, :] = tf[24 * g + 12 * parity:24 * g + 12 * parity + 12, :]
            at2[parity, part * 192:part * 192 + 192, :] = tp[...].astype(BF16)
        rows = pl.ds(part * 192, 192)
        there = atm.at[rows, frames_of(mine)]
        z_swaps.append(send(at2.at[1 - zp, rows], there, sem_a_s.at[2 + part], sem_a_r.at[2 + part], across))
        swaps.append(send(at2.at[zp, rows], there, sem_c_s.at[1 + part], sem_c_r.at[1 + part], mate))
        atm[rows, frames_of(mine)] = at2[zp, part * 192:part * 192 + 192, :]
    here = ab.at[frames_of(c)]
    a_swaps.append(send(here, here, sem_c_s.at[5], sem_c_r.at[5], mate))

    told(1)
    tell(2)

    pass_on((2, y_up, 0), (0, y_down, 1))
    for side in range(2):
        here = rows_of(y_far, xl, side)
        landed(here, 4 + side)
        push(here, 12 + side, along_x(x_step[side]))

    loads[1].wait()
    loads[2].wait()
    for item in u_swaps:
        item.wait_recv()
    for slot in range(4):
        first_frame = (xh * 16 + (z - zp) * 2 + slot) * T
        alive = jnp.where(position - t * T + first_frame < len_ref[0], 1.0, 0.0).astype(F32)

        def mask_upstream(k, _):
            rows, at_lanes = slice(slot * T, slot * T + T), lanes_of(k)
            ub[rows, at_lanes] = (ub[rows, at_lanes].astype(F32) * alive).astype(BF16)
            return 0

        lax.fori_loop(0, H // LANES, mask_upstream, 0)

    theirs = (1 - zp) * 2 + c
    for part in range(4):
        z_swaps[part].wait_recv()
        here = atm.at[pl.ds(part * 192, 192), frames_of(theirs)]
        swaps.append(send(here, here, sem_a_s.at[6 + part], sem_a_r.at[6 + part], mate))

    told(2)

    for item in swaps:
        item.wait_recv()

    def partial(n, start, width):
        rows = pl.ds(pl.multiple_of(n * 192, 192), 192)
        value = jnp.dot(atm[rows, :], ub[:, start:start + width], preferred_element_type=F32)
        return value.reshape(4, 48, width).astype(BF16)

    y_first = []
    for i in (2, 1, 3, 0):
        to_y = ys[i]
        py[to_y] = partial(to_y, CX, CY)
        if i:
            y_first.append(send(py.at[to_y], ry.at[i - 1], sem_p_s.at[2 + i], sem_p_r.at[2 + i], along_y(i)))

    def partial_x(n, _):
        px[n] = partial(n, 0, CX)
        return 0

    lax.fori_loop(0, 4, partial_x, 0)
    x_first = [
        send(px.at[:, blocks[i]], rx.at[i - 1], sem_p_s.at[i - 1], sem_p_r.at[i - 1], along_x(i))
        for i in (2, 1, 3)
    ]

    ag_swaps = []
    chip_rows = pl.ds(pl.multiple_of(zp * 2 * T, 2 * T), 2 * T)
    for n, from_y in ((6, y), (8, y_down), (10, y_up), (12, y_far)):
        for side in range(2):
            landed(rows_of(from_y, 1 - xl, side), n + side)
        cols = pl.ds(pl.multiple_of(from_y * 384, 384), 384)
        value = lax.dot_general(
            ub[chip_rows, :], wb[cols, :], (((1,), (1,)), ((), ())), preferred_element_type=F32
        )
        agp[0, :, cols] = value[:T]
        agp[1, :, cols] = value[T:]
        k = len(ag_swaps)
        ag_swaps.append(
            send(agp.at[oc, :, cols], agr.at[:, cols], sem_c_s.at[6 + k], sem_c_r.at[6 + k], mate)
        )

    for item in ag_swaps:
        item.wait_recv()

    def back_chunk(k, sums):
        at_lanes = lanes_of(k)
        normed = cv[:, at_lanes]
        scaled_grad = (agp[c, :, at_lanes] + agr[:, at_lanes]) * ds[:, at_lanes]
        gkb[TAPS:TAPS + 1, at_lanes] = jnp.sum(scaled_grad * normed, axis=0, keepdims=True)
        normed_grad = scaled_grad * gain_ref[at_lanes][None]
        ds[:, at_lanes] = normed_grad
        return (sums[0] + normed_grad, sums[1] + normed_grad * normed)

    sums = lax.fori_loop(0, CHUNKS, back_chunk, (zero, zero))
    first, second = [
        jnp.broadcast_to(jnp.sum(s, axis=1, keepdims=True) * (1.0 / D), (T, LANES)) for s in sums
    ]
    inv_live = inv * live

    def taps_chunk(k, _):
        at_lanes = lanes_of(k)
        source = xf[:, at_lanes]
        grad = inv_live * (ds[:, at_lanes] - first - cv[:, at_lanes] * second)
        cg[PAD:PAD + T, at_lanes] = grad
        for r in range(8):
            shifted = source[r:r + T + 24]
            for j in range(4):
                tap = 8 * j + r - 1
                if 0 <= tap < TAPS:
                    gkb[tap:tap + 1, at_lanes] = jnp.sum(grad * shifted[8 * j:8 * j + T], axis=0, keepdims=True)
        return 0

    lax.fori_loop(oc * 6, oc * 6 + 6, taps_chunk, 0)
    gk_swap = send(gkb.at[:, half(oc)], gcr, sem_t_s.at[0], sem_t_r.at[0], mate)
    lax.fori_loop(c * 6, c * 6 + 6, taps_chunk, 0)
    g_before = copy(cg.at[pl.ds(PAD, PAD)], cg.at[pl.ds(PAD + T, PAD)], sem_halo_s.at[2], sem_halo_r.at[3], before)
    g_after = copy(cg.at[pl.ds(T, PAD)], cg.at[pl.ds(0, PAD)], sem_halo_s.at[3], sem_halo_r.at[2], after)

    @pl.when(t > 0)
    def _():
        g_before.start()

    @pl.when(t < 31)
    def _():
        g_after.start()

    def pieces():
        for n in range(16):
            yield n, slice(n // 4 * 8, n // 4 * 8 + 8), slice(n % 4 * 192, n % 4 * 192 + 192)

    plane = (10, 9, 11, 6, 14, 2, 8, 5, 7, 13, 15, 1, 3, 4, 12)
    line = (4, 3, 5, 2, 6, 1, 7)
    here = y * 4 + x

    def in_plane(i):
        return ys[i // 4] * 4 + xr[i % 4], dev(i // 4, i % 4, z, c)

    early = sent_so_far()
    gk_swap.wait_recv()
    gh[...] = gkb[:, half(c)] + gcr[...]
    gp[...] = jnp.zeros((16, 8, 256), F32)
    for n, rows, cols in pieces():
        gp[n, :, 0:192] = gh[rows, cols]
    t_plane = []
    for i in plane:
        n, to = in_plane(i)
        t_plane.append(send(gp.at[n], zr.at[i - 1], sem_t_s.at[i], sem_t_r.at[i], to))

    def add(first, own, came, out):
        for item in first:
            item.wait_recv()

        def body(n, _):
            value = own(n).astype(F32)
            for i in range(3):
                value = value + came[i, n].astype(F32)
            out[n] = value.astype(BF16)
            return 0

        lax.fori_loop(0, 4, body, 0)

    add(x_first, lambda n: px[n, q], rx, s2x)
    x_second = [
        send(s2x.at[ys[i]], r2x.at[i - 1], sem_p_s.at[5 + i], sem_p_r.at[5 + i], along_y(i))
        for i in (2, 1, 3)
    ]
    add(y_first, lambda n: py[y, n], ry, s2y)
    y_second = [
        send(s2y.at[blocks[i]], r2y.at[i - 1], sem_p_s.at[8 + i], sem_p_r.at[8 + i], along_x(i))
        for i in (2, 1, 3)
    ]

    for item in a_swaps:
        item.wait_recv()

    def project_chunk(n, _):
        cols = pl.ds(pl.multiple_of(n * 256, 256), 256)
        value = jnp.dot(ab[...], wb[:, cols], preferred_element_type=F32).astype(BF16)
        pj[0, :, cols] = value[:T]
        pj[1, :, cols] = value[T:]
        return 0

    lax.fori_loop(0, 3, project_chunk, 0)
    pj_swap = send(pj.at[oc], pjr, sem_c_s.at[10], sem_c_r.at[10], mate)
    proj_ref[:, half(c)] = pj[c]

    @pl.when(t > 0)
    def _():
        g_after.wait_recv()

    @pl.when(t == 0)
    def _():
        cg[0:PAD, :] = jnp.zeros((PAD, D), F32)

    @pl.when(t < 31)
    def _():
        g_before.wait_recv()

    @pl.when(t == 31)
    def _():
        cg[PAD + T:, :] = jnp.zeros((PAD, D), F32)

    def input_chunk(k, _):
        at_lanes = lanes_of(k)
        value = conv(cg[:, at_lanes], kern_ref[:, at_lanes], False) * live
        gin_ref[:, at_lanes] = value.astype(BF16)
        return 0

    lax.fori_loop(0, 6, input_chunk, 0)
    all_sent(early)

    for item in t_plane:
        item.wait_recv()
    total = gp[here]
    for i in range(15):
        total = total + zr[i]
    xs[z] = total
    for i in line:
        slot = xs.at[z]
        send(slot, slot, sem_t_s.at[15 + i], sem_t_r.at[15 + i], along_z(i))

    for item in x_second + y_second:
        item.wait_recv()
    left, right = s2x[y].astype(F32), s2y[q].astype(F32)
    for i in range(3):
        left = left + r2x[i].astype(F32)
        right = right + r2y[i].astype(F32)
    facc[0:48, 0:CX] = left
    facc[0:48, CX:H] = right
    facc[48:56, :] = jnp.zeros((8, H), F32)
    for n in range(4):
        zs[n] = facc[12 * n:12 * n + 16, :].astype(BF16)
    w_z = [
        send(zs.at[zhs[i]], rz.at[i - 1], sem_z_s.at[i - 1], sem_z_r.at[i - 1], along_z(2 * i))
        for i in (2, 1, 3)
    ]

    lax.fori_loop(6, CHUNKS, input_chunk, 0)
    for i in range(1, 8):
        slot = xs.at[zr_[8 - i]]
        copy(slot, slot, sem_t_s.at[15 + i], sem_t_r.at[15 + i], mate).wait_recv()
    total = xs[0]
    for i in range(1, 8):
        total = total + xs[i]
    fg[here] = total
    middle = sent_so_far()
    for i in plane:
        send(fg.at[here], fg.at[here], sem_t_s.at[22 + i], sem_t_r.at[22 + i], in_plane(i)[1])

    stores = [pltpu.make_async_copy(gin_ref, gin_hbm, sem_out.at[0])]
    stores[0].start()
    all_sent(middle)

    @pl.when(t > 0)
    def _():
        to_before.wait_send()
        g_before.wait_send()

    @pl.when(t < 31)
    def _():
        to_after.wait_send()
        g_after.wait_send()

    pj_swap.wait_recv()
    proj_ref[:, half(oc)] = pjr[...]
    stores.append(pltpu.make_async_copy(proj_ref, proj_hbm, sem_out.at[1]))
    stores[1].start()

    for item in w_z:
        item.wait_recv()
    rows = zs[zh].astype(F32)
    for i in range(3):
        rows = rows + rz[i].astype(F32)
    fin[...] = jnp.zeros((2, 8, H), F32)
    fin[0, 0:6, :] = rows[0:6]
    fin[1, 0:6, :] = rows[6:12]
    w_swap = send(fin.at[oc], cr, sem_z_s.at[3], sem_z_r.at[3], mate)

    for i in range(1, 16):
        slot = fg.at[ys[-(i // 4) % 4] * 4 + xr[-(i % 4) % 4]]
        copy(slot, slot, sem_t_s.at[22 + i], sem_t_r.at[22 + i], mate).wait_recv()
    late = sent_so_far()
    t_swap = send(fg, fgr, sem_t_s.at[38], sem_t_r.at[38], mate)

    def put_taps(cols, source):
        for n, rows, part in pieces():
            gh[rows, part] = source[n, :, 0:192]
        gk_ref[:, cols] = gh[0:TAPS, :]
        gg_ref[:, cols] = gh[TAPS:TAPS + 1, :]

    put_taps(half(c), fg)
    all_sent(late)
    gw_ref[:, half(c)] = fin[c][0:6]
    t_swap.wait_recv()
    put_taps(half(oc), fgr)
    w_swap.wait_recv()
    gw_ref[:, half(oc)] = cr[0:6, :]
    for n, (src, dst) in enumerate(((gw_ref, gw_hbm), (gk_ref, gk_hbm), (gg_ref, gg_hbm))):
        stores.append(pltpu.make_async_copy(src, dst, sem_out.at[2 + n]))
        stores[-1].start()

    all_sent(started)
    for item in stores:
        item.wait()


def deliver(*refs):
    sources, results, kept, flat, sems = refs[:5], refs[5:10], refs[10:15], refs[15], refs[16]
    loads = [pltpu.make_async_copy(a, b, sems.at[n]) for n, (a, b) in enumerate(zip(sources, kept))]
    stores = [pltpu.make_async_copy(a, b, sems.at[5 + n]) for n, (a, b) in enumerate(zip(kept[:4] + (flat,), results))]
    for item in loads:
        item.start()
    for first, then in zip(loads[:4], stores):
        first.wait()
        then.start()
    loads[4].wait()
    flat[...] = kept[4][0]
    stores[4].start()
    for item in stores:
        item.wait()


def on_device(inputs, lengths, kernel, norm_gain, weight, cotangent):
    vmem = pl.BlockSpec(memory_space=pltpu.VMEM)
    dma = pltpu.SemaphoreType.DMA
    scratch = [
        pltpu.SMEM((1,), jnp.int32),
        pltpu.VMEM((T, D), BF16),
        pltpu.VMEM((TAPS, D), F32),
        pltpu.VMEM((D,), F32),
        pltpu.VMEM((T, D), BF16),
        pltpu.VMEM((T, D), BF16),
        pltpu.VMEM((6, D), F32),
        pltpu.VMEM((TAPS, D), F32),
        pltpu.VMEM((1, D), F32),
        pltpu.VMEM((2, PAD, D), BF16),
        pltpu.VMEM((T + 2 * PAD, D), F32),
        pltpu.VMEM((T, D), F32),
        pltpu.VMEM((T, D), F32),
        pltpu.VMEM((T, LANES), F32),
        pltpu.VMEM((2 * T, D), BF16),
        pltpu.VMEM((3 * LANES, T), F32),
        pltpu.VMEM((192, T), F32),
        pltpu.VMEM((2, H, T), BF16),
        pltpu.VMEM((H, 4 * T), BF16),
        pltpu.VMEM((4 * T, H), BF16),
        pltpu.VMEM((D, H), BF16),
        pltpu.VMEM((4, 4, 48, CX), BF16),
        pltpu.VMEM((4, 4, 48, CY), BF16),
        pltpu.VMEM((3, 4, 48, CX), BF16),
        pltpu.VMEM((3, 4, 48, CY), BF16),
        pltpu.VMEM((4, 48, CX), BF16),
        pltpu.VMEM((4, 48, CY), BF16),
        pltpu.VMEM((3, 48, CX), BF16),
        pltpu.VMEM((3, 48, CY), BF16),
        pltpu.VMEM((56, H), F32),
        pltpu.VMEM((4, 16, H), BF16),
        pltpu.VMEM((3, 16, H), BF16),
        pltpu.VMEM((2, 8, H), F32),
        pltpu.VMEM((8, H), F32),
        pltpu.VMEM((2, T, D), F32),
        pltpu.VMEM((T, D), F32),
        pltpu.VMEM((2, T, H), BF16),
        pltpu.VMEM((T, H), BF16),
        pltpu.VMEM((T + 2 * PAD, D), F32),
        pltpu.VMEM((32, D), F32),
        pltpu.VMEM((32, H), F32),
        pltpu.VMEM((32, H), F32),
        pltpu.VMEM((16, 8, 256), F32),
        pltpu.VMEM((15, 8, 256), F32),
        pltpu.VMEM((8, 8, 256), F32),
        pltpu.VMEM((16, 8, 256), F32),
        pltpu.VMEM((16, 8, 256), F32),
        dma((4,)), dma((4,)),
        dma((14,)), dma((14,)),
        dma((12,)), dma((12,)),
        dma((12,)), dma((12,)),
        dma((8,)), dma((8,)),
        dma((39,)), dma((39,)),
        dma((10,)), dma((10,)),
        dma((6,)), dma((5,)),
        pltpu.SemaphoreType.REGULAR((3,)),
    ]
    hbm = pl.BlockSpec(memory_space=pl.ANY)
    shapes = (
        jax.ShapeDtypeStruct((T, D), BF16),
        jax.ShapeDtypeStruct((T, D), BF16),
        jax.ShapeDtypeStruct((6, D), F32),
        jax.ShapeDtypeStruct((TAPS, D), F32),
        jax.ShapeDtypeStruct((1, D), F32),
    )
    results = pl.pallas_call(
        fused,
        out_shape=shapes,
        in_specs=[hbm] * 6,
        out_specs=[hbm] * 5,
        scratch_shapes=scratch,
        compiler_params=pltpu.CompilerParams(
            collective_id=0, has_side_effects=True, vmem_limit_bytes=60 << 20
        ),
        name="conv_module",
    )(inputs[0], lengths, kernel, norm_gain, weight, cotangent[0])
    projected, grad_input, grad_weight, grad_kernel, grad_gain = pl.pallas_call(
        deliver,
        out_shape=shapes[:4] + (jax.ShapeDtypeStruct((D,), F32),),
        in_specs=[hbm] * 5,
        out_specs=[hbm] * 5,
        scratch_shapes=[pltpu.VMEM(r.shape, r.dtype) for r in shapes] + [pltpu.VMEM((D,), F32), dma((10,))],
        compiler_params=pltpu.CompilerParams(vmem_limit_bytes=60 << 20),
        name="deliver",
    )(*results)
    return (projected[None], grad_input[None], grad_weight, grad_kernel, grad_gain)


def solution(mesh):
    in_specs = (
        P("batch", "tm", None),
        P("batch"),
        P(),
        P(),
        P("batch", None),
        P("batch", "tm", None),
    )
    out_specs = (P("batch", "tm", None), P("batch", "tm", None), P(("batch", "tm"), None), P(), P())
    return jax.shard_map(
        on_device, mesh=mesh, in_specs=in_specs, out_specs=out_specs, check_vma=False
    )
```

```python
import jax
import jax.numpy as jnp
from jax import lax
from jax.experimental import pallas as pl
from jax.experimental.pallas import tpu as pltpu
from jax.sharding import PartitionSpec as P

F32, BF16 = jnp.float32, jnp.bfloat16
MESH = pl.DeviceIdType.MESH
D, T, H, TAPS = 1536, 128, 768, 31
PAD = 16
CX, CY = 256, 512
LANES = 128
CHUNKS = D // LANES


def lanes_of(k):
    return pl.ds(pl.multiple_of(k * LANES, LANES), LANES)


def fused(
    x_hbm, len_hbm, kern_hbm, gain_hbm, w_hbm, cot_hbm,
    proj_hbm, gin_hbm, gw_hbm, gk_hbm, gg_hbm,
    len_ref, x_ref, kern_ref, gain_ref, proj_ref, gin_ref, gw_ref, gk_ref, gg_ref,
    hx, xf, cv, ds, rs_sum, ab, tf, tp, at2, atm, ub, wb, px, py, rx, ry, s2x, s2y, r2x, r2y,
    facc, zs, rz, fin, cr, agp, agr, pj, pjr, cg, gkb, gcr, gh, gp, zr, xs, fg, fgr,
    sem_halo_s, sem_halo_r, sem_w_s, sem_w_r, sem_c_s, sem_c_r, sem_p_s, sem_p_r,
    sem_z_s, sem_z_r, sem_t_s, sem_t_r, sem_a_s, sem_a_r, sem_in, sem_out, sem_far,
):
    b = lax.axis_index("batch")
    t = lax.axis_index("tm")
    y, xl = lax.div(b, 2), lax.rem(b, 2)
    xh, z, c = lax.div(t, 16), lax.rem(lax.div(t, 2), 8), lax.rem(t, 2)
    x = xh * 2 + xl
    oc = 1 - c

    ys = [y] + [lax.rem(y + i, 4) for i in range(1, 4)]
    xr = [x] + [lax.rem(x + i, 4) for i in range(1, 4)]
    zr_ = [z] + [lax.rem(z + i, 8) for i in range(1, 8)]
    low, high = [lax.rem(v, 2) for v in xr], [lax.div(v, 2) for v in xr]
    blocks = [l * 2 + h for l, h in zip(low, high)]

    def dev(dy, dx, z_, c_):
        return (ys[dy] * 2 + low[dx], high[dx] * 16 + z_ * 2 + c_)

    def along_y(i):
        return dev(i, 0, z, c)

    def along_x(i):
        return dev(0, i, z, c)

    def along_z(i):
        return dev(0, 0, zr_[i], c)

    mate = dev(0, 0, z, oc)
    zp = lax.rem(z, 2)
    zh = lax.div(z, 2)
    zhs = [zh] + [lax.rem(zh + i, 4) for i in range(1, 4)]
    z_mate = z + 1 - 2 * zp
    across, diagonal = dev(0, 0, z_mate, c), dev(0, 0, z_mate, oc)
    before, after = (b, t - 1), (b, t + 1)

    q = blocks[0]

    def half(c_):
        return pl.ds(pl.multiple_of(c_ * H, H), H)

    def frames_of(c_):
        return pl.ds(pl.multiple_of(c_ * T, T), T)

    started = []

    def copy(src, dst, ss, rs, to):
        return pltpu.make_async_remote_copy(
            src_ref=src, dst_ref=dst, send_sem=ss, recv_sem=rs, device_id=to, device_id_type=MESH
        )

    def send(*args):
        item = copy(*args)
        item.start()
        started.append(item)
        return item

    def sent_so_far():
        items = list(started)
        started.clear()
        return items

    def all_sent(items):
        for item in items:
            item.wait_send()

    barrier = pltpu.get_barrier_semaphore()

    def greet(to):
        pl.semaphore_signal(barrier, inc=1, device_id=to, device_id_type=MESH)

    greet(mate)
    greet(diagonal)
    beside = [along_x(1), along_x(3), along_y(1), along_y(3), along_z(1), along_z(7)]
    for to in beside:
        greet(to)

    @pl.when(t > 0)
    def _():
        greet(before)

    @pl.when(t < 31)
    def _():
        greet(after)

    mine = zp * 2 + c
    w_own = pl.ds(pl.multiple_of((y * 2 + xl) * 192, 192), 192)
    loads = [
        pltpu.make_async_copy(src, dst, sem_in.at[n])
        for n, (src, dst) in enumerate((
            (x_hbm, x_ref), (cot_hbm.at[:, half(c)], ub.at[frames_of(mine)]), (w_hbm.at[:, half(c)], wb.at[w_own]),
            (kern_hbm, kern_ref), (gain_hbm, gain_ref), (len_hbm, len_ref),
        ))
    ]
    for item in loads:
        item.start()
    others = 8 + jnp.where(t > 0, 1, 0) + jnp.where(t < 31, 1, 0)
    pl.semaphore_wait(barrier, others)

    to_before = copy(x_hbm.at[pl.ds(0, PAD)], hx.at[1], sem_halo_s.at[0], sem_halo_r.at[1], before)
    to_after = copy(x_hbm.at[pl.ds(T - PAD, PAD)], hx.at[0], sem_halo_s.at[1], sem_halo_r.at[0], after)

    @pl.when(t > 0)
    def _():
        to_before.start()

    @pl.when(t < 31)
    def _():
        to_after.start()

    u_swaps = [
        send(cot_hbm.at[:, half(c_)], ub.at[frames_of(mine)], ss, rs, to)
        for c_, ss, rs, to in (
            (oc, sem_c_s.at[0], sem_c_r.at[0], mate),
            (c, sem_a_s.at[0], sem_a_r.at[0], across),
            (oc, sem_a_s.at[1], sem_a_r.at[1], diagonal),
        )
    ]

    def tell(n):
        for to in beside:
            pl.semaphore_signal(sem_far.at[n], inc=1, device_id=to, device_id_type=MESH)

    def told(n):
        pl.semaphore_wait(sem_far.at[n], len(beside))

    def rows_of(y_, xl_, side):
        return wb.at[pl.ds(pl.multiple_of((y_ * 2 + xl_) * 192 + side * 96, 96), 96)]

    y_up, y_down, y_far = ys[1], ys[3], ys[2]
    x_step = (1, 3)

    def push(here, n, to):
        send(here, here, sem_w_s.at[n], sem_w_r.at[n], to)

    def landed(here, n):
        copy(here, here, sem_w_s.at[n], sem_w_r.at[n], mate).wait_recv()

    def push_own(side, n, to):
        send(w_hbm.at[pl.ds(side * 96, 96), half(c)], rows_of(y, xl, side), sem_w_s.at[n], sem_w_r.at[n], to)

    push_own(0, 0, along_y(1))
    push_own(1, 3, along_y(3))
    for side in range(2):
        push_own(side, 6 + side, along_x(x_step[side]))
    push_own(1, 1, along_y(1))
    push_own(0, 2, along_y(3))

    tell(0)

    loads[5].wait()
    position = t * T + lax.broadcasted_iota(jnp.int32, (T, LANES), 0)
    live = jnp.where(position < len_ref[0], 1.0, 0.0).astype(F32)
    loads[0].wait()

    def mask_chunk(k, _):
        at_lanes = lanes_of(k)
        masked = x_ref[:, at_lanes].astype(F32) * live
        xf[PAD:PAD + T, at_lanes] = masked
        return 0

    lax.fori_loop(0, CHUNKS, mask_chunk, 0)

    for item in loads[3:5]:
        item.wait()

    def conv(source, taps, forward):
        count = source.shape[0] - 32
        total = None
        for r in range(8):
            part = None
            for k in range(4):
                offset = 8 * k + r
                tap = offset - 1 if forward else TAPS - offset
                if 0 <= tap < TAPS:
                    value = taps[tap:tap + 1] * source[8 * k:8 * k + count + 8]
                    part = value if part is None else part + value
            part = part[r:r + count]
            total = part if total is None else total + part
        return total

    def conv_chunk(start, count):
        def body(k, total):
            at_lanes = lanes_of(k)
            value = conv(xf[start:start + count + 32, at_lanes], kern_ref[:, at_lanes], True)
            value = value * live[start:start + count]
            cv[start:start + count, at_lanes] = value
            return total + value
        rs_sum[start:start + count, :] = lax.fori_loop(0, CHUNKS, body, jnp.zeros((count, LANES), F32))

    conv_chunk(PAD, T - 2 * PAD)

    def alive_halo(side, row, frame):
        frames = frame + lax.broadcasted_iota(jnp.int32, (PAD, D), 0)
        alive = jnp.where(frames < len_ref[0], 1.0, 0.0).astype(F32)
        xf[row:row + PAD, :] = hx[side].astype(F32) * alive

    @pl.when(t > 0)
    def _():
        to_after.wait_recv()
        alive_halo(0, 0, t * T - PAD)

    @pl.when(t == 0)
    def _():
        xf[0:PAD, :] = jnp.zeros((PAD, D), F32)

    @pl.when(t < 31)
    def _():
        to_before.wait_recv()
        alive_halo(1, PAD + T, t * T + T)

    @pl.when(t == 31)
    def _():
        xf[PAD + T:, :] = jnp.zeros((PAD, D), F32)

    conv_chunk(0, PAD)
    conv_chunk(T - PAD, PAD)

    told(0)
    tell(1)

    zero = jnp.zeros((T, LANES), F32)
    total = rs_sum[...]
    average = jnp.broadcast_to(jnp.sum(total, axis=1, keepdims=True) * (1.0 / D), (T, LANES))

    def variance_chunk(k, total):
        centred = cv[:, lanes_of(k)] - average
        return total + centred * centred

    total = lax.fori_loop(0, CHUNKS, variance_chunk, zero)
    variance = jnp.sum(total, axis=1, keepdims=True) * (1.0 / D)
    inv = jnp.broadcast_to(lax.rsqrt(variance + 1e-05), (T, LANES))

    def act_chunk(k, _):
        at_lanes = lanes_of(k)
        normed = (cv[:, at_lanes] - average) * inv
        scaled = normed * gain_ref[at_lanes][None]
        gate = 1.0 / (1.0 + jnp.exp(-scaled))
        act = scaled * gate
        cv[:, at_lanes] = normed
        ds[:, at_lanes] = gate * (1.0 + scaled * (1.0 - gate))
        ab[frames_of(c), at_lanes] = act.astype(BF16)
        tf[pl.ds(pl.multiple_of(lax.rem(k, 3) * LANES, LANES), LANES), :] = act.T
        return 0

    def pass_on(*pieces):
        for n, from_y, side in pieces:
            here = rows_of(from_y, xl, side)
            landed(here, n + side)
            push(here, 8 + n + side, along_x(x_step[side]))

    pass_on((0, y_down, 0), (2, y_up, 1))
    push(rows_of(y_down, xl, 0), 4, along_y(1))
    push(rows_of(y_up, xl, 1), 5, along_y(3))

    swaps, z_swaps, a_swaps = [], [], []
    for part in range(4):
        lax.fori_loop(part * 3, part * 3 + 3, act_chunk, 0)
        for parity in range(2):
            for g in range(16):
                tp[12 * g:12 * g + 12, :] = tf[24 * g + 12 * parity:24 * g + 12 * parity + 12, :]
            at2[parity, part * 192:part * 192 + 192, :] = tp[...].astype(BF16)
        rows = pl.ds(part * 192, 192)
        there = atm.at[rows, frames_of(mine)]
        z_swaps.append(send(at2.at[1 - zp, rows], there, sem_a_s.at[2 + part], sem_a_r.at[2 + part], across))
        swaps.append(send(at2.at[zp, rows], there, sem_c_s.at[1 + part], sem_c_r.at[1 + part], mate))
        atm[rows, frames_of(mine)] = at2[zp, part * 192:part * 192 + 192, :]
    here = ab.at[frames_of(c)]
    a_swaps.append(send(here, here, sem_c_s.at[5], sem_c_r.at[5], mate))

    told(1)
    tell(2)

    pass_on((2, y_up, 0), (0, y_down, 1))
    for side in range(2):
        here = rows_of(y_far, xl, side)
        landed(here, 4 + side)
        push(here, 12 + side, along_x(x_step[side]))

    loads[1].wait()
    loads[2].wait()
    for item in u_swaps:
        item.wait_recv()
    for slot in range(4):
        first_frame = (xh * 16 + (z - zp) * 2 + slot) * T
        alive = jnp.where(position - t * T + first_frame < len_ref[0], 1.0, 0.0).astype(F32)

        def mask_upstream(k, _):
            rows, at_lanes = slice(slot * T, slot * T + T), lanes_of(k)
            ub[rows, at_lanes] = (ub[rows, at_lanes].astype(F32) * alive).astype(BF16)
            return 0

        lax.fori_loop(0, H // LANES, mask_upstream, 0)

    theirs = (1 - zp) * 2 + c
    for part in range(4):
        z_swaps[part].wait_recv()
        here = atm.at[pl.ds(part * 192, 192), frames_of(theirs)]
        swaps.append(send(here, here, sem_a_s.at[6 + part], sem_a_r.at[6 + part], mate))

    told(2)

    for item in swaps:
        item.wait_recv()

    def partial(n, start, width):
        rows = pl.ds(pl.multiple_of(n * 192, 192), 192)
        value = jnp.dot(atm[rows, :], ub[:, start:start + width], preferred_element_type=F32)
        return value.reshape(4, 48, width).astype(BF16)

    y_first = []
    for i in (2, 1, 3, 0):
        to_y = ys[i]
        py[to_y] = partial(to_y, CX, CY)
        if i:
            y_first.append(send(py.at[to_y], ry.at[i - 1], sem_p_s.at[2 + i], sem_p_r.at[2 + i], along_y(i)))

    def partial_x(n, _):
        px[n] = partial(n, 0, CX)
        return 0

    lax.fori_loop(0, 4, partial_x, 0)
    x_first = [
        send(px.at[:, blocks[i]], rx.at[i - 1], sem_p_s.at[i - 1], sem_p_r.at[i - 1], along_x(i))
        for i in (2, 1, 3)
    ]

    ag_swaps = []
    chip_rows = pl.ds(pl.multiple_of(zp * 2 * T, 2 * T), 2 * T)
    for n, from_y in ((6, y), (8, y_down), (10, y_up), (12, y_far)):
        for side in range(2):
            landed(rows_of(from_y, 1 - xl, side), n + side)
        cols = pl.ds(pl.multiple_of(from_y * 384, 384), 384)
        value = lax.dot_general(
            ub[chip_rows, :], wb[cols, :], (((1,), (1,)), ((), ())), preferred_element_type=F32
        )
        agp[0, :, cols] = value[:T]
        agp[1, :, cols] = value[T:]
        k = len(ag_swaps)
        ag_swaps.append(
            send(agp.at[oc, :, cols], agr.at[:, cols], sem_c_s.at[6 + k], sem_c_r.at[6 + k], mate)
        )

    for item in a_swaps:
        item.wait_recv()

    def project_chunk(n, _):
        cols = pl.ds(pl.multiple_of(n * 256, 256), 256)
        value = jnp.dot(ab[...], wb[:, cols], preferred_element_type=F32).astype(BF16)
        pj[0, :, cols] = value[:T]
        pj[1, :, cols] = value[T:]
        return 0

    lax.fori_loop(0, 3, project_chunk, 0)
    pj_swap = send(pj.at[oc], pjr, sem_c_s.at[10], sem_c_r.at[10], mate)
    proj_ref[:, half(c)] = pj[c]

    for item in ag_swaps:
        item.wait_recv()

    def back_chunk(k, sums):
        at_lanes = lanes_of(k)
        normed = cv[:, at_lanes]
        scaled_grad = (agp[c, :, at_lanes] + agr[:, at_lanes]) * ds[:, at_lanes]
        gkb[TAPS:TAPS + 1, at_lanes] = jnp.sum(scaled_grad * normed, axis=0, keepdims=True)
        normed_grad = scaled_grad * gain_ref[at_lanes][None]
        ds[:, at_lanes] = normed_grad
        return (sums[0] + normed_grad, sums[1] + normed_grad * normed)

    sums = lax.fori_loop(0, CHUNKS, back_chunk, (zero, zero))
    first, second = [
        jnp.broadcast_to(jnp.sum(s, axis=1, keepdims=True) * (1.0 / D), (T, LANES)) for s in sums
    ]
    inv_live = inv * live

    def taps_chunk(k, _):
        at_lanes = lanes_of(k)
        source = xf[:, at_lanes]
        grad = inv_live * (ds[:, at_lanes] - first - cv[:, at_lanes] * second)
        cg[PAD:PAD + T, at_lanes] = grad
        for r in range(8):
            shifted = source[r:r + T + 24]
            for j in range(4):
                tap = 8 * j + r - 1
                if 0 <= tap < TAPS:
                    gkb[tap:tap + 1, at_lanes] = jnp.sum(grad * shifted[8 * j:8 * j + T], axis=0, keepdims=True)
        return 0

    lax.fori_loop(oc * 6, oc * 6 + 6, taps_chunk, 0)
    gk_swap = send(gkb.at[:, half(oc)], gcr, sem_t_s.at[0], sem_t_r.at[0], mate)
    lax.fori_loop(c * 6, c * 6 + 6, taps_chunk, 0)
    g_before = copy(cg.at[pl.ds(PAD, PAD)], cg.at[pl.ds(PAD + T, PAD)], sem_halo_s.at[2], sem_halo_r.at[3], before)
    g_after = copy(cg.at[pl.ds(T, PAD)], cg.at[pl.ds(0, PAD)], sem_halo_s.at[3], sem_halo_r.at[2], after)

    @pl.when(t > 0)
    def _():
        g_before.start()

    @pl.when(t < 31)
    def _():
        g_after.start()

    def pieces():
        for n in range(16):
            yield n, slice(n // 4 * 8, n // 4 * 8 + 8), slice(n % 4 * 192, n % 4 * 192 + 192)

    plane = (10, 9, 11, 6, 14, 2, 8, 5, 7, 13, 15, 1, 3, 4, 12)
    line = (4, 3, 5, 2, 6, 1, 7)
    here = y * 4 + x

    def in_plane(i):
        return ys[i // 4] * 4 + xr[i % 4], dev(i // 4, i % 4, z, c)

    early = sent_so_far()
    gk_swap.wait_recv()
    gh[...] = gkb[:, half(c)] + gcr[...]
    gp[...] = jnp.zeros((16, 8, 256), F32)
    for n, rows, cols in pieces():
        gp[n, :, 0:192] = gh[rows, cols]
    t_plane = []
    for i in plane:
        n, to = in_plane(i)
        t_plane.append(send(gp.at[n], zr.at[i - 1], sem_t_s.at[i], sem_t_r.at[i], to))

    def add(first, own, came, out):
        for item in first:
            item.wait_recv()

        def body(n, _):
            value = own(n).astype(F32)
            for i in range(3):
                value = value + came[i, n].astype(F32)
            out[n] = value.astype(BF16)
            return 0

        lax.fori_loop(0, 4, body, 0)

    add(x_first, lambda n: px[n, q], rx, s2x)
    x_second = [
        send(s2x.at[ys[i]], r2x.at[i - 1], sem_p_s.at[5 + i], sem_p_r.at[5 + i], along_y(i))
        for i in (2, 1, 3)
    ]
    add(y_first, lambda n: py[y, n], ry, s2y)
    y_second = [
        send(s2y.at[blocks[i]], r2y.at[i - 1], sem_p_s.at[8 + i], sem_p_r.at[8 + i], along_x(i))
        for i in (2, 1, 3)
    ]

    @pl.when(t > 0)
    def _():
        g_after.wait_recv()

    @pl.when(t == 0)
    def _():
        cg[0:PAD, :] = jnp.zeros((PAD, D), F32)

    @pl.when(t < 31)
    def _():
        g_before.wait_recv()

    @pl.when(t == 31)
    def _():
        cg[PAD + T:, :] = jnp.zeros((PAD, D), F32)

    def input_chunk(k, _):
        at_lanes = lanes_of(k)
        value = conv(cg[:, at_lanes], kern_ref[:, at_lanes], False) * live
        gin_ref[:, at_lanes] = value.astype(BF16)
        return 0

    all_sent(early)

    for item in t_plane:
        item.wait_recv()
    total = gp[here]
    for i in range(15):
        total = total + zr[i]
    xs[z] = total
    for i in line:
        slot = xs.at[z]
        send(slot, slot, sem_t_s.at[15 + i], sem_t_r.at[15 + i], along_z(i))

    for item in x_second + y_second:
        item.wait_recv()
    left, right = s2x[y].astype(F32), s2y[q].astype(F32)
    for i in range(3):
        left = left + r2x[i].astype(F32)
        right = right + r2y[i].astype(F32)
    facc[0:48, 0:CX] = left
    facc[0:48, CX:H] = right
    facc[48:56, :] = jnp.zeros((8, H), F32)
    for n in range(4):
        zs[n] = facc[12 * n:12 * n + 16, :].astype(BF16)
    w_z = [
        send(zs.at[zhs[i]], rz.at[i - 1], sem_z_s.at[i - 1], sem_z_r.at[i - 1], along_z(2 * i))
        for i in (2, 1, 3)
    ]

    lax.fori_loop(0, CHUNKS, input_chunk, 0)
    for i in range(1, 8):
        slot = xs.at[zr_[8 - i]]
        copy(slot, slot, sem_t_s.at[15 + i], sem_t_r.at[15 + i], mate).wait_recv()
    total = xs[0]
    for i in range(1, 8):
        total = total + xs[i]
    fg[here] = total
    middle = sent_so_far()
    for i in plane:
        send(fg.at[here], fg.at[here], sem_t_s.at[22 + i], sem_t_r.at[22 + i], in_plane(i)[1])

    stores = [pltpu.make_async_copy(gin_ref, gin_hbm, sem_out.at[0])]
    stores[0].start()
    all_sent(middle)

    @pl.when(t > 0)
    def _():
        to_before.wait_send()
        g_before.wait_send()

    @pl.when(t < 31)
    def _():
        to_after.wait_send()
        g_after.wait_send()

    pj_swap.wait_recv()
    proj_ref[:, half(oc)] = pjr[...]
    stores.append(pltpu.make_async_copy(proj_ref, proj_hbm, sem_out.at[1]))
    stores[1].start()

    for item in w_z:
        item.wait_recv()
    rows = zs[zh].astype(F32)
    for i in range(3):
        rows = rows + rz[i].astype(F32)
    fin[...] = jnp.zeros((2, 8, H), F32)
    fin[0, 0:6, :] = rows[0:6]
    fin[1, 0:6, :] = rows[6:12]
    w_swap = send(fin.at[oc], cr, sem_z_s.at[3], sem_z_r.at[3], mate)

    for i in range(1, 16):
        slot = fg.at[ys[-(i // 4) % 4] * 4 + xr[-(i % 4) % 4]]
        copy(slot, slot, sem_t_s.at[22 + i], sem_t_r.at[22 + i], mate).wait_recv()
    late = sent_so_far()
    t_swap = send(fg, fgr, sem_t_s.at[38], sem_t_r.at[38], mate)

    def put_taps(cols, source):
        for n, rows, part in pieces():
            gh[rows, part] = source[n, :, 0:192]
        gk_ref[:, cols] = gh[0:TAPS, :]
        gg_ref[:, cols] = gh[TAPS:TAPS + 1, :]

    put_taps(half(c), fg)
    all_sent(late)
    gw_ref[:, half(c)] = fin[c][0:6]
    t_swap.wait_recv()
    put_taps(half(oc), fgr)
    w_swap.wait_recv()
    gw_ref[:, half(oc)] = cr[0:6, :]
    for n, (src, dst) in enumerate(((gw_ref, gw_hbm), (gk_ref, gk_hbm), (gg_ref, gg_hbm))):
        stores.append(pltpu.make_async_copy(src, dst, sem_out.at[2 + n]))
        stores[-1].start()

    all_sent(started)
    for item in stores:
        item.wait()


def deliver(*refs):
    sources, results, kept, flat, sems = refs[:5], refs[5:10], refs[10:15], refs[15], refs[16]
    loads = [pltpu.make_async_copy(a, b, sems.at[n]) for n, (a, b) in enumerate(zip(sources, kept))]
    stores = [pltpu.make_async_copy(a, b, sems.at[5 + n]) for n, (a, b) in enumerate(zip(kept[:4] + (flat,), results))]
    for item in loads:
        item.start()
    for first, then in zip(loads[:4], stores):
        first.wait()
        then.start()
    loads[4].wait()
    flat[...] = kept[4][0]
    stores[4].start()
    for item in stores:
        item.wait()


def on_device(inputs, lengths, kernel, norm_gain, weight, cotangent):
    vmem = pl.BlockSpec(memory_space=pltpu.VMEM)
    dma = pltpu.SemaphoreType.DMA
    scratch = [
        pltpu.SMEM((1,), jnp.int32),
        pltpu.VMEM((T, D), BF16),
        pltpu.VMEM((TAPS, D), F32),
        pltpu.VMEM((D,), F32),
        pltpu.VMEM((T, D), BF16),
        pltpu.VMEM((T, D), BF16),
        pltpu.VMEM((6, D), F32),
        pltpu.VMEM((TAPS, D), F32),
        pltpu.VMEM((1, D), F32),
        pltpu.VMEM((2, PAD, D), BF16),
        pltpu.VMEM((T + 2 * PAD, D), F32),
        pltpu.VMEM((T, D), F32),
        pltpu.VMEM((T, D), F32),
        pltpu.VMEM((T, LANES), F32),
        pltpu.VMEM((2 * T, D), BF16),
        pltpu.VMEM((3 * LANES, T), F32),
        pltpu.VMEM((192, T), F32),
        pltpu.VMEM((2, H, T), BF16),
        pltpu.VMEM((H, 4 * T), BF16),
        pltpu.VMEM((4 * T, H), BF16),
        pltpu.VMEM((D, H), BF16),
        pltpu.VMEM((4, 4, 48, CX), BF16),
        pltpu.VMEM((4, 4, 48, CY), BF16),
        pltpu.VMEM((3, 4, 48, CX), BF16),
        pltpu.VMEM((3, 4, 48, CY), BF16),
        pltpu.VMEM((4, 48, CX), BF16),
        pltpu.VMEM((4, 48, CY), BF16),
        pltpu.VMEM((3, 48, CX), BF16),
        pltpu.VMEM((3, 48, CY), BF16),
        pltpu.VMEM((56, H), F32),
        pltpu.VMEM((4, 16, H), BF16),
        pltpu.VMEM((3, 16, H), BF16),
        pltpu.VMEM((2, 8, H), F32),
        pltpu.VMEM((8, H), F32),
        pltpu.VMEM((2, T, D), F32),
        pltpu.VMEM((T, D), F32),
        pltpu.VMEM((2, T, H), BF16),
        pltpu.VMEM((T, H), BF16),
        pltpu.VMEM((T + 2 * PAD, D), F32),
        pltpu.VMEM((32, D), F32),
        pltpu.VMEM((32, H), F32),
        pltpu.VMEM((32, H), F32),
        pltpu.VMEM((16, 8, 256), F32),
        pltpu.VMEM((15, 8, 256), F32),
        pltpu.VMEM((8, 8, 256), F32),
        pltpu.VMEM((16, 8, 256), F32),
        pltpu.VMEM((16, 8, 256), F32),
        dma((4,)), dma((4,)),
        dma((14,)), dma((14,)),
        dma((12,)), dma((12,)),
        dma((12,)), dma((12,)),
        dma((8,)), dma((8,)),
        dma((39,)), dma((39,)),
        dma((10,)), dma((10,)),
        dma((6,)), dma((5,)),
        pltpu.SemaphoreType.REGULAR((3,)),
    ]
    hbm = pl.BlockSpec(memory_space=pl.ANY)
    shapes = (
        jax.ShapeDtypeStruct((T, D), BF16),
        jax.ShapeDtypeStruct((T, D), BF16),
        jax.ShapeDtypeStruct((6, D), F32),
        jax.ShapeDtypeStruct((TAPS, D), F32),
        jax.ShapeDtypeStruct((1, D), F32),
    )
    results = pl.pallas_call(
        fused,
        out_shape=shapes,
        in_specs=[hbm] * 6,
        out_specs=[hbm] * 5,
        scratch_shapes=scratch,
        compiler_params=pltpu.CompilerParams(
            collective_id=0, has_side_effects=True, vmem_limit_bytes=60 << 20
        ),
        name="conv_module",
    )(inputs[0], lengths, kernel, norm_gain, weight, cotangent[0])
    projected, grad_input, grad_weight, grad_kernel, grad_gain = pl.pallas_call(
        deliver,
        out_shape=shapes[:4] + (jax.ShapeDtypeStruct((D,), F32),),
        in_specs=[hbm] * 5,
        out_specs=[hbm] * 5,
        scratch_shapes=[pltpu.VMEM(r.shape, r.dtype) for r in shapes] + [pltpu.VMEM((D,), F32), dma((10,))],
        compiler_params=pltpu.CompilerParams(vmem_limit_bytes=60 << 20),
        name="deliver",
    )(*results)
    return (projected[None], grad_input[None], grad_weight, grad_kernel, grad_gain)


def solution(mesh):
    in_specs = (
        P("batch", "tm", None),
        P("batch"),
        P(),
        P(),
        P("batch", None),
        P("batch", "tm", None),
    )
    out_specs = (P("batch", "tm", None), P("batch", "tm", None), P(("batch", "tm"), None), P(), P())
    return jax.shard_map(
        on_device, mesh=mesh, in_specs=in_specs, out_specs=out_specs, check_vma=False
    )
```

```python
import jax
import jax.numpy as jnp
from jax import lax
from jax.experimental import pallas as pl
from jax.experimental.pallas import tpu as pltpu
from jax.sharding import PartitionSpec as P

F32, BF16 = jnp.float32, jnp.bfloat16
MESH = pl.DeviceIdType.MESH
D, T, H, TAPS = 1536, 128, 768, 31
PAD = 16
CX, CY = 256, 512
LANES = 128
CHUNKS = D // LANES


def lanes_of(k):
    return pl.ds(pl.multiple_of(k * LANES, LANES), LANES)


def fused(
    x_hbm, len_hbm, kern_hbm, gain_hbm, w_hbm, cot_hbm,
    proj_hbm, gin_hbm, gw_hbm, gk_hbm, gg_hbm,
    len_ref, x_ref, kern_ref, gain_ref, proj_ref, gin_ref, gw_ref, gk_ref, gg_ref,
    hx, xf, cv, ds, rs_sum, ab, tf, tp, at2, atm, ub, wb, px, py, rx, ry, s2x, s2y, r2x, r2y,
    facc, zs, rz, fin, cr, agp, agr, pj, pjr, cg, gkb, gcr, gh, gp, zr, xs, fg, fgr,
    sem_halo_s, sem_halo_r, sem_w_s, sem_w_r, sem_c_s, sem_c_r, sem_p_s, sem_p_r,
    sem_z_s, sem_z_r, sem_t_s, sem_t_r, sem_a_s, sem_a_r, sem_in, sem_out, sem_far,
):
    b = lax.axis_index("batch")
    t = lax.axis_index("tm")
    y, xl = lax.div(b, 2), lax.rem(b, 2)
    xh, z, c = lax.div(t, 16), lax.rem(lax.div(t, 2), 8), lax.rem(t, 2)
    x = xh * 2 + xl
    oc = 1 - c

    ys = [y] + [lax.rem(y + i, 4) for i in range(1, 4)]
    xr = [x] + [lax.rem(x + i, 4) for i in range(1, 4)]
    zr_ = [z] + [lax.rem(z + i, 8) for i in range(1, 8)]
    low, high = [lax.rem(v, 2) for v in xr], [lax.div(v, 2) for v in xr]
    blocks = [l * 2 + h for l, h in zip(low, high)]

    def dev(dy, dx, z_, c_):
        return (ys[dy] * 2 + low[dx], high[dx] * 16 + z_ * 2 + c_)

    def along_y(i):
        return dev(i, 0, z, c)

    def along_x(i):
        return dev(0, i, z, c)

    def along_z(i):
        return dev(0, 0, zr_[i], c)

    mate = dev(0, 0, z, oc)
    zp = lax.rem(z, 2)
    zh = lax.div(z, 2)
    zhs = [zh] + [lax.rem(zh + i, 4) for i in range(1, 4)]
    z_mate = z + 1 - 2 * zp
    across, diagonal = dev(0, 0, z_mate, c), dev(0, 0, z_mate, oc)
    before, after = (b, t - 1), (b, t + 1)

    q = blocks[0]

    def half(c_):
        return pl.ds(pl.multiple_of(c_ * H, H), H)

    def frames_of(c_):
        return pl.ds(pl.multiple_of(c_ * T, T), T)

    started = []

    def copy(src, dst, ss, rs, to):
        return pltpu.make_async_remote_copy(
            src_ref=src, dst_ref=dst, send_sem=ss, recv_sem=rs, device_id=to, device_id_type=MESH
        )

    def send(*args):
        item = copy(*args)
        item.start()
        started.append(item)
        return item

    def sent_so_far():
        items = list(started)
        started.clear()
        return items

    def all_sent(items):
        for item in items:
            item.wait_send()

    barrier = pltpu.get_barrier_semaphore()

    def greet(to):
        pl.semaphore_signal(barrier, inc=1, device_id=to, device_id_type=MESH)

    greet(mate)
    greet(diagonal)
    beside = [along_x(1), along_x(3), along_y(1), along_y(3), along_z(1), along_z(7)]
    for to in beside:
        greet(to)

    @pl.when(t > 0)
    def _():
        greet(before)

    @pl.when(t < 31)
    def _():
        greet(after)

    mine = zp * 2 + c
    w_own = pl.ds(pl.multiple_of((y * 2 + xl) * 192, 192), 192)
    loads = [
        pltpu.make_async_copy(src, dst, sem_in.at[n])
        for n, (src, dst) in enumerate((
            (x_hbm, x_ref), (cot_hbm.at[:, half(c)], ub.at[frames_of(mine)]), (w_hbm.at[:, half(c)], wb.at[w_own]),
            (kern_hbm, kern_ref), (gain_hbm, gain_ref), (len_hbm, len_ref),
        ))
    ]
    for item in loads:
        item.start()
    others = 8 + jnp.where(t > 0, 1, 0) + jnp.where(t < 31, 1, 0)
    pl.semaphore_wait(barrier, others)

    to_before = copy(x_hbm.at[pl.ds(0, PAD)], hx.at[1], sem_halo_s.at[0], sem_halo_r.at[1], before)
    to_after = copy(x_hbm.at[pl.ds(T - PAD, PAD)], hx.at[0], sem_halo_s.at[1], sem_halo_r.at[0], after)

    @pl.when(t > 0)
    def _():
        to_before.start()

    @pl.when(t < 31)
    def _():
        to_after.start()

    u_swaps = [
        send(cot_hbm.at[:, half(c_)], ub.at[frames_of(mine)], ss, rs, to)
        for c_, ss, rs, to in (
            (oc, sem_c_s.at[0], sem_c_r.at[0], mate),
            (c, sem_a_s.at[0], sem_a_r.at[0], across),
            (oc, sem_a_s.at[1], sem_a_r.at[1], diagonal),
        )
    ]

    def tell(n):
        for to in beside:
            pl.semaphore_signal(sem_far.at[n], inc=1, device_id=to, device_id_type=MESH)

    def told(n):
        pl.semaphore_wait(sem_far.at[n], len(beside))

    def rows_of(y_, xl_, side):
        return wb.at[pl.ds(pl.multiple_of((y_ * 2 + xl_) * 192 + side * 96, 96), 96)]

    y_up, y_down, y_far = ys[1], ys[3], ys[2]
    x_step = (1, 3)

    def push(here, n, to):
        send(here, here, sem_w_s.at[n], sem_w_r.at[n], to)

    def landed(here, n):
        copy(here, here, sem_w_s.at[n], sem_w_r.at[n], mate).wait_recv()

    def push_own(side, n, to):
        send(w_hbm.at[pl.ds(side * 96, 96), half(c)], rows_of(y, xl, side), sem_w_s.at[n], sem_w_r.at[n], to)

    push_own(0, 0, along_y(1))
    push_own(1, 3, along_y(3))
    for side in range(2):
        push_own(side, 6 + side, along_x(x_step[side]))
    push_own(1, 1, along_y(1))
    push_own(0, 2, along_y(3))

    tell(0)

    loads[5].wait()
    position = t * T + lax.broadcasted_iota(jnp.int32, (T, LANES), 0)
    live = jnp.where(position < len_ref[0], 1.0, 0.0).astype(F32)
    loads[0].wait()

    def mask_chunk(k, _):
        at_lanes = lanes_of(k)
        masked = x_ref[:, at_lanes].astype(F32) * live
        xf[PAD:PAD + T, at_lanes] = masked
        return 0

    lax.fori_loop(0, CHUNKS, mask_chunk, 0)

    for item in loads[3:5]:
        item.wait()

    def conv(source, taps, forward):
        count = source.shape[0] - 32
        total = None
        for r in range(8):
            part = None
            for k in range(4):
                offset = 8 * k + r
                tap = offset - 1 if forward else TAPS - offset
                if 0 <= tap < TAPS:
                    value = taps[tap:tap + 1] * source[8 * k:8 * k + count + 8]
                    part = value if part is None else part + value
            part = part[r:r + count]
            total = part if total is None else total + part
        return total

    def conv_chunk(start, count):
        def body(k, total):
            at_lanes = lanes_of(k)
            value = conv(xf[start:start + count + 32, at_lanes], kern_ref[:, at_lanes], True)
            value = value * live[start:start + count]
            cv[start:start + count, at_lanes] = value
            return total + value
        rs_sum[start:start + count, :] = lax.fori_loop(0, CHUNKS, body, jnp.zeros((count, LANES), F32))

    conv_chunk(PAD, T - 2 * PAD)

    def alive_halo(side, row, frame):
        frames = frame + lax.broadcasted_iota(jnp.int32, (PAD, D), 0)
        alive = jnp.where(frames < len_ref[0], 1.0, 0.0).astype(F32)
        xf[row:row + PAD, :] = hx[side].astype(F32) * alive

    @pl.when(t > 0)
    def _():
        to_after.wait_recv()
        alive_halo(0, 0, t * T - PAD)

    @pl.when(t == 0)
    def _():
        xf[0:PAD, :] = jnp.zeros((PAD, D), F32)

    @pl.when(t < 31)
    def _():
        to_before.wait_recv()
        alive_halo(1, PAD + T, t * T + T)

    @pl.when(t == 31)
    def _():
        xf[PAD + T:, :] = jnp.zeros((PAD, D), F32)

    conv_chunk(0, PAD)
    conv_chunk(T - PAD, PAD)

    told(0)
    tell(1)

    zero = jnp.zeros((T, LANES), F32)
    total = rs_sum[...]
    average = jnp.broadcast_to(jnp.sum(total, axis=1, keepdims=True) * (1.0 / D), (T, LANES))

    def variance_chunk(k, total):
        centred = cv[:, lanes_of(k)] - average
        return total + centred * centred

    total = lax.fori_loop(0, CHUNKS, variance_chunk, zero)
    variance = jnp.sum(total, axis=1, keepdims=True) * (1.0 / D)
    inv = jnp.broadcast_to(lax.rsqrt(variance + 1e-05), (T, LANES))

    def act_chunk(k, _):
        at_lanes = lanes_of(k)
        normed = (cv[:, at_lanes] - average) * inv
        scaled = normed * gain_ref[at_lanes][None]
        gate = 1.0 / (1.0 + jnp.exp(-scaled))
        act = scaled * gate
        cv[:, at_lanes] = normed
        ds[:, at_lanes] = gate * (1.0 + scaled * (1.0 - gate))
        ab[frames_of(c), at_lanes] = act.astype(BF16)
        tf[pl.ds(pl.multiple_of(lax.rem(k, 3) * LANES, LANES), LANES), :] = act.T
        return 0

    def pass_on(*pieces):
        for n, from_y, side in pieces:
            here = rows_of(from_y, xl, side)
            landed(here, n + side)
            push(here, 8 + n + side, along_x(x_step[side]))

    pass_on((0, y_down, 0), (2, y_up, 1))
    push(rows_of(y_down, xl, 0), 4, along_y(1))
    push(rows_of(y_up, xl, 1), 5, along_y(3))

    swaps, z_swaps, a_swaps = [], [], []
    for part in range(4):
        lax.fori_loop(part * 3, part * 3 + 3, act_chunk, 0)
        for parity in range(2):
            for g in range(16):
                tp[12 * g:12 * g + 12, :] = tf[24 * g + 12 * parity:24 * g + 12 * parity + 12, :]
            at2[parity, part * 192:part * 192 + 192, :] = tp[...].astype(BF16)
        rows = pl.ds(part * 192, 192)
        there = atm.at[rows, frames_of(mine)]
        z_swaps.append(send(at2.at[1 - zp, rows], there, sem_a_s.at[2 + part], sem_a_r.at[2 + part], across))
        swaps.append(send(at2.at[zp, rows], there, sem_c_s.at[1 + part], sem_c_r.at[1 + part], mate))
        atm[rows, frames_of(mine)] = at2[zp, part * 192:part * 192 + 192, :]
    here = ab.at[frames_of(c)]
    a_swaps.append(send(here, here, sem_c_s.at[5], sem_c_r.at[5], mate))

    told(1)
    tell(2)

    pass_on((2, y_up, 0), (0, y_down, 1))
    for side in range(2):
        here = rows_of(y_far, xl, side)
        landed(here, 4 + side)
        push(here, 12 + side, along_x(x_step[side]))

    loads[1].wait()
    loads[2].wait()
    for item in u_swaps:
        item.wait_recv()
    for slot in range(4):
        first_frame = (xh * 16 + (z - zp) * 2 + slot) * T
        alive = jnp.where(position - t * T + first_frame < len_ref[0], 1.0, 0.0).astype(F32)

        def mask_upstream(k, _):
            rows, at_lanes = slice(slot * T, slot * T + T), lanes_of(k)
            ub[rows, at_lanes] = (ub[rows, at_lanes].astype(F32) * alive).astype(BF16)
            return 0

        lax.fori_loop(0, H // LANES, mask_upstream, 0)

    chip_rows = pl.ds(pl.multiple_of(zp * 2 * T, 2 * T), 2 * T)
    ag_swaps = []

    def act_grad(n, from_y):
        for side in range(2):
            landed(rows_of(from_y, 1 - xl, side), n + side)
        cols = pl.ds(pl.multiple_of(from_y * 384, 384), 384)
        value = lax.dot_general(
            ub[chip_rows, :], wb[cols, :], (((1,), (1,)), ((), ())), preferred_element_type=F32
        )
        agp[0, :, cols] = value[:T]
        agp[1, :, cols] = value[T:]
        k = len(ag_swaps)
        ag_swaps.append(
            send(agp.at[oc, :, cols], agr.at[:, cols], sem_c_s.at[6 + k], sem_c_r.at[6 + k], mate)
        )

    act_grad(6, y)

    theirs = (1 - zp) * 2 + c
    for part in range(4):
        z_swaps[part].wait_recv()
        here = atm.at[pl.ds(part * 192, 192), frames_of(theirs)]
        swaps.append(send(here, here, sem_a_s.at[6 + part], sem_a_r.at[6 + part], mate))

    told(2)

    for item in swaps:
        item.wait_recv()

    def partial(n, start, width):
        rows = pl.ds(pl.multiple_of(n * 192, 192), 192)
        value = jnp.dot(atm[rows, :], ub[:, start:start + width], preferred_element_type=F32)
        return value.reshape(4, 48, width).astype(BF16)

    y_first = []
    for i in (2, 1, 3, 0):
        to_y = ys[i]
        py[to_y] = partial(to_y, CX, CY)
        if i:
            y_first.append(send(py.at[to_y], ry.at[i - 1], sem_p_s.at[2 + i], sem_p_r.at[2 + i], along_y(i)))

    def partial_x(n, _):
        px[n] = partial(n, 0, CX)
        return 0

    lax.fori_loop(0, 4, partial_x, 0)
    x_first = [
        send(px.at[:, blocks[i]], rx.at[i - 1], sem_p_s.at[i - 1], sem_p_r.at[i - 1], along_x(i))
        for i in (2, 1, 3)
    ]

    act_grad(8, y_down)
    act_grad(10, y_up)
    act_grad(12, y_far)

    for item in a_swaps:
        item.wait_recv()

    def project_chunk(n, _):
        cols = pl.ds(pl.multiple_of(n * 256, 256), 256)
        value = jnp.dot(ab[...], wb[:, cols], preferred_element_type=F32).astype(BF16)
        pj[0, :, cols] = value[:T]
        pj[1, :, cols] = value[T:]
        return 0

    lax.fori_loop(0, 3, project_chunk, 0)
    pj_swap = send(pj.at[oc], pjr, sem_c_s.at[10], sem_c_r.at[10], mate)
    proj_ref[:, half(c)] = pj[c]

    for item in ag_swaps:
        item.wait_recv()

    def back_chunk(k, sums):
        at_lanes = lanes_of(k)
        normed = cv[:, at_lanes]
        scaled_grad = (agp[c, :, at_lanes] + agr[:, at_lanes]) * ds[:, at_lanes]
        gkb[TAPS:TAPS + 1, at_lanes] = jnp.sum(scaled_grad * normed, axis=0, keepdims=True)
        normed_grad = scaled_grad * gain_ref[at_lanes][None]
        ds[:, at_lanes] = normed_grad
        return (sums[0] + normed_grad, sums[1] + normed_grad * normed)

    sums = lax.fori_loop(0, CHUNKS, back_chunk, (zero, zero))
    first, second = [
        jnp.broadcast_to(jnp.sum(s, axis=1, keepdims=True) * (1.0 / D), (T, LANES)) for s in sums
    ]
    inv_live = inv * live

    def taps_chunk(k, _):
        at_lanes = lanes_of(k)
        source = xf[:, at_lanes]
        grad = inv_live * (ds[:, at_lanes] - first - cv[:, at_lanes] * second)
        cg[PAD:PAD + T, at_lanes] = grad
        for r in range(8):
            shifted = source[r:r + T + 24]
            for j in range(4):
                tap = 8 * j + r - 1
                if 0 <= tap < TAPS:
                    gkb[tap:tap + 1, at_lanes] = jnp.sum(grad * shifted[8 * j:8 * j + T], axis=0, keepdims=True)
        return 0

    lax.fori_loop(oc * 6, oc * 6 + 6, taps_chunk, 0)
    gk_swap = send(gkb.at[:, half(oc)], gcr, sem_t_s.at[0], sem_t_r.at[0], mate)
    lax.fori_loop(c * 6, c * 6 + 6, taps_chunk, 0)
    g_before = copy(cg.at[pl.ds(PAD, PAD)], cg.at[pl.ds(PAD + T, PAD)], sem_halo_s.at[2], sem_halo_r.at[3], before)
    g_after = copy(cg.at[pl.ds(T, PAD)], cg.at[pl.ds(0, PAD)], sem_halo_s.at[3], sem_halo_r.at[2], after)

    @pl.when(t > 0)
    def _():
        g_before.start()

    @pl.when(t < 31)
    def _():
        g_after.start()

    def pieces():
        for n in range(16):
            yield n, slice(n // 4 * 8, n // 4 * 8 + 8), slice(n % 4 * 192, n % 4 * 192 + 192)

    plane = (10, 9, 11, 6, 14, 2, 8, 5, 7, 13, 15, 1, 3, 4, 12)
    line = (4, 3, 5, 2, 6, 1, 7)
    here = y * 4 + x

    def in_plane(i):
        return ys[i // 4] * 4 + xr[i % 4], dev(i // 4, i % 4, z, c)

    early = sent_so_far()
    gk_swap.wait_recv()
    gh[...] = gkb[:, half(c)] + gcr[...]
    gp[...] = jnp.zeros((16, 8, 256), F32)
    for n, rows, cols in pieces():
        gp[n, :, 0:192] = gh[rows, cols]
    t_plane = []
    for i in plane:
        n, to = in_plane(i)
        t_plane.append(send(gp.at[n], zr.at[i - 1], sem_t_s.at[i], sem_t_r.at[i], to))

    def add(first, own, came, out):
        for item in first:
            item.wait_recv()

        def body(n, _):
            value = own(n).astype(F32)
            for i in range(3):
                value = value + came[i, n].astype(F32)
            out[n] = value.astype(BF16)
            return 0

        lax.fori_loop(0, 4, body, 0)

    add(x_first, lambda n: px[n, q], rx, s2x)
    x_second = [
        send(s2x.at[ys[i]], r2x.at[i - 1], sem_p_s.at[5 + i], sem_p_r.at[5 + i], along_y(i))
        for i in (2, 1, 3)
    ]
    add(y_first, lambda n: py[y, n], ry, s2y)
    y_second = [
        send(s2y.at[blocks[i]], r2y.at[i - 1], sem_p_s.at[8 + i], sem_p_r.at[8 + i], along_x(i))
        for i in (2, 1, 3)
    ]

    @pl.when(t > 0)
    def _():
        g_after.wait_recv()

    @pl.when(t == 0)
    def _():
        cg[0:PAD, :] = jnp.zeros((PAD, D), F32)

    @pl.when(t < 31)
    def _():
        g_before.wait_recv()

    @pl.when(t == 31)
    def _():
        cg[PAD + T:, :] = jnp.zeros((PAD, D), F32)

    def input_chunk(k, _):
        at_lanes = lanes_of(k)
        value = conv(cg[:, at_lanes], kern_ref[:, at_lanes], False) * live
        gin_ref[:, at_lanes] = value.astype(BF16)
        return 0

    all_sent(early)

    for item in t_plane:
        item.wait_recv()
    total = gp[here]
    for i in range(15):
        total = total + zr[i]
    xs[z] = total
    for i in line:
        slot = xs.at[z]
        send(slot, slot, sem_t_s.at[15 + i], sem_t_r.at[15 + i], along_z(i))

    for item in x_second + y_second:
        item.wait_recv()
    left, right = s2x[y].astype(F32), s2y[q].astype(F32)
    for i in range(3):
        left = left + r2x[i].astype(F32)
        right = right + r2y[i].astype(F32)
    facc[0:48, 0:CX] = left
    facc[0:48, CX:H] = right
    facc[48:56, :] = jnp.zeros((8, H), F32)
    for n in range(4):
        zs[n] = facc[12 * n:12 * n + 16, :].astype(BF16)
    w_z = [
        send(zs.at[zhs[i]], rz.at[i - 1], sem_z_s.at[i - 1], sem_z_r.at[i - 1], along_z(2 * i))
        for i in (2, 1, 3)
    ]

    lax.fori_loop(0, CHUNKS, input_chunk, 0)
    for i in range(1, 8):
        slot = xs.at[zr_[8 - i]]
        copy(slot, slot, sem_t_s.at[15 + i], sem_t_r.at[15 + i], mate).wait_recv()
    total = xs[0]
    for i in range(1, 8):
        total = total + xs[i]
    fg[here] = total
    middle = sent_so_far()
    for i in plane:
        send(fg.at[here], fg.at[here], sem_t_s.at[22 + i], sem_t_r.at[22 + i], in_plane(i)[1])

    stores = [pltpu.make_async_copy(gin_ref, gin_hbm, sem_out.at[0])]
    stores[0].start()
    all_sent(middle)

    @pl.when(t > 0)
    def _():
        to_before.wait_send()
        g_before.wait_send()

    @pl.when(t < 31)
    def _():
        to_after.wait_send()
        g_after.wait_send()

    pj_swap.wait_recv()
    proj_ref[:, half(oc)] = pjr[...]
    stores.append(pltpu.make_async_copy(proj_ref, proj_hbm, sem_out.at[1]))
    stores[1].start()

    for item in w_z:
        item.wait_recv()
    rows = zs[zh].astype(F32)
    for i in range(3):
        rows = rows + rz[i].astype(F32)
    fin[...] = jnp.zeros((2, 8, H), F32)
    fin[0, 0:6, :] = rows[0:6]
    fin[1, 0:6, :] = rows[6:12]
    w_swap = send(fin.at[oc], cr, sem_z_s.at[3], sem_z_r.at[3], mate)

    for i in range(1, 16):
        slot = fg.at[ys[-(i // 4) % 4] * 4 + xr[-(i % 4) % 4]]
        copy(slot, slot, sem_t_s.at[22 + i], sem_t_r.at[22 + i], mate).wait_recv()
    late = sent_so_far()
    t_swap = send(fg, fgr, sem_t_s.at[38], sem_t_r.at[38], mate)

    def put_taps(cols, source):
        for n, rows, part in pieces():
            gh[rows, part] = source[n, :, 0:192]
        gk_ref[:, cols] = gh[0:TAPS, :]
        gg_ref[:, cols] = gh[TAPS:TAPS + 1, :]

    put_taps(half(c), fg)
    all_sent(late)
    gw_ref[:, half(c)] = fin[c][0:6]
    t_swap.wait_recv()
    put_taps(half(oc), fgr)
    w_swap.wait_recv()
    gw_ref[:, half(oc)] = cr[0:6, :]
    for n, (src, dst) in enumerate(((gw_ref, gw_hbm), (gk_ref, gk_hbm), (gg_ref, gg_hbm))):
        stores.append(pltpu.make_async_copy(src, dst, sem_out.at[2 + n]))
        stores[-1].start()

    all_sent(started)
    for item in stores:
        item.wait()


def deliver(*refs):
    sources, results, kept, flat, sems = refs[:5], refs[5:10], refs[10:15], refs[15], refs[16]
    loads = [pltpu.make_async_copy(a, b, sems.at[n]) for n, (a, b) in enumerate(zip(sources, kept))]
    stores = [pltpu.make_async_copy(a, b, sems.at[5 + n]) for n, (a, b) in enumerate(zip(kept[:4] + (flat,), results))]
    for item in loads:
        item.start()
    for first, then in zip(loads[:4], stores):
        first.wait()
        then.start()
    loads[4].wait()
    flat[...] = kept[4][0]
    stores[4].start()
    for item in stores:
        item.wait()


def on_device(inputs, lengths, kernel, norm_gain, weight, cotangent):
    vmem = pl.BlockSpec(memory_space=pltpu.VMEM)
    dma = pltpu.SemaphoreType.DMA
    scratch = [
        pltpu.SMEM((1,), jnp.int32),
        pltpu.VMEM((T, D), BF16),
        pltpu.VMEM((TAPS, D), F32),
        pltpu.VMEM((D,), F32),
        pltpu.VMEM((T, D), BF16),
        pltpu.VMEM((T, D), BF16),
        pltpu.VMEM((6, D), F32),
        pltpu.VMEM((TAPS, D), F32),
        pltpu.VMEM((1, D), F32),
        pltpu.VMEM((2, PAD, D), BF16),
        pltpu.VMEM((T + 2 * PAD, D), F32),
        pltpu.VMEM((T, D), F32),
        pltpu.VMEM((T, D), F32),
        pltpu.VMEM((T, LANES), F32),
        pltpu.VMEM((2 * T, D), BF16),
        pltpu.VMEM((3 * LANES, T), F32),
        pltpu.VMEM((192, T), F32),
        pltpu.VMEM((2, H, T), BF16),
        pltpu.VMEM((H, 4 * T), BF16),
        pltpu.VMEM((4 * T, H), BF16),
        pltpu.VMEM((D, H), BF16),
        pltpu.VMEM((4, 4, 48, CX), BF16),
        pltpu.VMEM((4, 4, 48, CY), BF16),
        pltpu.VMEM((3, 4, 48, CX), BF16),
        pltpu.VMEM((3, 4, 48, CY), BF16),
        pltpu.VMEM((4, 48, CX), BF16),
        pltpu.VMEM((4, 48, CY), BF16),
        pltpu.VMEM((3, 48, CX), BF16),
        pltpu.VMEM((3, 48, CY), BF16),
        pltpu.VMEM((56, H), F32),
        pltpu.VMEM((4, 16, H), BF16),
        pltpu.VMEM((3, 16, H), BF16),
        pltpu.VMEM((2, 8, H), F32),
        pltpu.VMEM((8, H), F32),
        pltpu.VMEM((2, T, D), F32),
        pltpu.VMEM((T, D), F32),
        pltpu.VMEM((2, T, H), BF16),
        pltpu.VMEM((T, H), BF16),
        pltpu.VMEM((T + 2 * PAD, D), F32),
        pltpu.VMEM((32, D), F32),
        pltpu.VMEM((32, H), F32),
        pltpu.VMEM((32, H), F32),
        pltpu.VMEM((16, 8, 256), F32),
        pltpu.VMEM((15, 8, 256), F32),
        pltpu.VMEM((8, 8, 256), F32),
        pltpu.VMEM((16, 8, 256), F32),
        pltpu.VMEM((16, 8, 256), F32),
        dma((4,)), dma((4,)),
        dma((14,)), dma((14,)),
        dma((12,)), dma((12,)),
        dma((12,)), dma((12,)),
        dma((8,)), dma((8,)),
        dma((39,)), dma((39,)),
        dma((10,)), dma((10,)),
        dma((6,)), dma((5,)),
        pltpu.SemaphoreType.REGULAR((3,)),
    ]
    hbm = pl.BlockSpec(memory_space=pl.ANY)
    shapes = (
        jax.ShapeDtypeStruct((T, D), BF16),
        jax.ShapeDtypeStruct((T, D), BF16),
        jax.ShapeDtypeStruct((6, D), F32),
        jax.ShapeDtypeStruct((TAPS, D), F32),
        jax.ShapeDtypeStruct((1, D), F32),
    )
    results = pl.pallas_call(
        fused,
        out_shape=shapes,
        in_specs=[hbm] * 6,
        out_specs=[hbm] * 5,
        scratch_shapes=scratch,
        compiler_params=pltpu.CompilerParams(
            collective_id=0, has_side_effects=True, vmem_limit_bytes=60 << 20
        ),
        name="conv_module",
    )(inputs[0], lengths, kernel, norm_gain, weight, cotangent[0])
    projected, grad_input, grad_weight, grad_kernel, grad_gain = pl.pallas_call(
        deliver,
        out_shape=shapes[:4] + (jax.ShapeDtypeStruct((D,), F32),),
        in_specs=[hbm] * 5,
        out_specs=[hbm] * 5,
        scratch_shapes=[pltpu.VMEM(r.shape, r.dtype) for r in shapes] + [pltpu.VMEM((D,), F32), dma((10,))],
        compiler_params=pltpu.CompilerParams(vmem_limit_bytes=60 << 20),
        name="deliver",
    )(*results)
    return (projected[None], grad_input[None], grad_weight, grad_kernel, grad_gain)


def solution(mesh):
    in_specs = (
        P("batch", "tm", None),
        P("batch"),
        P(),
        P(),
        P("batch", None),
        P("batch", "tm", None),
    )
    out_specs = (P("batch", "tm", None), P("batch", "tm", None), P(("batch", "tm"), None), P(), P())
    return jax.shard_map(
        on_device, mesh=mesh, in_specs=in_specs, out_specs=out_specs, check_vma=False
    )
```

```python
import jax
import jax.numpy as jnp
from jax import lax
from jax.experimental import pallas as pl
from jax.experimental.pallas import tpu as pltpu
from jax.sharding import PartitionSpec as P

F32, BF16 = jnp.float32, jnp.bfloat16
MESH = pl.DeviceIdType.MESH
D, T, H, TAPS = 1536, 128, 768, 31
PAD = 16
CX, CY = 256, 512
LANES = 128
CHUNKS = D // LANES


def lanes_of(k):
    return pl.ds(pl.multiple_of(k * LANES, LANES), LANES)


def fused(
    x_hbm, len_hbm, kern_hbm, gain_hbm, w_hbm, cot_hbm,
    proj_hbm, gin_hbm, gw_hbm, gk_hbm, gg_hbm,
    len_ref, x_ref, kern_ref, gain_ref, proj_ref, gin_ref, gw_ref, gk_ref, gg_ref,
    hx, xf, cv, ds, rs_sum, ab, tf, tp, at2, atm, ub, wb, px, py, rx, ry, s2x, s2y, r2x, r2y,
    facc, zs, rz, fin, cr, agp, agr, pj, pjr, cg, gkb, gcr, gh, gp, zr, xs, fg, fgr,
    sem_halo_s, sem_halo_r, sem_w_s, sem_w_r, sem_c_s, sem_c_r, sem_p_s, sem_p_r,
    sem_z_s, sem_z_r, sem_t_s, sem_t_r, sem_a_s, sem_a_r, sem_in, sem_out, sem_far,
):
    b = lax.axis_index("batch")
    t = lax.axis_index("tm")
    y, xl = lax.div(b, 2), lax.rem(b, 2)
    xh, z, c = lax.div(t, 16), lax.rem(lax.div(t, 2), 8), lax.rem(t, 2)
    x = xh * 2 + xl
    oc = 1 - c

    ys = [y] + [lax.rem(y + i, 4) for i in range(1, 4)]
    xr = [x] + [lax.rem(x + i, 4) for i in range(1, 4)]
    zr_ = [z] + [lax.rem(z + i, 8) for i in range(1, 8)]
    low, high = [lax.rem(v, 2) for v in xr], [lax.div(v, 2) for v in xr]
    blocks = [l * 2 + h for l, h in zip(low, high)]

    def dev(dy, dx, z_, c_):
        return (ys[dy] * 2 + low[dx], high[dx] * 16 + z_ * 2 + c_)

    def along_y(i):
        return dev(i, 0, z, c)

    def along_x(i):
        return dev(0, i, z, c)

    def along_z(i):
        return dev(0, 0, zr_[i], c)

    mate = dev(0, 0, z, oc)
    zp = lax.rem(z, 2)
    zh = lax.div(z, 2)
    zhs = [zh] + [lax.rem(zh + i, 4) for i in range(1, 4)]
    z_mate = z + 1 - 2 * zp
    across, diagonal = dev(0, 0, z_mate, c), dev(0, 0, z_mate, oc)
    before, after = (b, t - 1), (b, t + 1)

    q = blocks[0]

    def half(c_):
        return pl.ds(pl.multiple_of(c_ * H, H), H)

    def frames_of(c_):
        return pl.ds(pl.multiple_of(c_ * T, T), T)

    started = []

    def copy(src, dst, ss, rs, to):
        return pltpu.make_async_remote_copy(
            src_ref=src, dst_ref=dst, send_sem=ss, recv_sem=rs, device_id=to, device_id_type=MESH
        )

    def send(*args):
        item = copy(*args)
        item.start()
        started.append(item)
        return item

    def sent_so_far():
        items = list(started)
        started.clear()
        return items

    def all_sent(items):
        for item in items:
            item.wait_send()

    barrier = pltpu.get_barrier_semaphore()

    def greet(to):
        pl.semaphore_signal(barrier, inc=1, device_id=to, device_id_type=MESH)

    greet(mate)
    greet(diagonal)
    beside = [along_x(1), along_x(3), along_y(1), along_y(3), along_z(1), along_z(7)]
    for to in beside:
        greet(to)

    @pl.when(t > 0)
    def _():
        greet(before)

    @pl.when(t < 31)
    def _():
        greet(after)

    mine = zp * 2 + c
    w_own = pl.ds(pl.multiple_of((y * 2 + xl) * 192, 192), 192)
    loads = [
        pltpu.make_async_copy(src, dst, sem_in.at[n])
        for n, (src, dst) in enumerate((
            (x_hbm, x_ref), (cot_hbm.at[:, half(c)], ub.at[frames_of(mine)]), (w_hbm.at[:, half(c)], wb.at[w_own]),
            (kern_hbm, kern_ref), (gain_hbm, gain_ref), (len_hbm, len_ref),
        ))
    ]
    for item in loads:
        item.start()
    others = 8 + jnp.where(t > 0, 1, 0) + jnp.where(t < 31, 1, 0)
    pl.semaphore_wait(barrier, others)

    to_before = copy(x_hbm.at[pl.ds(0, PAD)], hx.at[1], sem_halo_s.at[0], sem_halo_r.at[1], before)
    to_after = copy(x_hbm.at[pl.ds(T - PAD, PAD)], hx.at[0], sem_halo_s.at[1], sem_halo_r.at[0], after)

    @pl.when(t > 0)
    def _():
        to_before.start()

    @pl.when(t < 31)
    def _():
        to_after.start()

    u_swaps = [
        send(cot_hbm.at[:, half(c_)], ub.at[frames_of(mine)], ss, rs, to)
        for c_, ss, rs, to in (
            (oc, sem_c_s.at[0], sem_c_r.at[0], mate),
            (c, sem_a_s.at[0], sem_a_r.at[0], across),
            (oc, sem_a_s.at[1], sem_a_r.at[1], diagonal),
        )
    ]

    def tell(n):
        for to in beside:
            pl.semaphore_signal(sem_far.at[n], inc=1, device_id=to, device_id_type=MESH)

    def told(n):
        pl.semaphore_wait(sem_far.at[n], len(beside))

    def rows_of(y_, xl_, side):
        return wb.at[pl.ds(pl.multiple_of((y_ * 2 + xl_) * 192 + side * 96, 96), 96)]

    y_up, y_down, y_far = ys[1], ys[3], ys[2]
    x_step = (1, 3)

    def push(here, n, to):
        send(here, here, sem_w_s.at[n], sem_w_r.at[n], to)

    def landed(here, n):
        copy(here, here, sem_w_s.at[n], sem_w_r.at[n], mate).wait_recv()

    def push_own(side, n, to):
        send(w_hbm.at[pl.ds(side * 96, 96), half(c)], rows_of(y, xl, side), sem_w_s.at[n], sem_w_r.at[n], to)

    push_own(0, 0, along_y(1))
    push_own(1, 3, along_y(3))
    for side in range(2):
        push_own(side, 6 + side, along_x(x_step[side]))
    push_own(1, 1, along_y(1))
    push_own(0, 2, along_y(3))

    tell(0)

    loads[5].wait()
    position = t * T + lax.broadcasted_iota(jnp.int32, (T, LANES), 0)
    live = jnp.where(position < len_ref[0], 1.0, 0.0).astype(F32)
    loads[0].wait()

    def mask_chunk(k, _):
        at_lanes = lanes_of(k)
        masked = x_ref[:, at_lanes].astype(F32) * live
        xf[PAD:PAD + T, at_lanes] = masked
        return 0

    lax.fori_loop(0, CHUNKS, mask_chunk, 0)

    for item in loads[3:5]:
        item.wait()

    def conv(source, taps, forward):
        count = source.shape[0] - 32
        total = None
        for r in range(8):
            part = None
            for k in range(4):
                offset = 8 * k + r
                tap = offset - 1 if forward else TAPS - offset
                if 0 <= tap < TAPS:
                    value = taps[tap:tap + 1] * source[8 * k:8 * k + count + 8]
                    part = value if part is None else part + value
            part = part[r:r + count]
            total = part if total is None else total + part
        return total

    def conv_chunk(start, count):
        def body(k, total):
            at_lanes = lanes_of(k)
            value = conv(xf[start:start + count + 32, at_lanes], kern_ref[:, at_lanes], True)
            value = value * live[start:start + count]
            cv[start:start + count, at_lanes] = value
            return total + value
        rs_sum[start:start + count, :] = lax.fori_loop(0, CHUNKS, body, jnp.zeros((count, LANES), F32))

    conv_chunk(PAD, T - 2 * PAD)

    def alive_halo(side, row, frame):
        frames = frame + lax.broadcasted_iota(jnp.int32, (PAD, D), 0)
        alive = jnp.where(frames < len_ref[0], 1.0, 0.0).astype(F32)
        xf[row:row + PAD, :] = hx[side].astype(F32) * alive

    @pl.when(t > 0)
    def _():
        to_after.wait_recv()
        alive_halo(0, 0, t * T - PAD)

    @pl.when(t == 0)
    def _():
        xf[0:PAD, :] = jnp.zeros((PAD, D), F32)

    @pl.when(t < 31)
    def _():
        to_before.wait_recv()
        alive_halo(1, PAD + T, t * T + T)

    @pl.when(t == 31)
    def _():
        xf[PAD + T:, :] = jnp.zeros((PAD, D), F32)

    conv_chunk(0, PAD)
    conv_chunk(T - PAD, PAD)

    told(0)
    tell(1)

    zero = jnp.zeros((T, LANES), F32)
    total = rs_sum[...]
    average = jnp.broadcast_to(jnp.sum(total, axis=1, keepdims=True) * (1.0 / D), (T, LANES))

    def variance_chunk(k, total):
        centred = cv[:, lanes_of(k)] - average
        return total + centred * centred

    total = lax.fori_loop(0, CHUNKS, variance_chunk, zero)
    variance = jnp.sum(total, axis=1, keepdims=True) * (1.0 / D)
    inv = jnp.broadcast_to(lax.rsqrt(variance + 1e-05), (T, LANES))

    def act_chunk(k, _):
        at_lanes = lanes_of(k)
        normed = (cv[:, at_lanes] - average) * inv
        scaled = normed * gain_ref[at_lanes][None]
        gate = 1.0 / (1.0 + jnp.exp(-scaled))
        act = scaled * gate
        cv[:, at_lanes] = normed
        ds[:, at_lanes] = gate * (1.0 + scaled * (1.0 - gate))
        ab[frames_of(c), at_lanes] = act.astype(BF16)
        tf[pl.ds(pl.multiple_of(lax.rem(k, 3) * LANES, LANES), LANES), :] = act.T
        return 0

    def pass_on(*pieces):
        for n, from_y, side in pieces:
            here = rows_of(from_y, xl, side)
            landed(here, n + side)
            push(here, 8 + n + side, along_x(x_step[side]))

    pass_on((0, y_down, 0), (2, y_up, 1))
    push(rows_of(y_down, xl, 0), 4, along_y(1))
    push(rows_of(y_up, xl, 1), 5, along_y(3))

    swaps, z_swaps, a_swaps = [], [], []
    for part in range(4):
        lax.fori_loop(part * 3, part * 3 + 3, act_chunk, 0)
        for parity in range(2):
            for g in range(16):
                tp[12 * g:12 * g + 12, :] = tf[24 * g + 12 * parity:24 * g + 12 * parity + 12, :]
            at2[parity, part * 192:part * 192 + 192, :] = tp[...].astype(BF16)
        rows = pl.ds(part * 192, 192)
        there = atm.at[rows, frames_of(mine)]
        z_swaps.append(send(at2.at[1 - zp, rows], there, sem_a_s.at[2 + part], sem_a_r.at[2 + part], across))
        swaps.append(send(at2.at[zp, rows], there, sem_c_s.at[1 + part], sem_c_r.at[1 + part], mate))
        atm[rows, frames_of(mine)] = at2[zp, part * 192:part * 192 + 192, :]
    here = ab.at[frames_of(c)]
    a_swaps.append(send(here, here, sem_c_s.at[5], sem_c_r.at[5], mate))

    told(1)
    tell(2)

    pass_on((2, y_up, 0), (0, y_down, 1))
    for side in range(2):
        here = rows_of(y_far, xl, side)
        landed(here, 4 + side)
        push(here, 12 + side, along_x(x_step[side]))

    loads[1].wait()
    loads[2].wait()
    for item in u_swaps:
        item.wait_recv()
    for slot in range(4):
        first_frame = (xh * 16 + (z - zp) * 2 + slot) * T
        alive = jnp.where(position - t * T + first_frame < len_ref[0], 1.0, 0.0).astype(F32)

        def mask_upstream(k, _):
            rows, at_lanes = slice(slot * T, slot * T + T), lanes_of(k)
            ub[rows, at_lanes] = (ub[rows, at_lanes].astype(F32) * alive).astype(BF16)
            return 0

        lax.fori_loop(0, H // LANES, mask_upstream, 0)

    chip_rows = pl.ds(pl.multiple_of(zp * 2 * T, 2 * T), 2 * T)
    ag_swaps = []

    def act_grad(n, from_y):
        for side in range(2):
            landed(rows_of(from_y, 1 - xl, side), n + side)
        cols = pl.ds(pl.multiple_of(from_y * 384, 384), 384)
        value = lax.dot_general(
            ub[chip_rows, :], wb[cols, :], (((1,), (1,)), ((), ())), preferred_element_type=F32
        )
        agp[0, :, cols] = value[:T]
        agp[1, :, cols] = value[T:]
        k = len(ag_swaps)
        ag_swaps.append(
            send(agp.at[oc, :, cols], agr.at[:, cols], sem_c_s.at[6 + k], sem_c_r.at[6 + k], mate)
        )

    act_grad(6, y)

    theirs = (1 - zp) * 2 + c
    for part in range(4):
        z_swaps[part].wait_recv()
        here = atm.at[pl.ds(part * 192, 192), frames_of(theirs)]
        swaps.append(send(here, here, sem_a_s.at[6 + part], sem_a_r.at[6 + part], mate))

    told(2)

    for item in swaps:
        item.wait_recv()

    def partial(n, start, width):
        rows = pl.ds(pl.multiple_of(n * 192, 192), 192)
        value = jnp.dot(atm[rows, :], ub[:, start:start + width], preferred_element_type=F32)
        return value.reshape(4, 48, width).astype(BF16)

    y_first = []
    for i in (2, 1, 3, 0):
        to_y = ys[i]
        py[to_y] = partial(to_y, CX, CY)
        if i:
            y_first.append(send(py.at[to_y], ry.at[i - 1], sem_p_s.at[2 + i], sem_p_r.at[2 + i], along_y(i)))

    def partial_x(n, _):
        px[n] = partial(n, 0, CX)
        return 0

    lax.fori_loop(0, 4, partial_x, 0)
    x_first = [
        send(px.at[:, blocks[i]], rx.at[i - 1], sem_p_s.at[i - 1], sem_p_r.at[i - 1], along_x(i))
        for i in (2, 1, 3)
    ]

    act_grad(8, y_down)
    act_grad(10, y_up)
    act_grad(12, y_far)

    for item in a_swaps:
        item.wait_recv()

    def project_chunk(n, _):
        cols = pl.ds(pl.multiple_of(n * 256, 256), 256)
        value = jnp.dot(ab[...], wb[:, cols], preferred_element_type=F32).astype(BF16)
        pj[0, :, cols] = value[:T]
        pj[1, :, cols] = value[T:]
        return 0

    lax.fori_loop(0, 3, project_chunk, 0)
    pj_swap = send(pj.at[oc], pjr, sem_c_s.at[10], sem_c_r.at[10], mate)
    proj_ref[:, half(c)] = pj[c]

    for item in ag_swaps:
        item.wait_recv()

    def back_chunk(k, sums):
        at_lanes = lanes_of(k)
        normed = cv[:, at_lanes]
        scaled_grad = (agp[c, :, at_lanes] + agr[:, at_lanes]) * ds[:, at_lanes]
        gkb[TAPS:TAPS + 1, at_lanes] = jnp.sum(scaled_grad * normed, axis=0, keepdims=True)
        normed_grad = scaled_grad * gain_ref[at_lanes][None]
        ds[:, at_lanes] = normed_grad
        return (sums[0] + normed_grad, sums[1] + normed_grad * normed)

    sums = lax.fori_loop(0, CHUNKS, back_chunk, (zero, zero))
    first, second = [
        jnp.broadcast_to(jnp.sum(s, axis=1, keepdims=True) * (1.0 / D), (T, LANES)) for s in sums
    ]
    inv_live = inv * live

    def taps_chunk(k, _):
        at_lanes = lanes_of(k)
        source = xf[:, at_lanes]
        grad = inv_live * (ds[:, at_lanes] - first - cv[:, at_lanes] * second)
        cg[PAD:PAD + T, at_lanes] = grad
        for r in range(8):
            shifted = source[r:r + T + 24]
            for j in range(4):
                tap = 8 * j + r - 1
                if 0 <= tap < TAPS:
                    gkb[tap:tap + 1, at_lanes] = jnp.sum(grad * shifted[8 * j:8 * j + T], axis=0, keepdims=True)
        return 0

    lax.fori_loop(oc * 6, oc * 6 + 6, taps_chunk, 0)
    gk_swap = send(gkb.at[:, half(oc)], gcr, sem_t_s.at[0], sem_t_r.at[0], mate)
    lax.fori_loop(c * 6, c * 6 + 6, taps_chunk, 0)
    g_before = copy(cg.at[pl.ds(PAD, PAD)], cg.at[pl.ds(PAD + T, PAD)], sem_halo_s.at[2], sem_halo_r.at[3], before)
    g_after = copy(cg.at[pl.ds(T, PAD)], cg.at[pl.ds(0, PAD)], sem_halo_s.at[3], sem_halo_r.at[2], after)

    @pl.when(t > 0)
    def _():
        g_before.start()

    @pl.when(t < 31)
    def _():
        g_after.start()

    def pieces():
        for n in range(16):
            yield n, slice(n // 4 * 8, n // 4 * 8 + 8), slice(n % 4 * 192, n % 4 * 192 + 192)

    plane = (10, 9, 11, 6, 14, 2, 8, 5, 7, 13, 15, 1, 3, 4, 12)
    line = (4, 3, 5, 2, 6, 1, 7)
    here = y * 4 + x

    def in_plane(i):
        return ys[i // 4] * 4 + xr[i % 4], dev(i // 4, i % 4, z, c)

    early = sent_so_far()
    gk_swap.wait_recv()
    gh[...] = gkb[:, half(c)] + gcr[...]
    gp[...] = jnp.zeros((16, 8, 256), F32)
    for n, rows, cols in pieces():
        gp[n, :, 0:192] = gh[rows, cols]
    t_plane = []
    for i in plane:
        n, to = in_plane(i)
        t_plane.append(send(gp.at[n], zr.at[i - 1], sem_t_s.at[i], sem_t_r.at[i], to))

    def add(first, own, came, out):
        for item in first:
            item.wait_recv()

        def body(n, _):
            value = own(n).astype(F32)
            for i in range(3):
                value = value + came[i, n].astype(F32)
            out[n] = value.astype(BF16)
            return 0

        lax.fori_loop(0, 4, body, 0)

    add(x_first, lambda n: px[n, q], rx, s2x)
    x_second = [
        send(s2x.at[ys[i]], r2x.at[i - 1], sem_p_s.at[5 + i], sem_p_r.at[5 + i], along_y(i))
        for i in (2, 1, 3)
    ]
    add(y_first, lambda n: py[y, n], ry, s2y)
    y_second = [
        send(s2y.at[blocks[i]], r2y.at[i - 1], sem_p_s.at[8 + i], sem_p_r.at[8 + i], along_x(i))
        for i in (2, 1, 3)
    ]

    @pl.when(t > 0)
    def _():
        g_after.wait_recv()

    @pl.when(t == 0)
    def _():
        cg[0:PAD, :] = jnp.zeros((PAD, D), F32)

    @pl.when(t < 31)
    def _():
        g_before.wait_recv()

    @pl.when(t == 31)
    def _():
        cg[PAD + T:, :] = jnp.zeros((PAD, D), F32)

    def input_chunk(k, _):
        at_lanes = lanes_of(k)
        value = conv(cg[:, at_lanes], kern_ref[:, at_lanes], False) * live
        gin_ref[:, at_lanes] = value.astype(BF16)
        return 0

    all_sent(early)

    for item in t_plane:
        item.wait_recv()
    total = gp[here]
    for i in range(15):
        total = total + zr[i]
    xs[z] = total
    for i in line:
        slot = xs.at[z]
        send(slot, slot, sem_t_s.at[15 + i], sem_t_r.at[15 + i], along_z(i))

    for item in x_second + y_second:
        item.wait_recv()
    left, right = s2x[y].astype(F32), s2y[q].astype(F32)
    for i in range(3):
        left = left + r2x[i].astype(F32)
        right = right + r2y[i].astype(F32)
    facc[0:48, 0:CX] = left
    facc[0:48, CX:H] = right
    facc[48:56, :] = jnp.zeros((8, H), F32)
    for n in range(4):
        zs[n] = facc[12 * n:12 * n + 16, :].astype(BF16)
    w_z = [
        send(zs.at[zhs[i]], rz.at[i - 1], sem_z_s.at[i - 1], sem_z_r.at[i - 1], along_z(2 * i))
        for i in (2, 1, 3)
    ]

    lax.fori_loop(0, CHUNKS, input_chunk, 0)
    for i in range(1, 8):
        slot = xs.at[zr_[8 - i]]
        copy(slot, slot, sem_t_s.at[15 + i], sem_t_r.at[15 + i], mate).wait_recv()
    total = xs[0]
    for i in range(1, 8):
        total = total + xs[i]
    fg[here] = total
    middle = sent_so_far()
    for i in plane:
        send(fg.at[here], fg.at[here], sem_t_s.at[22 + i], sem_t_r.at[22 + i], in_plane(i)[1])

    stores = [pltpu.make_async_copy(gin_ref, gin_hbm, sem_out.at[0])]
    stores[0].start()
    all_sent(middle)

    @pl.when(t > 0)
    def _():
        to_before.wait_send()
        g_before.wait_send()

    @pl.when(t < 31)
    def _():
        to_after.wait_send()
        g_after.wait_send()

    pj_swap.wait_recv()
    proj_ref[:, half(oc)] = pjr[...]
    stores.append(pltpu.make_async_copy(proj_ref, proj_hbm, sem_out.at[1]))
    stores[1].start()

    for item in w_z:
        item.wait_recv()
    rows = zs[zh].astype(F32)
    for i in range(3):
        rows = rows + rz[i].astype(F32)
    fin[...] = jnp.zeros((2, 8, H), F32)
    fin[0, 0:6, :] = rows[0:6]
    fin[1, 0:6, :] = rows[6:12]
    w_swap = send(fin.at[oc], cr, sem_z_s.at[3], sem_z_r.at[3], mate)

    for i in range(1, 16):
        slot = fg.at[ys[-(i // 4) % 4] * 4 + xr[-(i % 4) % 4]]
        copy(slot, slot, sem_t_s.at[22 + i], sem_t_r.at[22 + i], mate).wait_recv()
    late = sent_so_far()
    t_swap = send(fg, fgr, sem_t_s.at[38], sem_t_r.at[38], mate)

    def put_taps(cols, source):
        for n, rows, part in pieces():
            gh[rows, part] = source[n, :, 0:192]
        gk_ref[:, cols] = gh[0:TAPS, :]
        gg_ref[:, cols] = gh[TAPS:TAPS + 1, :]

    put_taps(half(c), fg)
    all_sent(late)
    gw_ref[:, half(c)] = fin[c][0:6]
    w_swap.wait_recv()
    gw_ref[:, half(oc)] = cr[0:6, :]
    t_swap.wait_recv()
    put_taps(half(oc), fgr)
    for n, (src, dst) in enumerate(((gw_ref, gw_hbm), (gk_ref, gk_hbm), (gg_ref, gg_hbm))):
        stores.append(pltpu.make_async_copy(src, dst, sem_out.at[2 + n]))
        stores[-1].start()

    all_sent(started)
    for item in stores:
        item.wait()


def deliver(*refs):
    sources, results, kept, flat, sems = refs[:5], refs[5:10], refs[10:15], refs[15], refs[16]
    loads = [pltpu.make_async_copy(a, b, sems.at[n]) for n, (a, b) in enumerate(zip(sources, kept))]
    stores = [pltpu.make_async_copy(a, b, sems.at[5 + n]) for n, (a, b) in enumerate(zip(kept[:4] + (flat,), results))]
    for item in loads:
        item.start()
    for first, then in zip(loads[:4], stores):
        first.wait()
        then.start()
    loads[4].wait()
    flat[...] = kept[4][0]
    stores[4].start()
    for item in stores:
        item.wait()


def on_device(inputs, lengths, kernel, norm_gain, weight, cotangent):
    vmem = pl.BlockSpec(memory_space=pltpu.VMEM)
    dma = pltpu.SemaphoreType.DMA
    scratch = [
        pltpu.SMEM((1,), jnp.int32),
        pltpu.VMEM((T, D), BF16),
        pltpu.VMEM((TAPS, D), F32),
        pltpu.VMEM((D,), F32),
        pltpu.VMEM((T, D), BF16),
        pltpu.VMEM((T, D), BF16),
        pltpu.VMEM((6, D), F32),
        pltpu.VMEM((TAPS, D), F32),
        pltpu.VMEM((1, D), F32),
        pltpu.VMEM((2, PAD, D), BF16),
        pltpu.VMEM((T + 2 * PAD, D), F32),
        pltpu.VMEM((T, D), F32),
        pltpu.VMEM((T, D), F32),
        pltpu.VMEM((T, LANES), F32),
        pltpu.VMEM((2 * T, D), BF16),
        pltpu.VMEM((3 * LANES, T), F32),
        pltpu.VMEM((192, T), F32),
        pltpu.VMEM((2, H, T), BF16),
        pltpu.VMEM((H, 4 * T), BF16),
        pltpu.VMEM((4 * T, H), BF16),
        pltpu.VMEM((D, H), BF16),
        pltpu.VMEM((4, 4, 48, CX), BF16),
        pltpu.VMEM((4, 4, 48, CY), BF16),
        pltpu.VMEM((3, 4, 48, CX), BF16),
        pltpu.VMEM((3, 4, 48, CY), BF16),
        pltpu.VMEM((4, 48, CX), BF16),
        pltpu.VMEM((4, 48, CY), BF16),
        pltpu.VMEM((3, 48, CX), BF16),
        pltpu.VMEM((3, 48, CY), BF16),
        pltpu.VMEM((56, H), F32),
        pltpu.VMEM((4, 16, H), BF16),
        pltpu.VMEM((3, 16, H), BF16),
        pltpu.VMEM((2, 8, H), F32),
        pltpu.VMEM((8, H), F32),
        pltpu.VMEM((2, T, D), F32),
        pltpu.VMEM((T, D), F32),
        pltpu.VMEM((2, T, H), BF16),
        pltpu.VMEM((T, H), BF16),
        pltpu.VMEM((T + 2 * PAD, D), F32),
        pltpu.VMEM((32, D), F32),
        pltpu.VMEM((32, H), F32),
        pltpu.VMEM((32, H), F32),
        pltpu.VMEM((16, 8, 256), F32),
        pltpu.VMEM((15, 8, 256), F32),
        pltpu.VMEM((8, 8, 256), F32),
        pltpu.VMEM((16, 8, 256), F32),
        pltpu.VMEM((16, 8, 256), F32),
        dma((4,)), dma((4,)),
        dma((14,)), dma((14,)),
        dma((12,)), dma((12,)),
        dma((12,)), dma((12,)),
        dma((8,)), dma((8,)),
        dma((39,)), dma((39,)),
        dma((10,)), dma((10,)),
        dma((6,)), dma((5,)),
        pltpu.SemaphoreType.REGULAR((3,)),
    ]
    hbm = pl.BlockSpec(memory_space=pl.ANY)
    shapes = (
        jax.ShapeDtypeStruct((T, D), BF16),
        jax.ShapeDtypeStruct((T, D), BF16),
        jax.ShapeDtypeStruct((6, D), F32),
        jax.ShapeDtypeStruct((TAPS, D), F32),
        jax.ShapeDtypeStruct((1, D), F32),
    )
    results = pl.pallas_call(
        fused,
        out_shape=shapes,
        in_specs=[hbm] * 6,
        out_specs=[hbm] * 5,
        scratch_shapes=scratch,
        compiler_params=pltpu.CompilerParams(
            collective_id=0, has_side_effects=True, vmem_limit_bytes=60 << 20
        ),
        name="conv_module",
    )(inputs[0], lengths, kernel, norm_gain, weight, cotangent[0])
    projected, grad_input, grad_weight, grad_kernel, grad_gain = pl.pallas_call(
        deliver,
        out_shape=shapes[:4] + (jax.ShapeDtypeStruct((D,), F32),),
        in_specs=[hbm] * 5,
        out_specs=[hbm] * 5,
        scratch_shapes=[pltpu.VMEM(r.shape, r.dtype) for r in shapes] + [pltpu.VMEM((D,), F32), dma((10,))],
        compiler_params=pltpu.CompilerParams(vmem_limit_bytes=60 << 20),
        name="deliver",
    )(*results)
    return (projected[None], grad_input[None], grad_weight, grad_kernel, grad_gain)


def solution(mesh):
    in_specs = (
        P("batch", "tm", None),
        P("batch"),
        P(),
        P(),
        P("batch", None),
        P("batch", "tm", None),
    )
    out_specs = (P("batch", "tm", None), P("batch", "tm", None), P(("batch", "tm"), None), P(), P())
    return jax.shard_map(
        on_device, mesh=mesh, in_specs=in_specs, out_specs=out_specs, check_vma=False
    )
```

```python
import jax
import jax.numpy as jnp
from jax import lax
from jax.experimental import pallas as pl
from jax.experimental.pallas import tpu as pltpu
from jax.sharding import PartitionSpec as P

F32, BF16 = jnp.float32, jnp.bfloat16
MESH = pl.DeviceIdType.MESH
D, T, H, TAPS = 1536, 128, 768, 31
PAD = 16
CX, CY = 256, 512
LANES = 128
CHUNKS = D // LANES


def lanes_of(k):
    return pl.ds(pl.multiple_of(k * LANES, LANES), LANES)


def fused(
    x_hbm, len_hbm, kern_hbm, gain_hbm, w_hbm, cot_hbm,
    proj_hbm, gin_hbm, gw_hbm, gk_hbm, gg_hbm,
    len_ref, x_ref, kern_ref, gain_ref, proj_ref, gin_ref, gw_ref, gk_ref, gg_ref,
    hx, xf, cv, ds, rs_sum, ab, tf, tp, at2, atm, ub, wb, px, py, rx, ry, s2x, s2y, r2x, r2y,
    facc, zs, rz, fin, cr, agp, agr, pj, pjr, cg, gkb, gcr, gh, gp, zr, xs, fg, fgr,
    sem_halo_s, sem_halo_r, sem_w_s, sem_w_r, sem_c_s, sem_c_r, sem_p_s, sem_p_r,
    sem_z_s, sem_z_r, sem_t_s, sem_t_r, sem_a_s, sem_a_r, sem_in, sem_out, sem_far,
):
    b = lax.axis_index("batch")
    t = lax.axis_index("tm")
    y, xl = lax.div(b, 2), lax.rem(b, 2)
    xh, z, c = lax.div(t, 16), lax.rem(lax.div(t, 2), 8), lax.rem(t, 2)
    x = xh * 2 + xl
    oc = 1 - c

    ys = [y] + [lax.rem(y + i, 4) for i in range(1, 4)]
    xr = [x] + [lax.rem(x + i, 4) for i in range(1, 4)]
    zr_ = [z] + [lax.rem(z + i, 8) for i in range(1, 8)]
    low, high = [lax.rem(v, 2) for v in xr], [lax.div(v, 2) for v in xr]
    blocks = [l * 2 + h for l, h in zip(low, high)]

    def dev(dy, dx, z_, c_):
        return (ys[dy] * 2 + low[dx], high[dx] * 16 + z_ * 2 + c_)

    def along_y(i):
        return dev(i, 0, z, c)

    def along_x(i):
        return dev(0, i, z, c)

    def along_z(i):
        return dev(0, 0, zr_[i], c)

    mate = dev(0, 0, z, oc)
    zp = lax.rem(z, 2)
    zh = lax.div(z, 2)
    zhs = [zh] + [lax.rem(zh + i, 4) for i in range(1, 4)]
    z_mate = z + 1 - 2 * zp
    across, diagonal = dev(0, 0, z_mate, c), dev(0, 0, z_mate, oc)
    before, after = (b, t - 1), (b, t + 1)

    q = blocks[0]

    def half(c_):
        return pl.ds(pl.multiple_of(c_ * H, H), H)

    def frames_of(c_):
        return pl.ds(pl.multiple_of(c_ * T, T), T)

    started = []

    def copy(src, dst, ss, rs, to):
        return pltpu.make_async_remote_copy(
            src_ref=src, dst_ref=dst, send_sem=ss, recv_sem=rs, device_id=to, device_id_type=MESH
        )

    def send(*args):
        item = copy(*args)
        item.start()
        started.append(item)
        return item

    def sent_so_far():
        items = list(started)
        started.clear()
        return items

    def all_sent(items):
        for item in items:
            item.wait_send()

    barrier = pltpu.get_barrier_semaphore()

    def greet(to):
        pl.semaphore_signal(barrier, inc=1, device_id=to, device_id_type=MESH)

    greet(mate)
    greet(diagonal)
    beside = [along_x(1), along_x(3), along_y(1), along_y(3), along_z(1), along_z(7)]
    for to in beside:
        greet(to)

    @pl.when(t > 0)
    def _():
        greet(before)

    @pl.when(t < 31)
    def _():
        greet(after)

    mine = zp * 2 + c
    w_own = pl.ds(pl.multiple_of((y * 2 + xl) * 192, 192), 192)
    loads = [
        pltpu.make_async_copy(src, dst, sem_in.at[n])
        for n, (src, dst) in enumerate((
            (x_hbm, x_ref), (cot_hbm.at[:, half(c)], ub.at[frames_of(mine)]), (w_hbm.at[:, half(c)], wb.at[w_own]),
            (kern_hbm, kern_ref), (gain_hbm, gain_ref), (len_hbm, len_ref),
        ))
    ]
    for item in loads:
        item.start()
    others = 8 + jnp.where(t > 0, 1, 0) + jnp.where(t < 31, 1, 0)
    pl.semaphore_wait(barrier, others)

    to_before = copy(x_hbm.at[pl.ds(0, PAD)], hx.at[1], sem_halo_s.at[0], sem_halo_r.at[1], before)
    to_after = copy(x_hbm.at[pl.ds(T - PAD, PAD)], hx.at[0], sem_halo_s.at[1], sem_halo_r.at[0], after)

    @pl.when(t > 0)
    def _():
        to_before.start()

    @pl.when(t < 31)
    def _():
        to_after.start()

    u_swaps = [
        send(cot_hbm.at[:, half(c_)], ub.at[frames_of(mine)], ss, rs, to)
        for c_, ss, rs, to in (
            (oc, sem_c_s.at[0], sem_c_r.at[0], mate),
            (c, sem_a_s.at[0], sem_a_r.at[0], across),
            (oc, sem_a_s.at[1], sem_a_r.at[1], diagonal),
        )
    ]

    def tell(n):
        for to in beside:
            pl.semaphore_signal(sem_far.at[n], inc=1, device_id=to, device_id_type=MESH)

    def told(n):
        pl.semaphore_wait(sem_far.at[n], len(beside))

    def rows_of(y_, xl_, side):
        return wb.at[pl.ds(pl.multiple_of((y_ * 2 + xl_) * 192 + side * 96, 96), 96)]

    y_up, y_down, y_far = ys[1], ys[3], ys[2]
    x_step = (1, 3)

    def push(here, n, to):
        send(here, here, sem_w_s.at[n], sem_w_r.at[n], to)

    def landed(here, n):
        copy(here, here, sem_w_s.at[n], sem_w_r.at[n], mate).wait_recv()

    def push_own(side, n, to):
        send(w_hbm.at[pl.ds(side * 96, 96), half(c)], rows_of(y, xl, side), sem_w_s.at[n], sem_w_r.at[n], to)

    push_own(0, 0, along_y(1))
    push_own(1, 3, along_y(3))
    for side in range(2):
        push_own(side, 6 + side, along_x(x_step[side]))
    push_own(1, 1, along_y(1))
    push_own(0, 2, along_y(3))

    tell(0)

    loads[5].wait()
    position = t * T + lax.broadcasted_iota(jnp.int32, (T, LANES), 0)
    live = jnp.where(position < len_ref[0], 1.0, 0.0).astype(F32)
    loads[0].wait()

    def mask_chunk(k, _):
        at_lanes = lanes_of(k)
        masked = x_ref[:, at_lanes].astype(F32) * live
        xf[PAD:PAD + T, at_lanes] = masked
        return 0

    lax.fori_loop(0, CHUNKS, mask_chunk, 0)

    for item in loads[3:5]:
        item.wait()

    def conv(source, taps, forward):
        count = source.shape[0] - 32
        total = None
        for r in range(8):
            part = None
            for k in range(4):
                offset = 8 * k + r
                tap = offset - 1 if forward else TAPS - offset
                if 0 <= tap < TAPS:
                    value = taps[tap:tap + 1] * source[8 * k:8 * k + count + 8]
                    part = value if part is None else part + value
            part = part[r:r + count]
            total = part if total is None else total + part
        return total

    def conv_chunk(start, count):
        def body(k, total):
            at_lanes = lanes_of(k)
            value = conv(xf[start:start + count + 32, at_lanes], kern_ref[:, at_lanes], True)
            value = value * live[start:start + count]
            cv[start:start + count, at_lanes] = value
            return total + value
        rs_sum[start:start + count, :] = lax.fori_loop(0, CHUNKS, body, jnp.zeros((count, LANES), F32))

    conv_chunk(PAD, T - 2 * PAD)

    def alive_halo(side, row, frame):
        frames = frame + lax.broadcasted_iota(jnp.int32, (PAD, D), 0)
        alive = jnp.where(frames < len_ref[0], 1.0, 0.0).astype(F32)
        xf[row:row + PAD, :] = hx[side].astype(F32) * alive

    @pl.when(t > 0)
    def _():
        to_after.wait_recv()
        alive_halo(0, 0, t * T - PAD)

    @pl.when(t == 0)
    def _():
        xf[0:PAD, :] = jnp.zeros((PAD, D), F32)

    @pl.when(t < 31)
    def _():
        to_before.wait_recv()
        alive_halo(1, PAD + T, t * T + T)

    @pl.when(t == 31)
    def _():
        xf[PAD + T:, :] = jnp.zeros((PAD, D), F32)

    conv_chunk(0, PAD)
    conv_chunk(T - PAD, PAD)

    told(0)
    tell(1)

    zero = jnp.zeros((T, LANES), F32)
    total = rs_sum[...]
    average = jnp.broadcast_to(jnp.sum(total, axis=1, keepdims=True) * (1.0 / D), (T, LANES))

    def variance_chunk(k, total):
        centred = cv[:, lanes_of(k)] - average
        return total + centred * centred

    total = lax.fori_loop(0, CHUNKS, variance_chunk, zero)
    variance = jnp.sum(total, axis=1, keepdims=True) * (1.0 / D)
    inv = jnp.broadcast_to(lax.rsqrt(variance + 1e-05), (T, LANES))

    def act_chunk(k, _):
        at_lanes = lanes_of(k)
        normed = (cv[:, at_lanes] - average) * inv
        scaled = normed * gain_ref[at_lanes][None]
        gate = 1.0 / (1.0 + jnp.exp(-scaled))
        act = scaled * gate
        cv[:, at_lanes] = normed
        ds[:, at_lanes] = gate * (1.0 + scaled * (1.0 - gate))
        ab[frames_of(c), at_lanes] = act.astype(BF16)
        tf[pl.ds(pl.multiple_of(lax.rem(k, 3) * LANES, LANES), LANES), :] = act.T
        return 0

    def pass_on(*pieces):
        for n, from_y, side in pieces:
            here = rows_of(from_y, xl, side)
            landed(here, n + side)
            push(here, 8 + n + side, along_x(x_step[side]))

    pass_on((0, y_down, 0), (2, y_up, 1))
    push(rows_of(y_down, xl, 0), 4, along_y(1))
    push(rows_of(y_up, xl, 1), 5, along_y(3))

    swaps, z_swaps, a_swaps = [], [], []
    for part in range(4):
        lax.fori_loop(part * 3, part * 3 + 3, act_chunk, 0)
        for parity in range(2):
            for g in range(16):
                tp[12 * g:12 * g + 12, :] = tf[24 * g + 12 * parity:24 * g + 12 * parity + 12, :]
            at2[parity, part * 192:part * 192 + 192, :] = tp[...].astype(BF16)
        rows = pl.ds(part * 192, 192)
        there = atm.at[rows, frames_of(mine)]
        z_swaps.append(send(at2.at[1 - zp, rows], there, sem_a_s.at[2 + part], sem_a_r.at[2 + part], across))
        swaps.append(send(at2.at[zp, rows], there, sem_c_s.at[1 + part], sem_c_r.at[1 + part], mate))
        atm[rows, frames_of(mine)] = at2[zp, part * 192:part * 192 + 192, :]
    here = ab.at[frames_of(c)]
    a_swaps.append(send(here, here, sem_c_s.at[5], sem_c_r.at[5], mate))

    told(1)
    tell(2)

    pass_on((2, y_up, 0), (0, y_down, 1))
    for side in range(2):
        here = rows_of(y_far, xl, side)
        landed(here, 4 + side)
        push(here, 12 + side, along_x(x_step[side]))

    loads[1].wait()
    loads[2].wait()
    for item in u_swaps:
        item.wait_recv()
    for slot in range(4):
        first_frame = (xh * 16 + (z - zp) * 2 + slot) * T
        alive = jnp.where(position - t * T + first_frame < len_ref[0], 1.0, 0.0).astype(F32)

        def mask_upstream(k, _):
            rows, at_lanes = slice(slot * T, slot * T + T), lanes_of(k)
            ub[rows, at_lanes] = (ub[rows, at_lanes].astype(F32) * alive).astype(BF16)
            return 0

        lax.fori_loop(0, H // LANES, mask_upstream, 0)

    chip_rows = pl.ds(pl.multiple_of(zp * 2 * T, 2 * T), 2 * T)
    ag_swaps = []

    def act_grad(n, from_y):
        for side in range(2):
            landed(rows_of(from_y, 1 - xl, side), n + side)
        cols = pl.ds(pl.multiple_of(from_y * 384, 384), 384)
        value = lax.dot_general(
            ub[chip_rows, :], wb[cols, :], (((1,), (1,)), ((), ())), preferred_element_type=F32
        )
        agp[0, :, cols] = value[:T]
        agp[1, :, cols] = value[T:]
        k = len(ag_swaps)
        ag_swaps.append(
            send(agp.at[oc, :, cols], agr.at[:, cols], sem_c_s.at[6 + k], sem_c_r.at[6 + k], mate)
        )

    act_grad(6, y)

    theirs = (1 - zp) * 2 + c
    for part in range(4):
        z_swaps[part].wait_recv()
        here = atm.at[pl.ds(part * 192, 192), frames_of(theirs)]
        swaps.append(send(here, here, sem_a_s.at[6 + part], sem_a_r.at[6 + part], mate))

    told(2)

    for item in swaps:
        item.wait_recv()

    def partial(n, start, width):
        rows = pl.ds(pl.multiple_of(n * 192, 192), 192)
        value = jnp.dot(atm[rows, :], ub[:, start:start + width], preferred_element_type=F32)
        return value.reshape(4, 48, width).astype(BF16)

    y_first = []
    for i in (2, 1, 3, 0):
        to_y = ys[i]
        py[to_y] = partial(to_y, CX, CY)
        if i:
            y_first.append(send(py.at[to_y], ry.at[i - 1], sem_p_s.at[2 + i], sem_p_r.at[2 + i], along_y(i)))

    act_grad(8, y_down)
    act_grad(10, y_up)
    act_grad(12, y_far)

    def partial_x(n, _):
        px[n] = partial(n, 0, CX)
        return 0

    lax.fori_loop(0, 4, partial_x, 0)
    x_first = [
        send(px.at[:, blocks[i]], rx.at[i - 1], sem_p_s.at[i - 1], sem_p_r.at[i - 1], along_x(i))
        for i in (2, 1, 3)
    ]

    for item in a_swaps:
        item.wait_recv()

    def project_chunk(n, _):
        cols = pl.ds(pl.multiple_of(n * 256, 256), 256)
        value = jnp.dot(ab[...], wb[:, cols], preferred_element_type=F32).astype(BF16)
        pj[0, :, cols] = value[:T]
        pj[1, :, cols] = value[T:]
        return 0

    lax.fori_loop(0, 3, project_chunk, 0)
    pj_swap = send(pj.at[oc], pjr, sem_c_s.at[10], sem_c_r.at[10], mate)
    proj_ref[:, half(c)] = pj[c]

    for item in ag_swaps:
        item.wait_recv()

    def back_chunk(k, sums):
        at_lanes = lanes_of(k)
        normed = cv[:, at_lanes]
        scaled_grad = (agp[c, :, at_lanes] + agr[:, at_lanes]) * ds[:, at_lanes]
        gkb[TAPS:TAPS + 1, at_lanes] = jnp.sum(scaled_grad * normed, axis=0, keepdims=True)
        normed_grad = scaled_grad * gain_ref[at_lanes][None]
        ds[:, at_lanes] = normed_grad
        return (sums[0] + normed_grad, sums[1] + normed_grad * normed)

    sums = lax.fori_loop(0, CHUNKS, back_chunk, (zero, zero))
    first, second = [
        jnp.broadcast_to(jnp.sum(s, axis=1, keepdims=True) * (1.0 / D), (T, LANES)) for s in sums
    ]
    inv_live = inv * live

    def taps_chunk(k, _):
        at_lanes = lanes_of(k)
        source = xf[:, at_lanes]
        grad = inv_live * (ds[:, at_lanes] - first - cv[:, at_lanes] * second)
        cg[PAD:PAD + T, at_lanes] = grad
        for r in range(8):
            shifted = source[r:r + T + 24]
            for j in range(4):
                tap = 8 * j + r - 1
                if 0 <= tap < TAPS:
                    gkb[tap:tap + 1, at_lanes] = jnp.sum(grad * shifted[8 * j:8 * j + T], axis=0, keepdims=True)
        return 0

    lax.fori_loop(oc * 6, oc * 6 + 6, taps_chunk, 0)
    gk_swap = send(gkb.at[:, half(oc)], gcr, sem_t_s.at[0], sem_t_r.at[0], mate)
    lax.fori_loop(c * 6, c * 6 + 6, taps_chunk, 0)
    g_before = copy(cg.at[pl.ds(PAD, PAD)], cg.at[pl.ds(PAD + T, PAD)], sem_halo_s.at[2], sem_halo_r.at[3], before)
    g_after = copy(cg.at[pl.ds(T, PAD)], cg.at[pl.ds(0, PAD)], sem_halo_s.at[3], sem_halo_r.at[2], after)

    @pl.when(t > 0)
    def _():
        g_before.start()

    @pl.when(t < 31)
    def _():
        g_after.start()

    def pieces():
        for n in range(16):
            yield n, slice(n // 4 * 8, n // 4 * 8 + 8), slice(n % 4 * 192, n % 4 * 192 + 192)

    plane = (10, 9, 11, 6, 14, 2, 8, 5, 7, 13, 15, 1, 3, 4, 12)
    line = (4, 3, 5, 2, 6, 1, 7)
    here = y * 4 + x

    def in_plane(i):
        return ys[i // 4] * 4 + xr[i % 4], dev(i // 4, i % 4, z, c)

    early = sent_so_far()
    gk_swap.wait_recv()
    gh[...] = gkb[:, half(c)] + gcr[...]
    gp[...] = jnp.zeros((16, 8, 256), F32)
    for n, rows, cols in pieces():
        gp[n, :, 0:192] = gh[rows, cols]
    t_plane = []
    for i in plane:
        n, to = in_plane(i)
        t_plane.append(send(gp.at[n], zr.at[i - 1], sem_t_s.at[i], sem_t_r.at[i], to))

    def add(first, own, came, out):
        for item in first:
            item.wait_recv()

        def body(n, _):
            value = own(n).astype(F32)
            for i in range(3):
                value = value + came[i, n].astype(F32)
            out[n] = value.astype(BF16)
            return 0

        lax.fori_loop(0, 4, body, 0)

    add(x_first, lambda n: px[n, q], rx, s2x)
    x_second = [
        send(s2x.at[ys[i]], r2x.at[i - 1], sem_p_s.at[5 + i], sem_p_r.at[5 + i], along_y(i))
        for i in (2, 1, 3)
    ]
    add(y_first, lambda n: py[y, n], ry, s2y)
    y_second = [
        send(s2y.at[blocks[i]], r2y.at[i - 1], sem_p_s.at[8 + i], sem_p_r.at[8 + i], along_x(i))
        for i in (2, 1, 3)
    ]

    @pl.when(t > 0)
    def _():
        g_after.wait_recv()

    @pl.when(t == 0)
    def _():
        cg[0:PAD, :] = jnp.zeros((PAD, D), F32)

    @pl.when(t < 31)
    def _():
        g_before.wait_recv()

    @pl.when(t == 31)
    def _():
        cg[PAD + T:, :] = jnp.zeros((PAD, D), F32)

    def input_chunk(k, _):
        at_lanes = lanes_of(k)
        value = conv(cg[:, at_lanes], kern_ref[:, at_lanes], False) * live
        gin_ref[:, at_lanes] = value.astype(BF16)
        return 0

    all_sent(early)

    for item in t_plane:
        item.wait_recv()
    total = gp[here]
    for i in range(15):
        total = total + zr[i]
    xs[z] = total
    for i in line:
        slot = xs.at[z]
        send(slot, slot, sem_t_s.at[15 + i], sem_t_r.at[15 + i], along_z(i))

    for item in x_second + y_second:
        item.wait_recv()
    left, right = s2x[y].astype(F32), s2y[q].astype(F32)
    for i in range(3):
        left = left + r2x[i].astype(F32)
        right = right + r2y[i].astype(F32)
    facc[0:48, 0:CX] = left
    facc[0:48, CX:H] = right
    facc[48:56, :] = jnp.zeros((8, H), F32)
    for n in range(4):
        zs[n] = facc[12 * n:12 * n + 16, :].astype(BF16)
    w_z = [
        send(zs.at[zhs[i]], rz.at[i - 1], sem_z_s.at[i - 1], sem_z_r.at[i - 1], along_z(2 * i))
        for i in (2, 1, 3)
    ]

    lax.fori_loop(0, CHUNKS, input_chunk, 0)
    for i in range(1, 8):
        slot = xs.at[zr_[8 - i]]
        copy(slot, slot, sem_t_s.at[15 + i], sem_t_r.at[15 + i], mate).wait_recv()
    total = xs[0]
    for i in range(1, 8):
        total = total + xs[i]
    fg[here] = total
    middle = sent_so_far()
    for i in plane:
        send(fg.at[here], fg.at[here], sem_t_s.at[22 + i], sem_t_r.at[22 + i], in_plane(i)[1])

    stores = [pltpu.make_async_copy(gin_ref, gin_hbm, sem_out.at[0])]
    stores[0].start()
    all_sent(middle)

    @pl.when(t > 0)
    def _():
        to_before.wait_send()
        g_before.wait_send()

    @pl.when(t < 31)
    def _():
        to_after.wait_send()
        g_after.wait_send()

    pj_swap.wait_recv()
    proj_ref[:, half(oc)] = pjr[...]
    stores.append(pltpu.make_async_copy(proj_ref, proj_hbm, sem_out.at[1]))
    stores[1].start()

    for item in w_z:
        item.wait_recv()
    rows = zs[zh].astype(F32)
    for i in range(3):
        rows = rows + rz[i].astype(F32)
    fin[...] = jnp.zeros((2, 8, H), F32)
    fin[0, 0:6, :] = rows[0:6]
    fin[1, 0:6, :] = rows[6:12]
    w_swap = send(fin.at[oc], cr, sem_z_s.at[3], sem_z_r.at[3], mate)

    for i in range(1, 16):
        slot = fg.at[ys[-(i // 4) % 4] * 4 + xr[-(i % 4) % 4]]
        copy(slot, slot, sem_t_s.at[22 + i], sem_t_r.at[22 + i], mate).wait_recv()
    late = sent_so_far()
    t_swap = send(fg, fgr, sem_t_s.at[38], sem_t_r.at[38], mate)

    def put_taps(cols, source):
        for n, rows, part in pieces():
            gh[rows, part] = source[n, :, 0:192]
        gk_ref[:, cols] = gh[0:TAPS, :]
        gg_ref[:, cols] = gh[TAPS:TAPS + 1, :]

    put_taps(half(c), fg)
    all_sent(late)
    gw_ref[:, half(c)] = fin[c][0:6]
    w_swap.wait_recv()
    gw_ref[:, half(oc)] = cr[0:6, :]
    t_swap.wait_recv()
    put_taps(half(oc), fgr)
    for n, (src, dst) in enumerate(((gw_ref, gw_hbm), (gk_ref, gk_hbm), (gg_ref, gg_hbm))):
        stores.append(pltpu.make_async_copy(src, dst, sem_out.at[2 + n]))
        stores[-1].start()

    all_sent(started)
    for item in stores:
        item.wait()


def deliver(*refs):
    sources, results, kept, flat, sems = refs[:5], refs[5:10], refs[10:15], refs[15], refs[16]
    loads = [pltpu.make_async_copy(a, b, sems.at[n]) for n, (a, b) in enumerate(zip(sources, kept))]
    stores = [pltpu.make_async_copy(a, b, sems.at[5 + n]) for n, (a, b) in enumerate(zip(kept[:4] + (flat,), results))]
    for item in loads:
        item.start()
    for first, then in zip(loads[:4], stores):
        first.wait()
        then.start()
    loads[4].wait()
    flat[...] = kept[4][0]
    stores[4].start()
    for item in stores:
        item.wait()


def on_device(inputs, lengths, kernel, norm_gain, weight, cotangent):
    vmem = pl.BlockSpec(memory_space=pltpu.VMEM)
    dma = pltpu.SemaphoreType.DMA
    scratch = [
        pltpu.SMEM((1,), jnp.int32),
        pltpu.VMEM((T, D), BF16),
        pltpu.VMEM((TAPS, D), F32),
        pltpu.VMEM((D,), F32),
        pltpu.VMEM((T, D), BF16),
        pltpu.VMEM((T, D), BF16),
        pltpu.VMEM((6, D), F32),
        pltpu.VMEM((TAPS, D), F32),
        pltpu.VMEM((1, D), F32),
        pltpu.VMEM((2, PAD, D), BF16),
        pltpu.VMEM((T + 2 * PAD, D), F32),
        pltpu.VMEM((T, D), F32),
        pltpu.VMEM((T, D), F32),
        pltpu.VMEM((T, LANES), F32),
        pltpu.VMEM((2 * T, D), BF16),
        pltpu.VMEM((3 * LANES, T), F32),
        pltpu.VMEM((192, T), F32),
        pltpu.VMEM((2, H, T), BF16),
        pltpu.VMEM((H, 4 * T), BF16),
        pltpu.VMEM((4 * T, H), BF16),
        pltpu.VMEM((D, H), BF16),
        pltpu.VMEM((4, 4, 48, CX), BF16),
        pltpu.VMEM((4, 4, 48, CY), BF16),
        pltpu.VMEM((3, 4, 48, CX), BF16),
        pltpu.VMEM((3, 4, 48, CY), BF16),
        pltpu.VMEM((4, 48, CX), BF16),
        pltpu.VMEM((4, 48, CY), BF16),
        pltpu.VMEM((3, 48, CX), BF16),
        pltpu.VMEM((3, 48, CY), BF16),
        pltpu.VMEM((56, H), F32),
        pltpu.VMEM((4, 16, H), BF16),
        pltpu.VMEM((3, 16, H), BF16),
        pltpu.VMEM((2, 8, H), F32),
        pltpu.VMEM((8, H), F32),
        pltpu.VMEM((2, T, D), F32),
        pltpu.VMEM((T, D), F32),
        pltpu.VMEM((2, T, H), BF16),
        pltpu.VMEM((T, H), BF16),
        pltpu.VMEM((T + 2 * PAD, D), F32),
        pltpu.VMEM((32, D), F32),
        pltpu.VMEM((32, H), F32),
        pltpu.VMEM((32, H), F32),
        pltpu.VMEM((16, 8, 256), F32),
        pltpu.VMEM((15, 8, 256), F32),
        pltpu.VMEM((8, 8, 256), F32),
        pltpu.VMEM((16, 8, 256), F32),
        pltpu.VMEM((16, 8, 256), F32),
        dma((4,)), dma((4,)),
        dma((14,)), dma((14,)),
        dma((12,)), dma((12,)),
        dma((12,)), dma((12,)),
        dma((8,)), dma((8,)),
        dma((39,)), dma((39,)),
        dma((10,)), dma((10,)),
        dma((6,)), dma((5,)),
        pltpu.SemaphoreType.REGULAR((3,)),
    ]
    hbm = pl.BlockSpec(memory_space=pl.ANY)
    shapes = (
        jax.ShapeDtypeStruct((T, D), BF16),
        jax.ShapeDtypeStruct((T, D), BF16),
        jax.ShapeDtypeStruct((6, D), F32),
        jax.ShapeDtypeStruct((TAPS, D), F32),
        jax.ShapeDtypeStruct((1, D), F32),
    )
    results = pl.pallas_call(
        fused,
        out_shape=shapes,
        in_specs=[hbm] * 6,
        out_specs=[hbm] * 5,
        scratch_shapes=scratch,
        compiler_params=pltpu.CompilerParams(
            collective_id=0, has_side_effects=True, vmem_limit_bytes=60 << 20
        ),
        name="conv_module",
    )(inputs[0], lengths, kernel, norm_gain, weight, cotangent[0])
    projected, grad_input, grad_weight, grad_kernel, grad_gain = pl.pallas_call(
        deliver,
        out_shape=shapes[:4] + (jax.ShapeDtypeStruct((D,), F32),),
        in_specs=[hbm] * 5,
        out_specs=[hbm] * 5,
        scratch_shapes=[pltpu.VMEM(r.shape, r.dtype) for r in shapes] + [pltpu.VMEM((D,), F32), dma((10,))],
        compiler_params=pltpu.CompilerParams(vmem_limit_bytes=60 << 20),
        name="deliver",
    )(*results)
    return (projected[None], grad_input[None], grad_weight, grad_kernel, grad_gain)


def solution(mesh):
    in_specs = (
        P("batch", "tm", None),
        P("batch"),
        P(),
        P(),
        P("batch", None),
        P("batch", "tm", None),
    )
    out_specs = (P("batch", "tm", None), P("batch", "tm", None), P(("batch", "tm"), None), P(), P())
    return jax.shard_map(
        on_device, mesh=mesh, in_specs=in_specs, out_specs=out_specs, check_vma=False
    )
```
